32 devices in a mesh: dp: 16 (over z, y, x), blk: 2 (over core).
Axes of the slice: x: 2, y: 2, z: 4, core: 2. Of those that a mesh axis runs over, the one named last changes fastest.
Arguments:
- inputs: bfloat16 [32, 256, 1152], P('dp', 'blk'), may hold values from -6 to 6
- conditioning: bfloat16 [32, 1152], P('dp'), may hold values from -6 to 6
- grid_sizes: int32 [32, 2], P('dp'), may hold values from 12 to 20, as said below
- ada_weight: bfloat16 [1152, 6912], P('blk'), may hold values from -0.1875 to 0.1875
- ada_bias: bfloat16 [6912], replicated, may hold values from -1.796875 to 1.796875
- qkv_weight: bfloat16 [1152, 3456], P('blk'), may hold values from -0.1875 to 0.1875
- qv_bias: bfloat16 [2304], replicated, may hold values from -1.796875 to 1.796875
- proj_weight: bfloat16 [1152, 1152], P('blk'), may hold values from -1.5 to 1.5
- proj_bias: bfloat16 [1152], replicated, may hold values from -1.796875 to 1.796875
- fc1_weight: bfloat16 [1152, 4608], P('blk'), may hold values from -0.1875 to 0.1875
- fc1_bias: bfloat16 [4608], replicated, may hold values from -1.796875 to 1.796875
- fc2_weight: bfloat16 [4608, 1152], P('blk'), may hold values from -0.09375 to 0.09375
- fc2_bias: bfloat16 [1152], replicated, may hold values from -1.796875 to 1.796875
- cotangent: bfloat16 [32, 256, 1152], P('dp', 'blk'), may hold values from -6 to 6
Outputs:
- output: bfloat16 [32, 256, 1152], P('dp', 'blk')
- input_grad: float32 [32, 256, 1152], P('dp', 'blk')
- cond_grad: float32 [32, 1152], P('dp')
- ada_weight_grad: float32 [1152, 6912], P('dp', 'blk')
- ada_bias_grad: float32 [6912], P('dp')
- qkv_weight_grad: float32 [1152, 3456], P('dp', 'blk')
- qv_bias_grad: float32 [2304], P('dp')
- proj_weight_grad: float32 [1152, 1152], P('dp', 'blk')
- proj_bias_grad: float32 [1152], P('dp')
- fc1_weight_grad: float32 [1152, 4608], P('dp', 'blk')
- fc1_bias_grad: float32 [4608], P('dp')
- fc2_weight_grad: float32 [4608, 1152], P('dp', 'blk')
- fc2_bias_grad: float32 [1152], P('dp')
The draws below stay inside these ranges and needn't reach their ends.
Inputs may be any that keep to these rules, and one draw needn't show every extreme that they name: `grid_sizes`: each row holds a latent grid's height and width, whose product lies between 144 and 256; the first image's grid is 20 by 12 and the second's 12 by 20.
All inputs are finite; a program needn't handle non-finite values.
Results may differ from the reference program's by a relative error of at most 0.014.
The reference program's roundings to bfloat16 on the way count: a program that leaves them out, or rounds other values in their place, can miss the bound.
Values may be sent and summed in bfloat16 or wider, within the bound.
No kernel may reach another device: no remote copies, remote signals or barrier semaphores. Data moves between devices by JAX's collectives and lax.ppermute only.
A program may use at most 320 MiB of HBM per device.

```python
import math
import jax
import jax.numpy as jnp
from jax import lax

D = 1152
HEADS = 16
FF = 4608
SLOTS = 256
IMAGES = 32


def draw_grid_sizes(key, part):
    key = jax.random.fold_in(key, 11)
    first, second = jax.random.split(key)
    heights = jax.random.randint(first, (IMAGES,), 12, 21)
    widest = jnp.minimum(20, SLOTS // heights)
    widths = jax.random.randint(second, (IMAGES,), 12, widest + 1)
    heights = heights.at[0].set(20).at[1].set(12)
    widths = widths.at[0].set(12).at[1].set(20)
    return jnp.stack([heights, widths], axis=1).astype(jnp.int32)


def spiked(values, own_key, source, target, shards_of, factor):
    def block_of(dim):
        return (jnp.arange(values.shape[dim]) // (values.shape[dim] // shards_of)).reshape((-1,) + (1,) * (values.ndim - 1 - dim))

    near = jax.random.permutation(own_key, shards_of)[block_of(target)]
    other_side = (block_of(target) + shards_of // 2) % shards_of
    return jnp.where((block_of(source) == near) | (block_of(source) == other_side), factor * values, values)


def steps_of(stream_key, dims, shards, smallest, top_value):
    def one(position, parts):
        draws = jax.random.uniform(jax.random.fold_in(jax.random.fold_in(stream_key, 6), position), (parts,), jnp.float32, smallest / len(shards), top_value / len(shards))
        return jnp.repeat(jnp.exp(draws), dims[position] // parts).reshape((-1,) + (1,) * (len(dims) - position - 1))

    factor_of = one(*shards[0])
    for cut in shards[1:]:
        factor_of = factor_of * one(*cut)
    return factor_of


def bell_draw(rng, shape, spread, most, cuts=(), kind=jnp.bfloat16):
    array = jax.random.normal(rng, shape, jnp.float32) * spread
    if len(cuts) > 0:
        array = steps_of(rng, shape, cuts, -0.22, 0.18) * array
    return jnp.clip(array, min=-most, max=most).astype(kind)


def heavy_noise(key, dims, spread, reach, cuts, heavy, kind=jnp.bfloat16):
    drawn = spread * jax.random.normal(key, dims, jnp.float32)
    if cuts:
        drawn = drawn * steps_of(key, dims, cuts, -0.22, 0.18)
    return jnp.clip(spiked(drawn, jax.random.fold_in(key, 3), *heavy), -reach, reach).astype(kind)


def setup_inputs(seed: int = 0) -> dict:
    streams_of = jax.random.split(jax.random.key(seed), 15)
    return {
        "inputs": bell_draw(streams_of[0], (IMAGES, SLOTS, D), 1.0, 6.0, ((0, 16), (1, 2))),
        "conditioning": bell_draw(streams_of[1], (IMAGES, D), 1.0, 6.0, ((0, 16),)),
        "grid_sizes": draw_grid_sizes(jax.random.fold_in(streams_of[14], 71), 0),
        "ada_weight": bell_draw(streams_of[3], (D, 6 * D), D ** -0.5, 0.1875, ((0, 2),)),
        "ada_bias": bell_draw(streams_of[4], (6 * D,), 0.3, 1.796875),
        "qkv_weight": bell_draw(streams_of[5], (D, 3 * D), D ** -0.5, 0.1875, ((0, 2),)),
        "qv_bias": bell_draw(streams_of[6], (2 * D,), 0.3, 1.796875),
        "proj_weight": bell_draw(streams_of[7], (D, D), (D // 64) ** -0.5, 1.5, ((0, 2),)),
        "proj_bias": bell_draw(streams_of[8], (D,), 0.3, 1.796875),
        "fc1_weight": bell_draw(streams_of[9], (D, FF), D ** -0.5, 0.1875, ((0, 2),)),
        "fc1_bias": bell_draw(streams_of[10], (FF,), 0.3, 1.796875),
        "fc2_weight": bell_draw(streams_of[11], (FF, D), FF ** -0.5, 0.09375, ((0, 2),)),
        "fc2_bias": bell_draw(streams_of[12], (D,), 0.3, 1.796875),
        "cotangent": heavy_noise(streams_of[13], (IMAGES, SLOTS, D), 1.0, 6.0, ((0, 16), (1, 2)), (0, 2, 16, 2.0)),
    }


@jax.custom_vjp
def low(v):
    return lax.optimization_barrier(v.astype(jnp.bfloat16)).astype(jnp.float32)

@jax.custom_vjp
def low_back(v):
    return v

def low_keep(v):
    return (low(v), None)

def low_pass(kept, grad):
    return (grad,)

def back_keep(v):
    return (v, None)

def back_low(kept, grad):
    return (low(grad),)
low.defvjp(low_keep, low_pass)
low_back.defvjp(back_keep, back_low)
EPS = 1e-06
MASKED = -1e+30

def product(left, right):
    return jnp.dot(left, right, precision=lax.Precision.HIGHEST)

def normalize(values_in):
    average = lax.optimization_barrier(jnp.mean(values_in, -1, keepdims=True))
    centred = values_in - average
    return centred * lax.rsqrt(lax.optimization_barrier(jnp.mean(centred * centred, -1, keepdims=True)) + EPS)

def image_group(params, batch, cond_rows, grid_areas):
    ada_weight, ada_bias, qkv_weight, qv_bias, proj_weight, proj_bias, fc1_weight, fc1_bias, fc2_weight, fc2_bias = params
    members, slot_count, model_width = batch.shape
    head_size = model_width // HEADS
    modulation = low_back(product(low(jax.nn.silu(cond_rows)), ada_weight) + ada_bias)
    pieces = [modulation[:, None, portion * model_width:(portion + 1) * model_width] for portion in range(6)]
    shift_attn, scale_attn, gate_attn, shift_mlp, scale_mlp, gate_mlp = pieces
    normed_attn = normalize(batch)
    h_attn = low(normed_attn * (1.0 + scale_attn) + shift_attn)
    qkv_rows = product(h_attn.reshape(members * slot_count, model_width), qkv_weight).reshape(members, slot_count, 3 * model_width)
    query_part = low(low_back(qkv_rows[..., :model_width] + qv_bias[:model_width]))
    key_part = low(low_back(qkv_rows[..., model_width:2 * model_width]))
    value_part = low(low_back(qkv_rows[..., 2 * model_width:] + qv_bias[model_width:]))
    head_shape = (members, slot_count, HEADS, head_size)
    scores = jnp.einsum('gqhd,gkhd->ghqk', query_part.reshape(head_shape), key_part.reshape(head_shape), precision=lax.Precision.HIGHEST) * head_size ** (-0.5)
    slot_index = jnp.arange(slot_count, dtype=jnp.int32)
    slot_valid = slot_index[None, :] < grid_areas[:, None]
    scores = low_back(jnp.where(slot_valid[:, None, None, :], scores, MASKED))
    exponent = jnp.exp(scores - lax.optimization_barrier(jnp.max(scores, -1, keepdims=True)))
    probs_low = low(exponent / lax.optimization_barrier(jnp.sum(exponent, -1, keepdims=True)))
    attended = jnp.einsum('ghqk,gkhd->gqhd', probs_low, value_part.reshape(head_shape), precision=lax.Precision.HIGHEST)
    attended = low(low_back(attended.reshape(members * slot_count, model_width)))
    attn_out = low_back(product(attended, proj_weight) + proj_bias).reshape(members, slot_count, model_width)
    middle = batch + gate_attn * attn_out
    normed_mlp = normalize(middle)
    h_mlp = low(normed_mlp * (1.0 + scale_mlp) + shift_mlp)
    hidden_pre = low_back(product(h_mlp.reshape(members * slot_count, model_width), fc1_weight) + fc1_bias)
    activated = low(jax.nn.gelu(hidden_pre, approximate=True))
    mlp_out = low_back(product(activated, fc2_weight) + fc2_bias).reshape(members, slot_count, model_width)
    result = middle + gate_mlp * mlp_out
    return jnp.where(slot_valid[:, :, None], result, 0.0)

def reference(inputs, conditioning, grid_sizes, ada_weight, ada_bias, qkv_weight, qv_bias, proj_weight, proj_bias, fc1_weight, fc1_bias, fc2_weight, fc2_bias, cotangent):
    params = tuple((weight.astype(jnp.float32) for weight in (ada_weight, ada_bias, qkv_weight, qv_bias, proj_weight, proj_bias, fc1_weight, fc1_bias, fc2_weight, fc2_bias)))
    members = math.gcd(IMAGES, 16)
    group_count = IMAGES // members
    grid_areas = (grid_sizes[:, 0] * grid_sizes[:, 1]).astype(jnp.int32).reshape(group_count, members)

    def forward(inputs_f32, cond_f32, weights):

        def advance(counter, pieces):
            return (counter, jax.checkpoint(image_group)(weights, pieces[0], pieces[1], pieces[2]))
        stacked = (inputs_f32.reshape(group_count, members, SLOTS, D), cond_f32.reshape(group_count, members, D), grid_areas)
        unused, results = lax.scan(advance, jnp.zeros((), jnp.float32), stacked)
        return results.reshape(IMAGES, SLOTS, D)
    output, pull = jax.vjp(forward, inputs.astype(jnp.float32), conditioning.astype(jnp.float32), params)
    input_grad, cond_grad, grads = pull(cotangent.astype(jnp.float32))
    return (output.astype(jnp.bfloat16), input_grad, cond_grad, grads[0], grads[1], grads[2], grads[3], grads[4], grads[5], grads[6], grads[7], grads[8], grads[9])
```

```python
import functools

import jax
import jax.numpy as jnp
from jax import lax
from jax.experimental import pallas as pl
from jax.experimental.pallas import tpu as pltpu
from jax.sharding import PartitionSpec as P

HEADS = 16
EPS = 1e-06
MASKED = -1e30
F32 = jnp.float32
BF16 = jnp.bfloat16
VMEM_LIMIT = 48 * 1024 * 1024


def normalize(values_in):
    average = jnp.mean(values_in, -1, keepdims=True)
    centred = values_in - average
    return centred * lax.rsqrt(jnp.mean(centred * centred, -1, keepdims=True) + EPS)


def gelu_tanh(values_in):
    return jax.nn.gelu(values_in, approximate=True)


def product(left, right):
    return jnp.dot(left, right, preferred_element_type=F32)


def transpose_product(left, right):
    return lax.dot_general(left, right, (((0,), (0,)), ((), ())), preferred_element_type=F32)


def product_back(left, right):
    return lax.dot_general(left, right, (((1,), (1,)), ((), ())), preferred_element_type=F32)


def swap(values_in):
    return lax.ppermute(values_in, "blk", [(0, 1), (1, 0)])


def pick(values_in, index, axis=0):
    return lax.dynamic_index_in_dim(values_in, index, axis, keepdims=False)


def in_order(core, mine, theirs, axis=0):
    first = jnp.where(core == 0, mine, theirs)
    second = jnp.where(core == 0, theirs, mine)
    return jnp.concatenate([first, second], axis)


def head_window(head, size):
    low, high = head * size, (head + 1) * size
    start, stop = low // 128 * 128, -(-high // 128) * 128
    lane = lax.broadcasted_iota(jnp.int32, (1, stop - start), 1) + start
    return slice(start, stop), (lane >= low) & (lane < high)


def attention_forward_kernel(size, scale, q_ref, k_ref, v_ref, valid_ref, out_ref, log_ref):
    valid = valid_ref[...] > 0
    rows = q_ref.shape[0]
    lane = lax.broadcasted_iota(jnp.int32, (1, 128), 1)
    logs = jnp.zeros((rows, 128), F32)
    for head in range(HEADS):
        columns, own = head_window(head, size)
        query = jnp.where(own, q_ref[:, columns].astype(F32), 0.0).astype(BF16)
        scores = jnp.where(valid, product_back(query, k_ref[:, columns]) * scale, MASKED)
        largest = jnp.max(scores, -1, keepdims=True)
        exponent = jnp.exp(scores - largest)
        totals = jnp.sum(exponent, -1, keepdims=True)
        probs = (exponent / totals).astype(BF16)
        attended = product(probs, v_ref[:, columns])
        out_ref[:, columns] = jnp.where(own, attended, out_ref[:, columns].astype(F32)).astype(BF16)
        logs = jnp.where(lane == head, largest + jnp.log(totals), logs)
    log_ref[...] = logs


def attention_backward_kernel(
    size, scale, q_ref, k_ref, v_ref, valid_ref, log_ref, grad_ref, gq_ref, gk_ref, gv_ref
):
    valid = valid_ref[...] > 0
    for head in range(HEADS):
        columns, own = head_window(head, size)
        query = q_ref[:, columns]
        key = k_ref[:, columns]
        grad = grad_ref[:, columns]
        own_query = jnp.where(own, query.astype(F32), 0.0).astype(BF16)
        own_grad = jnp.where(own, grad.astype(F32), 0.0).astype(BF16)
        scores = jnp.where(valid, product_back(own_query, key) * scale, MASKED)
        probs = jnp.exp(scores - log_ref[:, head : head + 1])
        grad_probs = product_back(own_grad, v_ref[:, columns])
        inner = jnp.sum(probs * grad_probs, -1, keepdims=True)
        grad_scores = (probs * (grad_probs - inner)).astype(BF16)
        grad_query = product(grad_scores, key) * scale
        grad_key = transpose_product(grad_scores, query) * scale
        grad_value = transpose_product(probs.astype(BF16), grad)
        gq_ref[:, columns] = jnp.where(own, grad_query, gq_ref[:, columns].astype(F32)).astype(BF16)
        gk_ref[:, columns] = jnp.where(own, grad_key, gk_ref[:, columns].astype(F32)).astype(BF16)
        gv_ref[:, columns] = jnp.where(own, grad_value, gv_ref[:, columns].astype(F32)).astype(BF16)


def attention_forward(query, key, value, valid):
    rows, width = query.shape
    size = width // HEADS
    return pl.pallas_call(
        functools.partial(attention_forward_kernel, size, size ** (-0.5)),
        out_shape=(
            jax.ShapeDtypeStruct((rows, width), BF16),
            jax.ShapeDtypeStruct((rows, 128), F32),
        ),
        compiler_params=pltpu.CompilerParams(vmem_limit_bytes=VMEM_LIMIT),
        cost_estimate=pl.CostEstimate(
            flops=8 * rows * rows * 256 * HEADS, bytes_accessed=8 * rows * width, transcendentals=rows * rows * HEADS
        ),
        name="attention_forward",
    )(query, key, value, valid)


def attention_backward(query, key, value, valid, logs, grad):
    rows, width = query.shape
    size = width // HEADS
    shape = jax.ShapeDtypeStruct((rows, width), BF16)
    return pl.pallas_call(
        functools.partial(attention_backward_kernel, size, size ** (-0.5)),
        out_shape=(shape, shape, shape),
        compiler_params=pltpu.CompilerParams(vmem_limit_bytes=VMEM_LIMIT),
        cost_estimate=pl.CostEstimate(
            flops=20 * rows * rows * 256 * HEADS, bytes_accessed=14 * rows * width, transcendentals=rows * rows * HEADS
        ),
        name="attention_backward",
    )(query, key, value, valid, logs, grad)


def axis_orders(count):
    bits = count.bit_length() - 1
    if bits == 4:
        return [(0, 1, 2, 3), (1, 2, 0, 3), (2, 0, 1, 3)]
    return [tuple((bit + turn) % bits for bit in range(bits)) for turn in range(min(3, bits))]


def reduce_chunk(values_in, order, count):
    bits = count.bit_length() - 1
    place = lax.axis_index("dp")
    left = list(range(bits - 1, -1, -1))
    current = values_in.reshape((2,) * bits + values_in.shape[1:])
    for step, bit in enumerate(order):
        mine = (place >> bit) & 1
        axis = left.index(bit)
        send = pick(current, 1 - mine, axis).astype(BF16)
        keep = pick(current, mine, axis)
        left.pop(axis)
        got = lax.ppermute(send, "dp", [(index, index ^ (1 << bit)) for index in range(count)])
        current = keep.astype(F32) + got.astype(F32)
        if step < bits - 1:
            current = current.astype(BF16)
    return current


def cut(rows):
    if rows % 8 or rows < 24:
        return [rows]
    tiles = rows // 8
    first = round(tiles * 4 / 9)
    second = round(tiles * 3 / 9)
    return [8 * first, 8 * second, rows - 8 * first - 8 * second]


def reduce_scatter(values_in):
    count = lax.axis_size("dp")
    rows = values_in.shape[0] // count
    blocks = values_in.reshape(count, rows, values_in.shape[1])
    done, start = [], 0
    for length, order in zip(cut(rows), axis_orders(count)):
        done.append(reduce_chunk(blocks[:, start : start + length], order, count))
        start += length
    return jnp.concatenate(done, 0)


def small_reduce_scatter(rows_in):
    count = lax.axis_size("dp")
    bits = count.bit_length() - 1
    place = lax.axis_index("dp")
    current = rows_in.reshape((2,) * bits + rows_in.shape[1:])
    for bit in range(bits - 1, -1, -1):
        mine = (place >> bit) & 1
        send = pick(current, 1 - mine)
        keep = pick(current, mine)
        got = lax.ppermute(send, "dp", [(index, index ^ (1 << bit)) for index in range(count)])
        current = keep + got
    return current


def gather_unordered(values_in):
    count = lax.axis_size("dp")
    current = values_in
    for bit in range(count.bit_length() - 1):
        got = lax.ppermute(current, "dp", [(index, index ^ (1 << bit)) for index in range(count)])
        current = jnp.concatenate([current, got], 0)
    return current


def on_device(
    inputs,
    conditioning,
    grid_sizes,
    ada_weight,
    ada_bias,
    qkv_weight,
    qv_bias,
    proj_weight,
    proj_bias,
    fc1_weight,
    fc1_bias,
    fc2_weight,
    fc2_bias,
    cotangent,
):
    images, strip, width = inputs.shape
    data_count = lax.axis_size("dp")
    core = lax.axis_index("blk")
    other = 1 - core
    place = lax.axis_index("dp")
    part = ada_weight.shape[0]
    hidden = fc1_weight.shape[1]
    half_hidden = hidden // 2

    mine_inputs, their_inputs = pick(inputs, core), swap(pick(inputs, other))
    mine_cot, their_cot = pick(cotangent, core), swap(pick(cotangent, other))
    qkv_full = in_order(core, qkv_weight, swap(qkv_weight))
    proj_full = in_order(core, proj_weight, swap(proj_weight))
    fc1_parts = fc1_weight.reshape(part, 2, half_hidden)
    fc1_half = in_order(core, pick(fc1_parts, core, 1), swap(pick(fc1_parts, other, 1)))

    cond_f32 = conditioning.astype(F32)
    silu_cond, silu_back = jax.vjp(jax.nn.silu, cond_f32)
    silu_low = silu_cond.astype(BF16)
    modulation_part = product(pick(silu_low.reshape(images, 2, part), core, 1), ada_weight)
    modulation = modulation_part + swap(modulation_part) + ada_bias.astype(F32)
    own_modulation = pick(modulation, core)[None, :]
    shift_attn, scale_attn, gate_attn, shift_mlp, scale_mlp, gate_mlp = [
        own_modulation[:, index * width : (index + 1) * width] for index in range(6)
    ]
    silu_all = gather_unordered(silu_low)
    silu_rows = pick(silu_all.reshape(images * data_count, data_count, width // data_count), place, 1)

    area = pick(grid_sizes[:, 0] * grid_sizes[:, 1], core)
    near = jnp.arange(strip, dtype=jnp.int32)
    positions = jnp.concatenate([core * strip + near, other * strip + near])
    valid = positions < area
    valid_row = valid.astype(F32)[None, :]
    valid_column = valid[:, None]

    tokens = jnp.concatenate([mine_inputs, their_inputs], 0).astype(F32)
    cot = jnp.concatenate([mine_cot, their_cot], 0).astype(F32)
    grad_out = jnp.where(valid_column, cot, 0.0)
    grad_mlp = (gate_mlp * grad_out).astype(BF16)
    grad_mlp_other = swap(grad_mlp)
    grad_mlp_all = jnp.concatenate([grad_mlp, grad_mlp_other], 0)

    normed_attn, norm_back_attn = jax.vjp(normalize, tokens)
    h_attn = (normed_attn * (1.0 + scale_attn) + shift_attn).astype(BF16)
    h_attn_all = jnp.concatenate([h_attn, swap(h_attn)], 0)
    qkv_rows = product(h_attn, qkv_full)
    bias_f32 = qv_bias.astype(F32)
    query = (qkv_rows[:, :width] + bias_f32[:width]).astype(BF16)
    key = qkv_rows[:, width : 2 * width].astype(BF16)
    value = (qkv_rows[:, 2 * width :] + bias_f32[width:]).astype(BF16)
    attended, logs = attention_forward(query, key, value, valid_row)
    attended_all = jnp.concatenate([attended, swap(attended)], 0)
    attn = product(attended, proj_full) + proj_bias.astype(F32)
    middle = tokens + gate_attn * attn
    normed_mlp, norm_back_mlp = jax.vjp(normalize, middle)
    h_mlp = (normed_mlp * (1.0 + scale_mlp) + shift_mlp).astype(BF16)
    h_mlp_all = jnp.concatenate([h_mlp, swap(h_mlp)], 0)

    fc1_bias_half = pick(fc1_bias.astype(F32).reshape(2, half_hidden), core)
    hidden_pre = product(h_mlp_all, fc1_half) + fc1_bias_half
    activated, gelu_back = jax.vjp(gelu_tanh, hidden_pre)
    activated_low = activated.astype(BF16)
    grad_act = product_back(grad_mlp_all, fc2_weight)
    grad_pre = gelu_back(grad_act)[0].astype(BF16)
    fc1_term = transpose_product(h_mlp_all, grad_pre)
    fc1_grad = reduce_scatter(fc1_term)

    rows = images * strip
    grad_mlp_columns = pick(grad_mlp_all.reshape(2 * rows, 2, part), core, 1)
    grad_mlp_turned = jnp.concatenate([grad_mlp_columns[rows:], grad_mlp_columns[:rows]], 0)
    fc2_term = in_order(
        core,
        transpose_product(activated_low, grad_mlp_columns).astype(BF16),
        transpose_product(swap(activated_low), grad_mlp_turned).astype(BF16),
    )
    fc2_grad = reduce_scatter(fc2_term)

    mlp_part = product(activated_low, fc2_weight)
    mlp = mlp_part[:rows] + swap(mlp_part[rows:]) + fc2_bias.astype(F32)
    result = jnp.where(valid_column, middle + gate_mlp * mlp, 0.0).astype(BF16)
    grad_h_part = product_back(grad_pre, fc1_half)
    grad_h_mlp = grad_h_part[:rows] + swap(grad_h_part[rows:])

    grad_middle = grad_out + norm_back_mlp(grad_h_mlp * (1.0 + scale_mlp))[0]
    grad_attn = (gate_attn * grad_middle).astype(BF16)
    grad_attn_parts = grad_attn.reshape(rows, 2, part)
    grad_attn_columns = jnp.concatenate(
        [pick(grad_attn_parts, core, 1), swap(pick(grad_attn_parts, other, 1))], 0
    )
    proj_term = transpose_product(attended_all, grad_attn_columns)
    proj_grad = reduce_scatter(proj_term)
    grad_attended = product_back(grad_attn, proj_full).astype(BF16)
    grad_query, grad_key, grad_value = attention_backward(
        query, key, value, valid_row, logs, grad_attended
    )
    grad_qkv = jnp.concatenate([grad_query, grad_key, grad_value], 1)
    grad_qkv_parts = grad_qkv.reshape(rows, 2, 3 * part)
    grad_qkv_columns = jnp.concatenate(
        [pick(grad_qkv_parts, core, 1), swap(pick(grad_qkv_parts, other, 1))], 0
    )
    qkv_term = transpose_product(h_attn_all, grad_qkv_columns)
    qkv_grad = reduce_scatter(qkv_term)

    grad_h_attn = product_back(grad_qkv, qkv_full)
    input_grad = grad_middle + norm_back_attn(grad_h_attn * (1.0 + scale_attn))[0]

    grad_modulation = jnp.concatenate(
        [
            jnp.sum(grad_h_attn, 0),
            jnp.sum(grad_h_attn * normed_attn, 0),
            jnp.sum(grad_middle * attn, 0),
            jnp.sum(grad_h_mlp, 0),
            jnp.sum(grad_h_mlp * normed_mlp, 0),
            jnp.sum(grad_out * mlp, 0),
        ]
    ).astype(BF16)[None, :]
    modulation_low = in_order(core, grad_modulation, swap(grad_modulation))
    silu_grad_part = product_back(modulation_low, ada_weight)
    silu_grad = in_order(core, silu_grad_part, swap(silu_grad_part), 1)
    cond_grad = silu_back(silu_grad)[0]
    modulation_columns = pick(modulation_low.reshape(images, 2, 3 * width), core, 1)
    modulation_all = gather_unordered(modulation_columns)
    ada_grad = transpose_product(silu_rows, modulation_all)

    sum_f32 = lambda array: jnp.sum(array.astype(F32), 0)
    fc1_bias_part = sum_f32(grad_pre)
    fc1_bias_sums = in_order(core, fc1_bias_part, jnp.zeros_like(fc1_bias_part))
    bias_rows = jnp.concatenate(
        [
            sum_f32(grad_modulation).reshape(data_count, -1),
            jnp.concatenate([sum_f32(grad_query), sum_f32(grad_value)]).reshape(data_count, -1),
            sum_f32(grad_attn).reshape(data_count, -1),
            fc1_bias_sums.reshape(data_count, -1),
            sum_f32(grad_mlp).reshape(data_count, -1),
        ],
        1,
    )
    bias_sums = small_reduce_scatter(bias_rows + swap(bias_rows))
    lengths = [6 * width, 2 * width, width, hidden, width]
    ends, at = [], 0
    for length in lengths:
        at += length // data_count
        ends.append(at)
    biases = jnp.split(bias_sums, ends[:-1])

    back = lambda array: in_order(core, array[None, :strip], swap(array[None, strip:]))
    return (
        back(result),
        back(input_grad),
        cond_grad,
        ada_grad,
        biases[0],
        qkv_grad,
        biases[1],
        proj_grad,
        biases[2],
        fc1_grad,
        biases[3],
        fc2_grad,
        biases[4],
    )


def solution(mesh):
    rows = P("dp", "blk", None)
    weight = P("blk", None)
    grads = (P("dp", "blk"), P("dp"))
    placed = (rows, P("dp", None), P("dp", None)) + (weight, P()) * 5 + (rows,)
    return jax.shard_map(
        on_device,
        mesh=mesh,
        in_specs=placed,
        out_specs=(rows, rows, P("dp", None)) + grads * 5,
        check_vma=False,
    )
```

```python
import functools
import math

import jax
import jax.numpy as jnp
from jax import lax
from jax.experimental import pallas as pl
from jax.experimental.pallas import tpu as pltpu
from jax.sharding import PartitionSpec as P

HEADS = 16
EPS = 1e-06
MASKED = -1e30
F32 = jnp.float32
BF16 = jnp.bfloat16
GELU_A = math.sqrt(2.0 / math.pi)
GELU_B = 0.044715
NEAR, FAR = 0, 1
COST = 1000


def product(left, right):
    return jnp.dot(left, right, preferred_element_type=F32)


def transpose_product(left, right):
    return lax.dot_general(left, right, (((0,), (0,)), ((), ())), preferred_element_type=F32)


def product_back(left, right):
    return lax.dot_general(left, right, (((1,), (1,)), ((), ())), preferred_element_type=F32)


def swap(values_in):
    return lax.ppermute(values_in, "blk", [(0, 1), (1, 0)])


def pick(values_in, index, axis=0):
    return lax.dynamic_index_in_dim(values_in, index, axis, keepdims=False)


def columns_of(values_in, index, length):
    return lax.dynamic_slice_in_dim(values_in, index * length, length, 1)


def in_order(core, mine, theirs, axis=0):
    first = jnp.where(core == 0, mine, theirs)
    second = jnp.where(core == 0, theirs, mine)
    return jnp.concatenate([first, second], axis)


def after(values_in, token):
    return lax.optimization_barrier((values_in, token))[0]


def call(kernel, outs, ins, scratch=(), name=None, prefetch=(), limit=24):
    specs, arrays = [], []
    for item in prefetch:
        specs.append(pl.BlockSpec(memory_space=pltpu.SMEM))
        arrays.append(item)
    place = lambda item: pl.BlockSpec(memory_space=pltpu.HBM if isinstance(item, tuple) else pltpu.VMEM)
    plain = lambda item: item[0] if isinstance(item, tuple) else item
    return pl.pallas_call(
        kernel,
        out_shape=tuple(plain(out) for out in outs),
        in_specs=specs + [place(item) for item in ins],
        out_specs=tuple(place(out) for out in outs),
        scratch_shapes=list(scratch),
        compiler_params=pltpu.CompilerParams(vmem_limit_bytes=limit * 1024 * 1024),
        cost_estimate=pl.CostEstimate(flops=COST, bytes_accessed=10**6, transcendentals=0),
        name=name,
    )(*arrays, *[plain(item) for item in ins])


class Outgoing:
    def __init__(self, sems):
        self.sems, self.copies = sems, []

    def start(self, source, target):
        copy = pltpu.make_async_copy(source, target, self.sems.at[len(self.copies)])
        copy.start()
        self.copies.append(copy)

    def wait(self):
        for copy in self.copies:
            copy.wait()


def shape_f32(*dims):
    return jax.ShapeDtypeStruct(dims, F32)


def shape_bf16(*dims):
    return jax.ShapeDtypeStruct(dims, BF16)


def row_mean(values_in):
    return jnp.mean(values_in, -1, keepdims=True)


def normalize(values_in):
    centred = values_in - row_mean(values_in)
    inverse = lax.rsqrt(row_mean(centred * centred) + EPS)
    return centred * inverse, inverse


def normalize_back(normed, inverse, grad):
    return inverse * (grad - row_mean(grad) - normed * row_mean(grad * normed))


def head_window(head, size):
    low, high = head * size, (head + 1) * size
    start, stop = low // 128 * 128, -(-high // 128) * 128
    lane = lax.broadcasted_iota(jnp.int32, (1, stop - start), 1) + start
    return slice(start, stop), (lane >= low) & (lane < high)


def valid_slots(ids_ref, rows, dimension):
    strip = rows // 2
    shape = (1, rows) if dimension == 1 else (rows, 1)
    near = lax.broadcasted_iota(jnp.int32, shape, dimension)
    core = ids_ref[0]
    position = jnp.where(near < strip, core * strip + near, (1 - core) * strip + near - strip)
    return position < ids_ref[1]


def start_rows(core, mine, theirs, target, sems, at):
    rows = mine.shape[0]
    copies = (
        pltpu.make_async_copy(mine, target.at[pl.ds(pl.multiple_of(core * rows, 64), rows)], sems.at[at]),
        pltpu.make_async_copy(
            theirs, target.at[pl.ds(pl.multiple_of((1 - core) * rows, 64), rows)], sems.at[at + 1]
        ),
    )
    for copy in copies:
        copy.start()
    return copies


def pieces_of(mod_ref, width):
    return [mod_ref[:, index * width : (index + 1) * width] for index in range(6)]


def front_kernel(
    ids_ref,
    mine_ref,
    theirs_ref,
    mod_ref,
    wq_mine,
    wq_theirs,
    wp_mine,
    wp_theirs,
    qv_bias_ref,
    proj_bias_ref,
    both_out,
    q_out,
    k_out,
    v_out,
    log_out,
    attn_out,
    h_mlp_ref,
    wq_ref,
    wp_ref,
    both_ref,
    q_ref,
    k_ref,
    v_ref,
    log_ref,
    attn_ref,
    sems,
    out_sems,
):
    out = Outgoing(out_sems)
    core = ids_ref[0]
    q_copies = start_rows(core, wq_mine, wq_theirs, wq_ref, sems, 0)
    p_copies = start_rows(core, wp_mine, wp_theirs, wp_ref, sems, 2)
    rows, width = q_ref.shape
    size = width // HEADS
    shift_attn, scale_attn, gate_attn, shift_mlp, scale_mlp, _ = pieces_of(mod_ref, width)
    tokens = jnp.concatenate([mine_ref[...], theirs_ref[...]], 0).astype(F32)
    normed, _ = normalize(tokens)
    h_attn = (normed * (1.0 + scale_attn) + shift_attn).astype(BF16)
    both_ref[0] = h_attn
    out.start(both_ref.at[0], both_out.at[0])
    for copy in q_copies:
        copy.wait()
    q_ref[...] = (product(h_attn, wq_ref[:, :width]) + qv_bias_ref[:, :width].astype(F32)).astype(BF16)
    k_ref[...] = product(h_attn, wq_ref[:, width : 2 * width]).astype(BF16)
    v_ref[...] = (
        product(h_attn, wq_ref[:, 2 * width :]) + qv_bias_ref[:, width:].astype(F32)
    ).astype(BF16)

    for source, target in ((q_ref, q_out), (k_ref, k_out), (v_ref, v_out)):
        out.start(source, target)

    valid = valid_slots(ids_ref, rows, 1)
    lane = lax.broadcasted_iota(jnp.int32, (1, 128), 1)
    logs = jnp.zeros((rows, 128), F32)
    for head in range(HEADS):
        columns, own = head_window(head, size)
        query = jnp.where(own, q_ref[:, columns].astype(F32), 0.0).astype(BF16)
        scores = jnp.where(valid, product_back(query, k_ref[:, columns]) * size ** (-0.5), MASKED)
        largest = jnp.max(scores, -1, keepdims=True)
        exponent = jnp.exp(scores - largest)
        totals = jnp.sum(exponent, -1, keepdims=True)
        probs = (exponent / totals).astype(BF16)
        attended = product(probs, v_ref[:, columns])
        before = both_ref[1, :, columns].astype(F32)
        both_ref[1, :, columns] = jnp.where(own, attended, before).astype(BF16)
        logs = jnp.where(lane == head, largest + jnp.log(totals), logs)
    log_ref[...] = logs
    out.start(log_ref, log_out)
    out.start(both_ref.at[1], both_out.at[1])

    for copy in p_copies:
        copy.wait()
    attn = product(both_ref[1], wp_ref[...]) + proj_bias_ref[...].astype(F32)
    attn_ref[...] = attn
    out.start(attn_ref, attn_out)
    normed_mlp, _ = normalize(tokens + gate_attn * attn)
    h_mlp_ref[...] = (normed_mlp * (1.0 + scale_mlp) + shift_mlp).astype(BF16)
    out.wait()


def bits_in_order(kind, core):
    return (core, 1 - core, 2, 3) if kind == NEAR else (2, core, 1 - core, 3)


def store_halves(read, kind, ids_ref, keep_ref, send_ref, columns=slice(None), high=None):
    core = ids_ref[0]
    order = bits_in_order(kind, core)
    mine = ids_ref[2 + order[0]]
    for index in range(8 if high is None else 4):
        if high is None:
            slot = index
            base = ((index >> 2) << order[1]) + (((index >> 1) & 1) << order[2]) + ((index & 1) << order[3])
        else:
            slot = (index, high)
            base = ((index >> 1) << order[1]) + ((index & 1) << order[2])
        for target, value in ((keep_ref, mine), (send_ref, 1 - mine)):
            block = base + (value << order[0])
            where = slot if isinstance(slot, tuple) else (slot,)
            target[(*where, slice(None), columns)] = read(block).astype(BF16)


def rows_of(total_ref, stride, first, count):
    return lambda block: total_ref[pl.ds(pl.multiple_of(block * stride + first, 8), count), :]


def start_hidden_weights(core, w1_mine, w1_theirs, w2, w1_ref, w2_ref, sems, chunks):
    half = w1_theirs.shape[1]
    length = half // chunks
    copies = []
    for chunk in range(chunks):
        here = pl.ds(chunk * length, length)
        mine = w1_mine.at[:, pl.ds(pl.multiple_of(core * half + chunk * length, 128), length)]
        second = pltpu.make_async_copy(w2.at[here], w2_ref.at[here], sems.at[3 * chunk + 2])
        second.start()
        first = start_rows(core, mine, w1_theirs.at[:, here], w1_ref.at[:, here], sems, 3 * chunk)
        copies.append((second, *first))
    return copies


def hidden_kernel(
    ids_ref,
    h_own_ref,
    h_other_ref,
    gm_own_ref,
    gm_other_ref,
    w1_mine,
    w1_theirs,
    w2,
    bias_ref,
    act_ref,
    gp_ref,
    bias_grad_ref,
    *rest,
):
    core = ids_ref[0]
    w1_ref, w2_ref, total_ref, sems = rest[-4:]
    if len(rest) > 4:
        keep_out, send_out, keep_ref, send_ref, out_sems = rest[:5]
        out = Outgoing(out_sems)
    length, half = total_ref.shape[1], act_ref.shape[1]
    copies = start_hidden_weights(core, w1_mine, w1_theirs, w2, w1_ref, w2_ref, sems, half // length)
    h_all = jnp.concatenate([h_own_ref[...], h_other_ref[...]], 0)
    gm_all = jnp.concatenate([gm_own_ref[...], gm_other_ref[...]], 0)
    for chunk in range(half // length):
        for copy in copies[chunk]:
            copy.wait()
        here = slice(chunk * length, (chunk + 1) * length)
        bias = bias_ref[:, pl.ds(pl.multiple_of(core * half + chunk * length, 128), length)].astype(F32)
        grad_act = product_back(gm_all, w2_ref[here, :])
        value = product(h_all, w1_ref[:, here]) + bias
        square = value * value
        tanh = jnp.tanh(GELU_A * value * (1.0 + GELU_B * square))
        half_up = 0.5 * (1.0 + tanh)
        act_ref[:, here] = (value * half_up).astype(BF16)
        slope = half_up + 0.5 * value * (1.0 - tanh * tanh) * (GELU_A * (1.0 + 3.0 * GELU_B * square))
        grad_pre = (grad_act * slope).astype(BF16)
        gp_ref[:, here] = grad_pre
        bias_grad_ref[:, here] = jnp.sum(grad_pre.astype(F32), 0, keepdims=True)
        if len(rest) > 4:
            total_ref[...] = transpose_product(h_all, grad_pre)
            rows = keep_ref.shape[2]
            read = rows_of(total_ref, rows, 0, rows)
            store_halves(read, NEAR, ids_ref, keep_ref.at[chunk], send_ref.at[chunk])
            out.start(send_ref.at[chunk], send_out.at[:, :, here])
            out.start(keep_ref.at[chunk], keep_out.at[:, :, here])
    if len(rest) > 4:
        out.wait()


def fc2_grad_kernel(ids_ref, gm_own_ref, gm_other_ref, *rest):
    act_ref, got_ref, targets, outs = rest[0], rest[1], rest[2:6], rest[6:10]
    columns_ref, turned_ref, total_ref, out_sems = rest[10:]
    out = Outgoing(out_sems)
    core = ids_ref[0]
    rows, part = gm_own_ref.shape[0], columns_ref.shape[1]
    for index in range(2):

        @pl.when(core == index)
        def _():
            own = gm_own_ref[:, index * part : (index + 1) * part]
            other = gm_other_ref[:, index * part : (index + 1) * part]
            columns_ref[:rows] = own
            columns_ref[rows:] = other
            turned_ref[:rows] = other
            turned_ref[rows:] = own

    near, far = outs[0].shape[2], outs[2].shape[2]
    half_block = near + far
    length = act_ref.shape[1] // 3
    for side, (ref, grads) in enumerate(((act_ref, columns_ref), (got_ref, turned_ref))):
        for start in range(0, 3 * length, length):
            here = slice(start, start + length)
            total_ref[here, :] = transpose_product(ref[:, here], grads[...])
        high = core if side == 0 else 1 - core
        for kind, (first, count) in enumerate(((0, near), (near, far))):
            for place in range(2):
                store_halves(
                    rows_of(total_ref, 2 * half_block, place * half_block + first, count),
                    kind,
                    ids_ref,
                    outs[2 * kind],
                    outs[2 * kind + 1],
                    slice(place * part, (place + 1) * part),
                    high,
                )
            for index in (2 * kind + 1, 2 * kind):
                out.start(outs[index].at[:, high], targets[index].at[:, high])
    out.wait()


def advance_kernel(ids_ref, keep_there, got_there, keep_here, got_here, send_ref, next_ref):
    send_ref[...] = (keep_there[...].astype(F32) + got_there[...].astype(F32)).astype(BF16)
    next_ref[...] = (keep_here[...].astype(F32) + got_here[...].astype(F32)).astype(BF16)


def advance_call(ids, keep, got, kind, step):
    count, rows, columns = keep.shape[0] // 2, *keep.shape[1:]

    def half(there):
        def index_map(index, ids_ref):
            mine = ids_ref[2 + bits_in_order(kind, ids_ref[0])[step]]
            return ((1 - mine if there else mine) * count + index, 0, 0)

        return pl.BlockSpec((1, rows, columns), index_map)

    out = pl.BlockSpec((1, rows, columns), lambda index, ids_ref: (index, 0, 0))
    shape = shape_bf16(count, rows, columns)
    return pl.pallas_call(
        advance_kernel,
        out_shape=(shape, shape),
        grid_spec=pltpu.PrefetchScalarGridSpec(
            num_scalar_prefetch=1,
            grid=(count,),
            in_specs=[half(True), half(True), half(False), half(False)],
            out_specs=(out, out),
        ),
        compiler_params=pltpu.CompilerParams(vmem_limit_bytes=16 * 1024 * 1024),
        cost_estimate=pl.CostEstimate(flops=COST, bytes_accessed=10**6, transcendentals=0),
        name="advance",
    )(ids, keep, got, keep, got)


def partial_kernel(
    ids_ref, act_ref, gp_ref, w1_mine, w1_theirs, w2, own_ref, their_ref, w1_ref, w2_ref, sems
):
    core = ids_ref[0]
    half = act_ref.shape[1]
    rows, width = own_ref.shape[1:]
    length = width // 3
    seconds = []
    for chunk in range(3):
        here = pl.ds(chunk * length, length)
        seconds.append(pltpu.make_async_copy(w2.at[:, here], w2_ref.at[:, here], sems.at[2 + chunk]))
        seconds[-1].start()
    mine = w1_mine.at[:, pl.ds(pl.multiple_of(core * half, 128), half)]
    firsts = start_rows(core, mine, w1_theirs, w1_ref, sems, 0)
    for index in range(2):
        for chunk in range(3):
            here = slice(chunk * length, (chunk + 1) * length)
            if index == 0:
                seconds[chunk].wait()
                value = product(act_ref[...], w2_ref[:, here])
            else:
                if chunk == 0:
                    for copy in firsts:
                        copy.wait()
                value = product_back(gp_ref[...], w1_ref[here, :])
            own_ref[index, :, here] = value[:rows]
            their_ref[index, :, here] = value[rows:]


def middle_back_kernel(
    ids_ref,
    mine_ref,
    theirs_ref,
    cot_mine_ref,
    cot_theirs_ref,
    mod_ref,
    attn_ref,
    part_ref,
    got_ref,
    wp_mine,
    wp_theirs,
    q_ref,
    k_ref,
    v_ref,
    log_ref,
    grad_middle_out,
    gq_out,
    gk_out,
    gv_out,
    g_mine_ref,
    g_send_ref,
    sums_ref,
    wp_ref,
    ga_ref,
    grad_middle_ref,
    gq_ref,
    gk_ref,
    gv_ref,
    sems,
    out_sems,
):
    out = Outgoing(out_sems)
    core = ids_ref[0]
    copies = start_rows(core, wp_mine, wp_theirs, wp_ref, sems, 0)
    rows, width = q_ref.shape
    size, part = width // HEADS, width // 2
    _, _, gate_attn, _, scale_mlp, _ = pieces_of(mod_ref, width)
    tokens = jnp.concatenate([mine_ref[...], theirs_ref[...]], 0).astype(F32)
    cot = jnp.concatenate([cot_mine_ref[...], cot_theirs_ref[...]], 0).astype(F32)
    grad_out = jnp.where(valid_slots(ids_ref, rows, 0), cot, 0.0)
    grad_h = part_ref[1] + got_ref[1]
    attn = attn_ref[...]
    normed, inverse = normalize(tokens + gate_attn * attn)
    grad_middle = grad_out + normalize_back(normed, inverse, grad_h * (1.0 + scale_mlp))
    grad_middle_ref[...] = grad_middle
    out.start(grad_middle_ref, grad_middle_out)
    grad_attn = (gate_attn * grad_middle).astype(BF16)
    column_sum = lambda array: jnp.sum(array, 0, keepdims=True)
    sums_ref[0:1] = column_sum(grad_middle * attn)
    sums_ref[1:2] = column_sum(grad_h)
    sums_ref[2:3] = column_sum(grad_h * normed)
    sums_ref[3:4] = column_sum(grad_attn.astype(F32))
    for copy in copies:
        copy.wait()
    ga_ref[...] = product_back(grad_attn, wp_ref[...]).astype(BF16)

    valid = valid_slots(ids_ref, rows, 1)
    scale = size ** (-0.5)
    for head in range(HEADS):
        columns, own = head_window(head, size)
        query = q_ref[:, columns]
        key = k_ref[:, columns]
        grad = ga_ref[:, columns]
        own_query = jnp.where(own, query.astype(F32), 0.0).astype(BF16)
        own_grad = jnp.where(own, grad.astype(F32), 0.0).astype(BF16)
        scores = jnp.where(valid, product_back(own_query, key) * scale, MASKED)
        probs = jnp.exp(scores - log_ref[:, head : head + 1])
        grad_probs = product_back(own_grad, v_ref[:, columns])
        inner = jnp.sum(probs * grad_probs, -1, keepdims=True)
        grad_scores = (probs * (grad_probs - inner)).astype(BF16)
        grad_query = product(grad_scores, key) * scale
        grad_key = transpose_product(grad_scores, query) * scale
        grad_value = transpose_product(probs.astype(BF16), grad)
        gq_ref[:, columns] = jnp.where(own, grad_query, gq_ref[:, columns].astype(F32)).astype(BF16)
        gk_ref[:, columns] = jnp.where(own, grad_key, gk_ref[:, columns].astype(F32)).astype(BF16)
        gv_ref[:, columns] = jnp.where(own, grad_value, gv_ref[:, columns].astype(F32)).astype(BF16)
    for source, target in ((gq_ref, gq_out), (gk_ref, gk_out), (gv_ref, gv_out)):
        out.start(source, target)
    sums_ref[4:5] = column_sum(gq_ref[...].astype(F32))
    sums_ref[5:6] = column_sum(gv_ref[...].astype(F32))

    @pl.when(core == 0)
    def _():
        fill_half(0, g_mine_ref, grad_attn, gq_ref, gk_ref, gv_ref, width, part)
        fill_half(1, g_send_ref, grad_attn, gq_ref, gk_ref, gv_ref, width, part)

    @pl.when(core == 1)
    def _():
        fill_half(1, g_mine_ref, grad_attn, gq_ref, gk_ref, gv_ref, width, part)
        fill_half(0, g_send_ref, grad_attn, gq_ref, gk_ref, gv_ref, width, part)
    out.wait()


def fill_half(index, fill, grad_attn, gq_ref, gk_ref, gv_ref, width, part):
    if index == 0:
        fill[:, :width] = gq_ref[...]
        fill[:, width : width + part] = gk_ref[:, :part]
    else:
        fill[:, :part] = gk_ref[:, part:]
        fill[:, part : part + width] = gv_ref[...]
    fill[:, width + part :] = grad_attn[:, index * part : (index + 1) * part]


def qkv_grad_kernel(ids_ref, g_mine_ref, g_got_ref, both_ref, both_got_ref, *rest):
    targets, outs, total_ref, out_sems = rest[:4], rest[4:8], rest[8], rest[9]
    out = Outgoing(out_sems)
    width = both_ref.shape[2]
    grads = jnp.concatenate([g_mine_ref[...], g_got_ref[...]], 0)
    h_attn = jnp.concatenate([both_ref[0], both_got_ref[0]], 0)
    attended = jnp.concatenate([both_ref[1], both_got_ref[1]], 0)
    wide = 3 * width // 2
    rows, length = outs[0].shape[1], total_ref.shape[1]
    for chunk in (2, 0, 1):
        start = chunk * length
        if start + length <= wide:
            total_ref[...] = transpose_product(h_attn, grads[:, start : start + length])
            kind, columns = NEAR, slice(start, start + length)
        else:
            cut_at = wide - start
            total_ref[:, :cut_at] = transpose_product(h_attn, grads[:, start:wide])
            total_ref[:, cut_at:] = transpose_product(attended, grads[:, wide:])
            kind, columns = FAR, slice(0, length)
        store_halves(
            rows_of(total_ref, rows, 0, rows), kind, ids_ref, outs[2 * kind], outs[2 * kind + 1], columns
        )
        for index in (2 * kind + 1, 2 * kind):
            out.start(outs[index].at[:, :, columns], targets[index].at[:, :, columns])
    out.wait()


def last_kernel(
    ids_ref,
    mine_ref,
    theirs_ref,
    cot_mine_ref,
    cot_theirs_ref,
    mod_ref,
    attn_ref,
    part_ref,
    got_ref,
    fc2_bias_ref,
    wq_mine,
    wq_theirs,
    gq_ref,
    gk_ref,
    gv_ref,
    grad_middle_ref,
    sums_ref,
    result_ref,
    input_grad_ref,
    mod_grad_ref,
    wq_ref,
    sems,
):
    core = ids_ref[0]
    copies = start_rows(core, wq_mine, wq_theirs, wq_ref, sems, 0)
    rows, width = gq_ref.shape
    _, scale_attn, gate_attn, _, _, gate_mlp = pieces_of(mod_ref, width)
    tokens = jnp.concatenate([mine_ref[...], theirs_ref[...]], 0).astype(F32)
    cot = jnp.concatenate([cot_mine_ref[...], cot_theirs_ref[...]], 0).astype(F32)
    valid = valid_slots(ids_ref, rows, 0)
    mlp = part_ref[0] + got_ref[0] + fc2_bias_ref[...].astype(F32)
    middle = tokens + gate_attn * attn_ref[...]
    result_ref[...] = jnp.where(valid, middle + gate_mlp * mlp, 0.0).astype(BF16)
    column_sum = lambda array: jnp.sum(array, 0, keepdims=True)
    gate_mlp_sum = column_sum(jnp.where(valid, cot, 0.0) * mlp)
    normed, inverse = normalize(tokens)
    for copy in copies:
        copy.wait()
    grad_h = product_back(gq_ref[...], wq_ref[:, :width])
    grad_h += product_back(gk_ref[...], wq_ref[:, width : 2 * width])
    grad_h += product_back(gv_ref[...], wq_ref[:, 2 * width :])
    input_grad_ref[...] = grad_middle_ref[...] + normalize_back(
        normed, inverse, grad_h * (1.0 + scale_attn)
    )
    parts = (
        column_sum(grad_h),
        column_sum(grad_h * normed),
        sums_ref[0:1],
        sums_ref[1:2],
        sums_ref[2:3],
        gate_mlp_sum,
    )
    for index, value in enumerate(parts):
        mod_grad_ref[:, index * width : (index + 1) * width] = value


def partners(bit, count):
    return [(index, index ^ (1 << bit)) for index in range(count)]


def reduce_chunk(values_in, order, count):
    bits = count.bit_length() - 1
    place = lax.axis_index("dp")
    left = list(range(bits - 1, -1, -1))
    current = values_in.reshape((2,) * bits + values_in.shape[1:])
    for step, bit in enumerate(order):
        mine = (place >> bit) & 1
        axis = left.index(bit)
        send = pick(current, 1 - mine, axis).astype(BF16)
        keep = pick(current, mine, axis)
        left.pop(axis)
        got = lax.ppermute(send, "dp", partners(bit, count))
        current = keep.astype(F32) + got.astype(F32)
        if step < bits - 1:
            current = current.astype(BF16)
    return current


def reduce_scatter(values_in):
    count = lax.axis_size("dp")
    rows = values_in.shape[0] // count
    blocks = values_in.reshape(count, rows, values_in.shape[1])
    return reduce_chunk(blocks, range(count.bit_length() - 1), count)


class Flow:
    def __init__(self, ids, kind, keep, send):
        self.ids, self.kind, self.step = ids, kind, 0
        self.keep = keep
        self.send(send)

    def send(self, array):
        pairs = []
        for core in range(2):
            bit = bits_in_order(self.kind, core)[self.step]
            pairs += [(2 * place + core, 2 * (place ^ (1 << bit)) + core) for place in range(16)]
        self.got = lax.ppermute(array, ("dp", "blk"), pairs)

    def advance(self, token):
        got = after(self.got, token)
        self.step += 1
        if self.step == 4:
            self.total = (self.keep.astype(F32) + got.astype(F32))[0]
            return self.total
        send, self.keep = advance_call(self.ids, self.keep, got, self.kind, self.step)
        self.send(send)
        return send


class Gather:
    def __init__(self, array):
        self.array, self.bit, self.got = array, 0, None
        self.count = lax.axis_size("dp")
        self.send()

    def send(self):
        bits = self.count.bit_length() - 1
        self.got = lax.ppermute(self.array, "dp", partners(bits - 1 - self.bit, self.count))

    def advance(self, token):
        self.array = jnp.concatenate([self.array, after(self.got, token)], 0)
        self.bit += 1
        if 1 << self.bit < self.count:
            self.send()
        return self.array


def on_device(
    inputs,
    conditioning,
    grid_sizes,
    ada_weight,
    ada_bias,
    qkv_weight,
    qv_bias,
    proj_weight,
    proj_bias,
    fc1_weight,
    fc1_bias,
    fc2_weight,
    fc2_bias,
    cotangent,
):
    images, strip, width = inputs.shape
    data_count = lax.axis_size("dp")
    core = lax.axis_index("blk")
    other = 1 - core
    place = lax.axis_index("dp")
    part = ada_weight.shape[0]
    hidden = fc1_weight.shape[1]
    half_hidden = hidden // 2
    rows = images * strip
    split = data_count == 16
    area = pick(grid_sizes[:, 0] * grid_sizes[:, 1], core)
    ids = jnp.stack([core, area] + [(place >> bit) & 1 for bit in range(4)]).astype(jnp.int32)

    pair = jnp.stack([pick(inputs, other), pick(cotangent, other)])
    pair = swap(pair)
    mine_inputs, their_inputs = pick(inputs, core), pair[0]
    mine_cot, their_cot = pick(cotangent, core), pair[1]
    qkv_theirs = swap(qkv_weight)
    proj_theirs = swap(proj_weight)
    fc1_theirs = swap(columns_of(fc1_weight, other, half_hidden))

    cond_f32 = conditioning.astype(F32)
    silu_cond, silu_back = jax.vjp(jax.nn.silu, cond_f32)
    silu_low = silu_cond.astype(BF16)
    modulation_part = product(columns_of(silu_low, core, part), ada_weight)
    modulation = modulation_part + swap(modulation_part) + ada_bias.astype(F32)
    own_modulation = pick(modulation, core)[None, :]
    gate_mlp = own_modulation[:, 5 * width :]

    near = jnp.arange(strip, dtype=jnp.int32)
    valid = (jnp.concatenate([core * strip + near, other * strip + near]) < area)[:, None]
    cot = jnp.concatenate([mine_cot, their_cot], 0).astype(F32)
    grad_mlp = (gate_mlp * jnp.where(valid, cot, 0.0)).astype(BF16)
    grad_mlp_other = swap(grad_mlp)

    square = shape_bf16(rows, width)
    sems = lambda count: pltpu.SemaphoreType.DMA((count,))
    outs = [shape_bf16(2, rows, width), square, square, square, shape_f32(rows, 128), shape_f32(rows, width)]
    buffers = lambda shapes: [pltpu.VMEM(shape.shape, shape.dtype) for shape in shapes]
    both, query, key, value, logs, attn, h_mlp = call(
        front_kernel,
        [(out, "hbm") for out in outs] + [square],
        (
            after(mine_inputs, grad_mlp_other),
            their_inputs,
            own_modulation,
            (qkv_weight, "hbm"),
            (qkv_theirs, "hbm"),
            (proj_weight, "hbm"),
            (proj_theirs, "hbm"),
            qv_bias[None, :],
            proj_bias[None, :],
        ),
        [pltpu.VMEM((width, 3 * width), BF16), pltpu.VMEM((width, width), BF16)] + buffers(outs) + [sems(4), sems(7)],
        name="front",
        prefetch=(ids,),
    )
    h_mlp_other = swap(h_mlp)
    both_got = swap(after(both, h_mlp_other))

    length = half_hidden // 3
    block = width // 16
    weights = ((fc1_weight, "hbm"), (fc1_theirs, "hbm"), (fc2_weight, "hbm"))
    room = [pltpu.VMEM((width, half_hidden), BF16), pltpu.VMEM((half_hidden, width), BF16)]
    wide = shape_bf16(2 * rows, half_hidden)
    flowing = [(shape_bf16(8, block, half_hidden), "hbm")] * 2 if split else []
    staged = [pltpu.VMEM((3, 8, block, length), BF16)] * 2 + [sems(6)] if split else []
    results = call(
        hidden_kernel,
        [wide, wide, shape_f32(1, half_hidden)] + flowing,
        (h_mlp, h_mlp_other, grad_mlp, grad_mlp_other, *weights, fc1_bias[None, :]),
        staged + room + [pltpu.VMEM((width, length), F32), sems(9)],
        name="hidden",
        prefetch=(ids,),
        limit=32,
    )
    act, grad_pre, fc1_bias_part = results[:3]
    act_got = swap(act)
    if split:
        fc1_flow = Flow(ids, NEAR, *results[3:])
    pair_f32 = shape_f32(2, rows, width)
    own_part, their_part = call(
        partial_kernel,
        (pair_f32, pair_f32),
        (after(act, both_got), grad_pre, *weights),
        room + [sems(5)],
        name="partial",
        prefetch=(ids,),
        limit=32,
    )
    got_part = swap(their_part)
    token = their_part
    if split:
        stripes = hidden // 16 // 6
        near, far = shape_bf16(4, 2, stripes, width), shape_bf16(4, 2, 2 * stripes, width)
        outs = [near, near, far, far]
        results = call(
            fc2_grad_kernel,
            [(out, "hbm") for out in outs],
            (after(grad_mlp, token), grad_mlp_other, act, act_got),
            buffers(outs)
            + [pltpu.VMEM((2 * rows, part), BF16)] * 2
            + [pltpu.VMEM((half_hidden, part), F32), sems(8)],
            name="fc2_grad",
            prefetch=(ids,),
        )
        results = [array.reshape(8, *array.shape[2:]) for array in results]
        fc2_near, fc2_far = Flow(ids, NEAR, *results[:2]), Flow(ids, FAR, *results[2:])
        token = results[1]

    pads = shape_bf16(rows, 4 * part)
    outs = [shape_f32(rows, width), square, square, square]
    grad_middle, grad_query, grad_key, grad_value, g_mine, g_send, sums = call(
        middle_back_kernel,
        [(out, "hbm") for out in outs] + [pads, pads, shape_f32(8, width)],
        (
            mine_inputs,
            their_inputs,
            mine_cot,
            their_cot,
            own_modulation,
            attn,
            after(own_part, token),
            got_part,
            (proj_weight, "hbm"),
            (proj_theirs, "hbm"),
            query,
            key,
            value,
            logs,
        ),
        [pltpu.VMEM((width, width), BF16), pltpu.VMEM((rows, width), BF16)] + buffers(outs) + [sems(2), sems(4)],
        name="middle_back",
        prefetch=(ids,),
    )
    g_got = swap(g_send)
    token = g_send
    if split:
        token = fc1_flow.advance(token)
        near, far = shape_bf16(8, block, 2 * length), shape_bf16(8, block, length)
        outs = [near, near, far, far]
        results = call(
            qkv_grad_kernel,
            [(out, "hbm") for out in outs],
            (after(g_mine, token), g_got, both, both_got),
            buffers(outs) + [pltpu.VMEM((width, length), F32), sems(6)],
            name="qkv_grad",
            prefetch=(ids,),
        )
        qkv_near, qkv_far = Flow(ids, NEAR, *results[:2]), Flow(ids, FAR, *results[2:])
        token = fc2_near.advance(results[1])

    result, input_grad, mod_sums = call(
        last_kernel,
        (square, shape_f32(rows, width), shape_f32(1, 6 * width)),
        (
            mine_inputs,
            their_inputs,
            mine_cot,
            their_cot,
            own_modulation,
            attn,
            own_part,
            got_part,
            fc2_bias[None, :],
            (qkv_weight, "hbm"),
            (qkv_theirs, "hbm"),
            after(grad_query, token),
            grad_key,
            grad_value,
            grad_middle,
            sums,
        ),
        (pltpu.VMEM((width, 3 * width), BF16), sems(2)),
        name="last",
        prefetch=(ids,),
    )
    def advance(token, *flows):
        for flow in flows:
            token = flow.advance(token)
        return token

    token = mod_sums
    if split:
        token = advance(token, fc2_far, fc1_flow)

    together = lambda array, axis: lax.all_gather(array, "blk", axis=axis, tiled=True)
    modulation_low = together(after(mod_sums, token).astype(BF16), 0)
    silu_grad = together(product_back(modulation_low, ada_weight), 1)
    cond_grad = silu_back(silu_grad)[0]
    by_device = lambda array: array.reshape(data_count, -1)
    image_bias = jnp.concatenate(
        [by_device(sums[4:6]), by_device(sums[3]), by_device(jnp.sum(after(grad_mlp, token).astype(F32), 0))], 1
    )
    small = jnp.concatenate(
        [
            silu_low,
            columns_of(modulation_low, core, 3 * width),
            image_bias.astype(BF16).reshape(images, -1),
            fc1_bias_part.astype(BF16).reshape(images, -1),
        ],
        1,
    )
    gather = Gather(small)
    back = lambda array: in_order(core, array[None, :strip], swap(array[None, strip:]))
    if split:
        token = advance(small, qkv_near, qkv_far, gather)
        output = back(after(result, token))
        token = advance(token, fc2_near, fc2_far, gather)
        input_grad = back(after(input_grad, token))
        token = advance(token, fc1_flow, qkv_near, qkv_far, gather)
        token = advance(token, fc2_near, fc2_far, gather)
    else:
        output, input_grad = back(result), back(input_grad)
        while 1 << gather.bit < data_count:
            token = gather.advance(token)
    gathered = gather.array
    silu_rows = columns_of(gathered[:, :width], place, width // data_count)
    modulation_all = gathered[:, width : 4 * width]
    ada_grad = transpose_product(silu_rows, modulation_all)
    bias_all = gathered[:, 4 * width :].astype(F32)
    image_count = image_bias.size // images
    image_sums = jnp.sum(bias_all[:, :image_count].reshape(data_count, data_count, -1), 0)
    hidden_sums = jnp.sum(bias_all[:, image_count:].reshape(data_count, data_count // 2, -1), 0)
    ada_sums = jnp.sum(modulation_all.astype(F32), 0).reshape(data_count // 2, -1)
    near_half = jnp.where(place // (data_count // 2) == core, 1.0, 0.0)
    in_half = place % (data_count // 2)
    bias_sums = lax.psum(
        jnp.concatenate(
            [pick(ada_sums, in_half) * near_half, pick(image_sums, place), pick(hidden_sums, in_half) * near_half]
        ),
        "blk",
    )
    ends, at = [], 0
    for count in [6 * width, 2 * width, width, width]:
        at += count // data_count
        ends.append(at)
    ada_bias_grad, qv_bias_grad, proj_bias_grad, fc2_bias_grad, fc1_bias_grad = jnp.split(bias_sums, ends)
    biases = (ada_bias_grad, qv_bias_grad, proj_bias_grad, fc1_bias_grad, fc2_bias_grad)

    if split:
        token = advance(token, fc1_flow, qkv_near, qkv_far, fc2_near, fc2_far, qkv_near, qkv_far)
        fc1_grad = fc1_flow.total
        fc2_total = jnp.concatenate([fc2_near.total, fc2_far.total], 0)
        fc2_grad = jnp.concatenate([fc2_total[:, :part], fc2_total[:, part:]], 0)
        qkv_grad = jnp.concatenate([qkv_near.total, qkv_far.total[:, : 3 * part - 2 * length]], 1)
        proj_grad = qkv_far.total[:, 3 * part - 2 * length :]
    else:
        h_mlp_all = jnp.concatenate([h_mlp, h_mlp_other], 0)
        fc1_grad = reduce_scatter(transpose_product(h_mlp_all, grad_pre))
        grad_mlp_all = columns_of(jnp.concatenate([grad_mlp, grad_mlp_other], 0), core, part)
        turned = jnp.concatenate([grad_mlp_all[rows:], grad_mlp_all[:rows]], 0)
        fc2_term = in_order(
            core,
            transpose_product(act, grad_mlp_all).astype(BF16),
            transpose_product(act_got, turned).astype(BF16),
        )
        fc2_grad = reduce_scatter(fc2_term)
        g_all = jnp.concatenate([g_mine, g_got], 0)
        h_attn_all = jnp.concatenate([both[0], both_got[0]], 0)
        attended_all = jnp.concatenate([both[1], both_got[1]], 0)
        qkv_grad = reduce_scatter(transpose_product(h_attn_all, g_all[:, : 3 * part]))
        proj_grad = reduce_scatter(transpose_product(attended_all, g_all[:, 3 * part :]))
    return (
        output,
        input_grad,
        cond_grad,
        ada_grad,
        biases[0],
        qkv_grad,
        biases[1],
        proj_grad,
        biases[2],
        fc1_grad,
        biases[3],
        fc2_grad,
        biases[4],
    )


def solution(mesh):
    rows = P("dp", "blk", None)
    weight = P("blk", None)
    grads = (P("dp", "blk"), P("dp"))
    placed = (rows, P("dp", None), P("dp", None)) + (weight, P()) * 5 + (rows,)
    return jax.shard_map(
        on_device,
        mesh=mesh,
        in_specs=placed,
        out_specs=(rows, rows, P("dp", None)) + grads * 5,
        check_vma=False,
    )
```

```python
import functools
import math

import jax
import jax.numpy as jnp
from jax import lax
from jax.experimental import pallas as pl
from jax.experimental.pallas import tpu as pltpu
from jax.sharding import PartitionSpec as P

HEADS = 16
EPS = 1e-06
MASKED = -1e30
F32 = jnp.float32
BF16 = jnp.bfloat16
GELU_A = math.sqrt(2.0 / math.pi)
GELU_B = 0.044715
NEAR, FAR = 0, 1
COSTS = {}
PLACES = {"hbm": pltpu.HBM, "smem": pltpu.SMEM}


def product(left, right):
    return jnp.dot(left, right, preferred_element_type=F32)


def transpose_product(left, right):
    return lax.dot_general(left, right, (((0,), (0,)), ((), ())), preferred_element_type=F32)


def product_back(left, right):
    return lax.dot_general(left, right, (((1,), (1,)), ((), ())), preferred_element_type=F32)


def swap(values_in):
    return lax.ppermute(values_in, "blk", [(0, 1), (1, 0)])


def pick(values_in, index, axis=0):
    return lax.dynamic_index_in_dim(values_in, index, axis, keepdims=False)


def columns_of(values_in, index, length):
    return lax.dynamic_slice_in_dim(values_in, index * length, length, 1)


def in_order(core, mine, theirs, axis=0):
    first = jnp.where(core == 0, mine, theirs)
    second = jnp.where(core == 0, theirs, mine)
    return jnp.concatenate([first, second], axis)


def after(values_in, token):
    return lax.optimization_barrier((values_in, token))[0]


def call(kernel, outs, ins, scratch=(), name=None, wait_for=()):
    count, waits = len(ins), len(wait_for)
    ins = [*ins, *hbm(*wait_for)]
    body = lambda *refs: kernel(*refs[:count], *refs[count + waits :])
    place = lambda item: pl.BlockSpec(memory_space=PLACES[item[1]] if isinstance(item, tuple) else pltpu.VMEM)
    plain = lambda item: item[0] if isinstance(item, tuple) else item
    return pl.pallas_call(
        body,
        out_shape=tuple(plain(out) for out in outs),
        in_specs=[place(item) for item in ins],
        out_specs=tuple(place(out) for out in outs),
        scratch_shapes=list(scratch),
        compiler_params=pltpu.CompilerParams(vmem_limit_bytes=58 * 1024 * 1024),
        cost_estimate=pl.CostEstimate(flops=COSTS.get(name, 10**11), bytes_accessed=10**6, transcendentals=0),
        name=name,
    )(*[plain(item) for item in ins])


def hbm(*items):
    return [(item, "hbm") for item in items]


class Copies:
    def __init__(self, sems):
        self.sems, self.copies = sems, []

    def start(self, source, target):
        copy = pltpu.make_async_copy(source, target, self.sems.at[len(self.copies)])
        copy.start()
        self.copies.append(copy)
        return copy

    def wait(self):
        for copy in self.copies:
            copy.wait()


def shape_f32(*dims):
    return jax.ShapeDtypeStruct(dims, F32)


def shape_bf16(*dims):
    return jax.ShapeDtypeStruct(dims, BF16)


def row_mean(values_in):
    return jnp.mean(values_in, -1, keepdims=True)


def normalize(values_in):
    centred = values_in - row_mean(values_in)
    inverse = lax.rsqrt(row_mean(centred * centred) + EPS)
    return centred * inverse, inverse


def normalize_back(normed, inverse, grad):
    return inverse * (grad - row_mean(grad) - normed * row_mean(grad * normed))


def head_window(head, size):
    low, high = head * size, (head + 1) * size
    start, stop = low // 128 * 128, -(-high // 128) * 128
    lane = lax.broadcasted_iota(jnp.int32, (1, stop - start), 1) + start
    return slice(start, stop), (lane >= low) & (lane < high)


def device_bits():
    place = lax.axis_index("dp")
    return lax.axis_index("blk"), lambda bit: (place >> bit) & 1


def valid_slots(core, sizes_ref, rows, dimension):
    strip = rows // 2
    shape = (1, rows) if dimension == 1 else (rows, 1)
    near = lax.broadcasted_iota(jnp.int32, shape, dimension)
    position = jnp.where(near < strip, core * strip + near, (1 - core) * strip + near - strip)
    return position < sizes_ref[core, 0] * sizes_ref[core, 1]


def start_rows(core, mine, theirs, target, copies):
    rows = mine.shape[0]
    at = lambda which: target.at[pl.ds(pl.multiple_of(which * rows, 64), rows)]
    return copies.start(mine, at(core)), copies.start(theirs, at(1 - core))


def wait_all(*copies):
    for copy in copies:
        copy.wait()


def pieces_of(mod_ref, width):
    return [mod_ref[0:1, index * width : (index + 1) * width] for index in range(6)]


def column_sum(array):
    return jnp.sum(array, 0, keepdims=True)


def prelude_kernel(
    cond_ref, inputs, cot, ada, w1, pair_ref, w1_ref, part_ref, silu_ref, ada_ref, ada_sems, sems
):
    core, _ = device_bits()
    other = 1 - core
    width, part = inputs.shape[2], ada.shape[0]
    half = w1_ref.shape[1]
    arriving, leaving = Copies(ada_sems), Copies(sems)
    leaving.start(inputs.at[other], pair_ref.at[0])
    leaving.start(cot, pair_ref.at[pl.ds(1, 2)])
    for piece in range(6):
        here = slice(piece * width, (piece + 1) * width)
        arriving.start(ada.at[:, here], ada_ref.at[:, here])
    leaving.start(w1.at[:, pl.ds(pl.multiple_of(other * half, 128), half)], w1_ref)
    cond = cond_ref[...].astype(F32)
    silu = (cond / (1.0 + jnp.exp(-cond))).astype(BF16)
    silu_ref[...] = silu
    low = silu.astype(F32)
    own = jnp.where(core == 0, low[:, :part], low[:, part:]).astype(BF16)
    for piece in range(6):
        here = slice(piece * width, (piece + 1) * width)
        arriving.copies[piece].wait()
        part_ref[:, here] = product(own, ada_ref[:, here])
    leaving.wait()


def front_kernel(
    sizes_ref,
    part_ref,
    got_ref,
    ada_bias_ref,
    qv_bias_ref,
    proj_bias_ref,
    inputs,
    pair,
    wq_mine,
    wq_theirs,
    wp_mine,
    wp_theirs,
    both_out,
    q_out,
    k_out,
    v_out,
    log_out,
    attn_out,
    h_mlp_ref,
    mod_ref,
    tokens_ref,
    wq_ref,
    wp_ref,
    both_ref,
    q_ref,
    k_ref,
    v_ref,
    log_ref,
    attn_ref,
    sems,
    out_sems,
):
    core, _ = device_bits()
    rows, width = q_ref.shape
    size, strip = width // HEADS, rows // 2
    arriving, out = Copies(sems), Copies(out_sems)
    token_copies = (
        arriving.start(inputs.at[core], tokens_ref.at[pl.ds(0, strip)]),
        arriving.start(pair.at[0], tokens_ref.at[pl.ds(strip, strip)]),
    )
    thirds = [pl.ds(index * width, width) for index in range(3)]
    q_copies = [
        start_rows(core, wq_mine.at[:, here], wq_theirs.at[:, here], wq_ref.at[:, here], arriving) for here in thirds
    ]
    p_copies = start_rows(core, wp_mine, wp_theirs, wp_ref, arriving)
    ada_bias = ada_bias_ref[...].astype(F32)
    for row, which in enumerate((core, 1 - core)):
        mod_ref[row : row + 1] = part_ref[pl.ds(which, 1), :] + got_ref[pl.ds(which, 1), :] + ada_bias
    shift_attn, scale_attn, gate_attn, shift_mlp, scale_mlp, _ = pieces_of(mod_ref, width)
    wait_all(*token_copies)
    tokens = tokens_ref[...].astype(F32)
    normed, _ = normalize(tokens)
    h_attn = (normed * (1.0 + scale_attn) + shift_attn).astype(BF16)
    both_ref[0] = h_attn
    out.start(both_ref.at[0], both_out.at[0])
    q_bias = qv_bias_ref[:, :width].astype(F32)
    v_bias = qv_bias_ref[:, width:].astype(F32)
    wait_all(*q_copies[0])
    q_ref[...] = (product(h_attn, wq_ref[:, :width]) + q_bias).astype(BF16)
    wait_all(*q_copies[1])
    k_ref[...] = product(h_attn, wq_ref[:, width : 2 * width]).astype(BF16)
    wait_all(*q_copies[2])
    v_ref[...] = (product(h_attn, wq_ref[:, 2 * width :]) + v_bias).astype(BF16)
    for source, target in ((q_ref, q_out), (k_ref, k_out), (v_ref, v_out)):
        out.start(source, target)

    valid = valid_slots(core, sizes_ref, rows, 1)
    lane = lax.broadcasted_iota(jnp.int32, (1, 128), 1)
    logs = jnp.zeros((rows, 128), F32)
    for head in range(HEADS):
        columns, own = head_window(head, size)
        query = jnp.where(own, q_ref[:, columns].astype(F32), 0.0).astype(BF16)
        scores = jnp.where(valid, product_back(query, k_ref[:, columns]) * size ** (-0.5), MASKED)
        largest = jnp.max(scores, -1, keepdims=True)
        exponent = jnp.exp(scores - largest)
        totals = jnp.sum(exponent, -1, keepdims=True)
        probs = (exponent / totals).astype(BF16)
        attended = product(probs, v_ref[:, columns])
        before = both_ref[1, :, columns].astype(F32)
        both_ref[1, :, columns] = jnp.where(own, attended, before).astype(BF16)
        logs = jnp.where(lane == head, largest + jnp.log(totals), logs)
    log_ref[...] = logs
    out.start(log_ref, log_out)
    out.start(both_ref.at[1], both_out.at[1])

    wait_all(*p_copies)
    proj_bias = proj_bias_ref[...].astype(F32)
    attn = product(both_ref[1], wp_ref[...]) + proj_bias
    attn_ref[...] = attn
    out.start(attn_ref, attn_out)
    normed_mlp, _ = normalize(tokens + gate_attn * attn)
    h_mlp_ref[...] = (normed_mlp * (1.0 + scale_mlp) + shift_mlp).astype(BF16)
    out.wait()


def bits_in_order(kind, core):
    return (core, 1 - core, 2, 3) if kind == NEAR else (2, core, 1 - core, 3)


def store_halves(read, kind, keep_ref, send_ref, columns=slice(None), high=None):
    core, bit_of = device_bits()
    order = bits_in_order(kind, core)
    mine = bit_of(order[0])
    for index in range(8 if high is None else 4):
        if high is None:
            base = ((index >> 2) << order[1]) + (((index >> 1) & 1) << order[2]) + ((index & 1) << order[3])
        else:
            base = ((index >> 1) << order[1]) + ((index & 1) << order[2])
        for target, value in ((keep_ref, mine), (send_ref, 1 - mine)):
            block = base + (value << order[0])
            target[index, :, columns] = read(block).astype(BF16)


def rows_of(total_ref, stride, first, count):
    return lambda block: total_ref[pl.ds(pl.multiple_of(block * stride + first, 8), count), :]


def hidden_kernel(
    sizes_ref,
    h_own_ref,
    h_other_ref,
    mod_ref,
    bias_ref,
    cot,
    pair,
    w1_mine,
    w1_theirs,
    w2,
    act_out,
    gm_out,
    own_out,
    their_out,
    hidden_bias_ref,
    out_bias_ref,
    *rest,
):
    core, _ = device_bits()
    other = 1 - core
    cot_ref, gm_ref, act_ref, gp_ref, w1_ref, w2_ref, part_ref, total_ref, sems, out_sems = rest[-10:]
    flowing = len(rest) > 11
    if flowing:
        keep_out, send_out, keep_ref, send_ref = rest[:4]
    else:
        gp_out = rest[0]
    length, half = total_ref.shape[1], act_ref.shape[1]
    rows, width = h_own_ref.shape
    arriving, out = Copies(sems), Copies(out_sems)
    cots = [
        arriving.start(source, cot_ref.at[at])
        for at, source in enumerate((cot.at[core], pair.at[1 + core], pair.at[1 + other], cot.at[other]))
    ]
    copies = []
    for start in range(0, half, length):
        here = pl.ds(start, length)
        mine = w1_mine.at[:, pl.ds(pl.multiple_of(core * half + start, 128), length)]
        second = arriving.start(w2.at[here], w2_ref.at[here])
        first = start_rows(core, mine, w1_theirs.at[:, here], w1_ref.at[:, here], arriving)
        copies.append((second, *first))
    wait_all(*cots)
    for row, which in enumerate((core, other)):
        array = jnp.concatenate([cot_ref[2 * row], cot_ref[2 * row + 1]], 0).astype(F32)
        valid = valid_slots(which, sizes_ref, rows, 0)
        gate = mod_ref[row : row + 1, 5 * width :]
        grad = (gate * jnp.where(valid, array, 0.0)).astype(BF16)
        gm_ref[row * rows : (row + 1) * rows] = grad
        if row == 0:
            out_bias_ref[...] = column_sum(grad.astype(F32))
    out.start(gm_ref, gm_out)
    h_all = jnp.concatenate([h_own_ref[...], h_other_ref[...]], 0)
    for chunk, start in enumerate(range(0, half, length)):
        wait_all(*copies[chunk])
        here = slice(start, start + length)
        at = pl.multiple_of(core * half + start, 128)
        bias = bias_ref[:, pl.ds(at, length)].astype(F32)
        grad_act = product_back(gm_ref[...], w2_ref[here, :])
        value = product(h_all, w1_ref[:, here]) + bias
        square = value * value
        tanh = jnp.tanh(GELU_A * value * (1.0 + GELU_B * square))
        half_up = 0.5 * (1.0 + tanh)
        act_ref[:, here] = (value * half_up).astype(BF16)
        out.start(act_ref.at[:, here], act_out.at[:, here])
        slope = half_up + 0.5 * value * (1.0 - tanh * tanh) * (GELU_A * (1.0 + 3.0 * GELU_B * square))
        grad_pre = (grad_act * slope).astype(BF16)
        gp_ref[:, here] = grad_pre
        hidden_bias_ref[:, here] = column_sum(grad_pre.astype(F32))
        if flowing:
            total_ref[...] = transpose_product(h_all, grad_pre)
            count = keep_ref.shape[2]
            store_halves(rows_of(total_ref, count, 0, count), NEAR, keep_ref.at[chunk], send_ref.at[chunk])
            out.start(send_ref.at[chunk], send_out.at[:, :, here])
            out.start(keep_ref.at[chunk], keep_out.at[:, :, here])
        else:
            out.start(gp_ref.at[:, here], gp_out.at[:, here])
    step = width // 3
    for index in range(2):
        for start in range(0, width, step):
            here = slice(start, start + step)
            if index == 0:
                part_ref[index, :, here] = product(act_ref[...], w2_ref[:, here])
            else:
                part_ref[index, :, here] = product_back(gp_ref[...], w1_ref[here, :])
        out.start(part_ref.at[index, pl.ds(rows, rows)], their_out.at[index])
        out.start(part_ref.at[index, pl.ds(0, rows)], own_out.at[index])
    out.wait()


def fc2_grad_kernel(
    act, act_got, gm, keep_out, send_out, act_ref, gm_ref, columns_ref, total_ref, keep_ref, send_ref, sems, out_sems
):
    core, _ = device_bits()
    arriving, out = Copies(sems), Copies(out_sems)
    rows, part = gm_ref.shape[0] // 2, columns_ref.shape[2]
    gm_copy = arriving.start(gm, gm_ref)
    length = act_ref.shape[2] // 3
    for side, source in enumerate((act, act_got)):
        for start in range(0, 3 * length, length):
            here = pl.ds(start, length)
            arriving.start(source.at[:, here], act_ref.at[side, :, here])
    gm_copy.wait()
    for index in range(2):

        @pl.when(core == index)
        def _():
            own = gm_ref[:rows, index * part : (index + 1) * part]
            other = gm_ref[rows:, index * part : (index + 1) * part]
            columns_ref[0, :rows] = own
            columns_ref[0, rows:] = other
            columns_ref[1, :rows] = other
            columns_ref[1, rows:] = own

    count = keep_ref.shape[2]
    for side in range(2):
        for index in range(3):
            arriving.copies[1 + 3 * side + index].wait()
            here = slice(index * length, (index + 1) * length)
            total_ref[here, :] = transpose_product(act_ref[side, :, here], columns_ref[side])
        for place in range(2):
            store_halves(
                rows_of(total_ref, 2 * count, place * count, count),
                FAR,
                keep_ref.at[side],
                send_ref.at[side],
                slice(place * part, (place + 1) * part),
                True,
            )
        high = core if side == 0 else 1 - core
        out.start(send_ref.at[side], send_out.at[:, high])
        out.start(keep_ref.at[side], keep_out.at[:, high])
    out.wait()


def advance_kernel(kind, step, keep, got, send_out, next_out, keep_ref, got_ref, sum_ref, sems, out_sems):
    core, bit_of = device_bits()
    mine = bit_of(bits_in_order(kind, core)[step])
    count = send_out.shape[0]
    arriving, out = Copies(sems), Copies(out_sems)
    halves = (1 - mine, mine)
    for index in range(2 * count):
        block = halves[index // count] * count + index % count
        arriving.start(keep.at[block], keep_ref.at[index])
        arriving.start(got.at[block], got_ref.at[index])
    for index in range(2 * count):
        wait_all(*arriving.copies[2 * index : 2 * index + 2])
        sum_ref[index] = (keep_ref[index].astype(F32) + got_ref[index].astype(F32)).astype(BF16)
        out.start(sum_ref.at[index], (send_out if index < count else next_out).at[index % count])
    out.wait()


def advance_call(keep, got, kind, step, token):
    count = keep.shape[0] // 2
    half = shape_bf16(count, *keep.shape[1:])
    buffer = pltpu.VMEM(keep.shape, BF16)
    return call(
        functools.partial(advance_kernel, kind, step),
        hbm(half, half),
        hbm(keep, got),
        (buffer, buffer, buffer, pltpu.SemaphoreType.DMA((4 * count,)), pltpu.SemaphoreType.DMA((2 * count,))),
        name="advance",
        wait_for=jax.tree.leaves(token),
    )


def join_kernel(first_ref, second_ref, out_ref):
    count = first_ref.shape[0]
    out_ref[:count] = first_ref[...]
    out_ref[count:] = second_ref[...]


def finish_kernel(keep_ref, got_ref, *outs):
    total = keep_ref[0].astype(F32) + got_ref[0].astype(F32)
    rows = total.shape[0]
    start = 0
    for out in outs:
        length = out.shape[1]
        for at in range(out.shape[0] // rows):
            out[at * rows : (at + 1) * rows] = total[:, start : start + length]
            start += length


def ada_kernel(gathered_ref, ada_ref, sums_ref, silu_ref):
    rows, width = gathered_ref.shape[0], silu_ref.shape[0]
    mine = ada_ref.shape[0]
    place = lax.axis_index("dp")
    silu_ref[...] = gathered_ref[:, :width].astype(F32).T
    own = silu_ref[pl.ds(pl.multiple_of(place * mine, 8), mine), :].astype(BF16)
    ada_ref[...] = product(own, gathered_ref[:, width : 4 * width])
    odd = lax.broadcasted_iota(jnp.int32, (2, rows), 1) % 2
    row = lax.broadcasted_iota(jnp.int32, (2, rows), 0)
    sums_ref[...] = product(jnp.where(odd == row, 1.0, 0.0).astype(BF16), gathered_ref[:, width:])


def silu_kernel(grad_ref, ada, out_ref, ada_ref, sems):
    arriving = Copies(sems)
    rows = ada.shape[0] // sems.shape[0]
    for start in range(0, ada.shape[0], rows):
        arriving.start(ada.at[pl.ds(start, rows)], ada_ref.at[pl.ds(start, rows)])
    arriving.wait()
    out_ref[...] = product_back(grad_ref[...], ada_ref[...])


def middle_back_kernel(
    sizes_ref,
    mod_ref,
    inputs,
    cot,
    pair,
    attn,
    own_part,
    got_part,
    wp_mine,
    wp_theirs,
    query_in,
    key_in,
    value_in,
    log_in,
    grad_middle_out,
    gq_out,
    gk_out,
    gv_out,
    g_mine_out,
    g_send_out,
    sums_ref,
    strips_ref,
    attn_ref,
    parts_ref,
    wp_ref,
    q_ref,
    k_ref,
    v_ref,
    log_ref,
    ga_ref,
    grad_middle_ref,
    gq_ref,
    gk_ref,
    gv_ref,
    g_mine_ref,
    g_send_ref,
    sems,
    out_sems,
):
    core, _ = device_bits()
    arriving, out = Copies(sems), Copies(out_sems)
    for at, source in enumerate((inputs.at[core], pair.at[0], cot.at[core], pair.at[1 + core])):
        arriving.start(source, strips_ref.at[at])
    for source, target in ((attn, attn_ref), (own_part.at[1], parts_ref.at[0]), (got_part.at[1], parts_ref.at[1])):
        arriving.start(source, target)
    first = list(arriving.copies)
    p_copies = start_rows(core, wp_mine, wp_theirs, wp_ref, arriving)
    later = [
        arriving.start(source, target)
        for source, target in ((query_in, q_ref), (key_in, k_ref), (value_in, v_ref), (log_in, log_ref))
    ]
    rows, width = q_ref.shape
    size, part = width // HEADS, width // 2
    _, _, gate_attn, _, scale_mlp, _ = pieces_of(mod_ref, width)
    wait_all(*first)
    tokens = jnp.concatenate([strips_ref[0], strips_ref[1]], 0).astype(F32)
    cotangent = jnp.concatenate([strips_ref[2], strips_ref[3]], 0).astype(F32)
    grad_out = jnp.where(valid_slots(core, sizes_ref, rows, 0), cotangent, 0.0)
    grad_h = parts_ref[0] + parts_ref[1]
    normed, inverse = normalize(tokens + gate_attn * attn_ref[...])
    grad_middle = grad_out + normalize_back(normed, inverse, grad_h * (1.0 + scale_mlp))
    grad_middle_ref[...] = grad_middle
    out.start(grad_middle_ref, grad_middle_out)
    grad_attn = (gate_attn * grad_middle).astype(BF16)
    sums_ref[0:1] = column_sum(grad_middle * attn_ref[...])
    sums_ref[1:2] = column_sum(grad_h)
    sums_ref[2:3] = column_sum(grad_h * normed)
    sums_ref[3:4] = column_sum(grad_attn.astype(F32))
    wait_all(*p_copies)
    ga_ref[...] = product_back(grad_attn, wp_ref[...]).astype(BF16)

    valid = valid_slots(core, sizes_ref, rows, 1)
    scale = size ** (-0.5)
    wait_all(*later)
    for head in range(HEADS):
        columns, own = head_window(head, size)
        query = q_ref[:, columns]
        key = k_ref[:, columns]
        grad = ga_ref[:, columns]
        own_query = jnp.where(own, query.astype(F32), 0.0).astype(BF16)
        own_grad = jnp.where(own, grad.astype(F32), 0.0).astype(BF16)
        scores = jnp.where(valid, product_back(own_query, key) * scale, MASKED)
        probs = jnp.exp(scores - log_ref[:, head : head + 1])
        grad_probs = product_back(own_grad, v_ref[:, columns])
        inner = jnp.sum(probs * grad_probs, -1, keepdims=True)
        grad_scores = (probs * (grad_probs - inner)).astype(BF16)
        grad_query = product(grad_scores, key) * scale
        grad_key = transpose_product(grad_scores, query) * scale
        grad_value = transpose_product(probs.astype(BF16), grad)
        gq_ref[:, columns] = jnp.where(own, grad_query, gq_ref[:, columns].astype(F32)).astype(BF16)
        gk_ref[:, columns] = jnp.where(own, grad_key, gk_ref[:, columns].astype(F32)).astype(BF16)
        gv_ref[:, columns] = jnp.where(own, grad_value, gv_ref[:, columns].astype(F32)).astype(BF16)
    for source, target in ((gq_ref, gq_out), (gk_ref, gk_out), (gv_ref, gv_out)):
        out.start(source, target)

    for which, refs in ((0, (g_mine_ref, g_send_ref)), (1, (g_send_ref, g_mine_ref))):

        @pl.when(core == which)
        def _():
            for index, fill in enumerate(refs):
                fill_half(index, fill, grad_attn, gq_ref, gk_ref, gv_ref, width, part)

    out.start(g_send_ref, g_send_out)
    out.start(g_mine_ref, g_mine_out)
    sums_ref[4:5] = column_sum(gq_ref[...].astype(F32))
    sums_ref[5:6] = column_sum(gv_ref[...].astype(F32))
    out.wait()


def fill_half(index, fill, grad_attn, gq_ref, gk_ref, gv_ref, width, part):
    if index == 0:
        fill[:, :width] = gq_ref[...]
        fill[:, width : width + part] = gk_ref[:, :part]
    else:
        fill[:, :part] = gk_ref[:, part:]
        fill[:, part : part + width] = gv_ref[...]
    fill[:, width + part :] = grad_attn[:, index * part : (index + 1) * part]


def qkv_grad_kernel(
    g_mine, g_got, both, both_got, keep_out, send_out, g_ref, x_ref, total_ref, keep_ref, send_ref, sems, out_sems
):
    arriving, out = Copies(sems), Copies(out_sems)
    rows, width = both.shape[1:]
    upper, lower = pl.ds(0, rows), pl.ds(rows, rows)
    arriving.start(both.at[0], x_ref.at[0, upper])
    arriving.start(both_got.at[0], x_ref.at[0, lower])
    arriving.start(g_mine, g_ref.at[upper])
    arriving.start(g_got, g_ref.at[lower])
    arriving.start(both.at[1], x_ref.at[1, upper])
    arriving.start(both_got.at[1], x_ref.at[1, lower])
    wide = 3 * width // 2
    count, length = keep_ref.shape[2], total_ref.shape[1]
    wait_all(*arriving.copies[:4])
    for chunk in range(3):
        start = chunk * length
        if start + length <= wide:
            total_ref[...] = transpose_product(x_ref[0], g_ref[:, start : start + length])
        else:
            wait_all(*arriving.copies[4:])
            cut_at = wide - start
            total_ref[:, :cut_at] = transpose_product(x_ref[0], g_ref[:, start:wide])
            total_ref[:, cut_at:] = transpose_product(x_ref[1], g_ref[:, wide:])
        store_halves(rows_of(total_ref, count, 0, count), NEAR, keep_ref.at[chunk], send_ref.at[chunk])
        here = pl.ds(start, length)
        out.start(send_ref.at[chunk], send_out.at[:, :, here])
        out.start(keep_ref.at[chunk], keep_out.at[:, :, here])
    out.wait()


def last_kernel(
    sizes_ref,
    mod_ref,
    bias_ref,
    sums_ref,
    inputs,
    cot,
    pair,
    attn,
    own_part,
    got_part,
    wq_mine,
    wq_theirs,
    gq_in,
    gk_in,
    gv_in,
    grad_middle_in,
    result_out,
    result_send_out,
    input_out,
    input_send_out,
    mod_grad_ref,
    strips_ref,
    attn_ref,
    parts_ref,
    wq_ref,
    gq_ref,
    gk_ref,
    gv_ref,
    grad_middle_ref,
    result_ref,
    input_ref,
    sems,
    out_sems,
):
    core, _ = device_bits()
    arriving, out = Copies(sems), Copies(out_sems)
    for at, source in enumerate((inputs.at[core], pair.at[0], cot.at[core], pair.at[1 + core])):
        arriving.start(source, strips_ref.at[at])
    for source, target in ((attn, attn_ref), (own_part.at[0], parts_ref.at[0]), (got_part.at[0], parts_ref.at[1])):
        arriving.start(source, target)
    first = list(arriving.copies)
    grads = [arriving.start(source, target) for source, target in ((gq_in, gq_ref), (gk_in, gk_ref), (gv_in, gv_ref))]
    q_copies = start_rows(core, wq_mine, wq_theirs, wq_ref, arriving)
    middle_copy = arriving.start(grad_middle_in, grad_middle_ref)
    rows, width = gq_ref.shape
    strip = rows // 2
    _, scale_attn, gate_attn, _, _, gate_mlp = pieces_of(mod_ref, width)
    wait_all(*first)
    tokens = jnp.concatenate([strips_ref[0], strips_ref[1]], 0).astype(F32)
    cotangent = jnp.concatenate([strips_ref[2], strips_ref[3]], 0).astype(F32)
    valid = valid_slots(core, sizes_ref, rows, 0)
    mlp = parts_ref[0] + parts_ref[1] + bias_ref[...].astype(F32)
    middle = tokens + gate_attn * attn_ref[...]
    result_ref[...] = jnp.where(valid, middle + gate_mlp * mlp, 0.0).astype(BF16)
    out.start(result_ref.at[pl.ds(strip, strip)], result_send_out)
    out.start(result_ref.at[pl.ds(0, strip)], result_out)
    gate_mlp_sum = column_sum(jnp.where(valid, cotangent, 0.0) * mlp)
    normed, inverse = normalize(tokens)
    wait_all(*grads, *q_copies)
    grad_h = product_back(gq_ref[...], wq_ref[:, :width])
    grad_h += product_back(gk_ref[...], wq_ref[:, width : 2 * width])
    grad_h += product_back(gv_ref[...], wq_ref[:, 2 * width :])
    middle_copy.wait()
    input_ref[...] = grad_middle_ref[...] + normalize_back(normed, inverse, grad_h * (1.0 + scale_attn))
    out.start(input_ref.at[pl.ds(strip, strip)], input_send_out)
    out.start(input_ref.at[pl.ds(0, strip)], input_out)
    parts = (
        column_sum(grad_h),
        column_sum(grad_h * normed),
        sums_ref[0:1],
        sums_ref[1:2],
        sums_ref[2:3],
        gate_mlp_sum,
    )
    for index, value in enumerate(parts):
        mod_grad_ref[:, index * width : (index + 1) * width] = value
    out.wait()


def partners(bit, count):
    return [(index, index ^ (1 << bit)) for index in range(count)]


def reduce_chunk(values_in, order, count):
    bits = count.bit_length() - 1
    place = lax.axis_index("dp")
    left = list(range(bits - 1, -1, -1))
    current = values_in.reshape((2,) * bits + values_in.shape[1:])
    for step, bit in enumerate(order):
        mine = (place >> bit) & 1
        axis = left.index(bit)
        send = pick(current, 1 - mine, axis).astype(BF16)
        keep = pick(current, mine, axis)
        left.pop(axis)
        got = lax.ppermute(send, "dp", partners(bit, count))
        current = keep.astype(F32) + got.astype(F32)
        if step < bits - 1:
            current = current.astype(BF16)
    return current


def reduce_scatter(values_in):
    count = lax.axis_size("dp")
    rows = values_in.shape[0] // count
    blocks = values_in.reshape(count, rows, values_in.shape[1])
    return reduce_chunk(blocks, range(count.bit_length() - 1), count)


class Flow:
    def __init__(self, kind, keep, send, *shapes):
        self.kind, self.step, self.shapes = kind, 0, shapes
        self.keep = keep
        self.send(send)

    def send(self, array):
        pairs = []
        for core in range(2):
            bit = bits_in_order(self.kind, core)[self.step]
            pairs += [(2 * place + core, 2 * (place ^ (1 << bit)) + core) for place in range(16)]
        self.got = lax.ppermute(array, ("dp", "blk"), pairs)

    def advance(self, token):
        got = self.got
        self.step += 1
        if self.step == 4:
            self.totals = call(
                finish_kernel, self.shapes, [self.keep, got], name="finish", wait_for=jax.tree.leaves(token)
            )
            return self.totals[0]
        send, self.keep = advance_call(self.keep, got, self.kind, self.step, token)
        self.send(send)
        return send


class Gather:
    def __init__(self, array):
        self.array, self.bit, self.got = array, 0, None
        self.count = lax.axis_size("dp")
        self.send()

    def send(self):
        bits = self.count.bit_length() - 1
        self.got = lax.ppermute(self.array, "dp", partners(bits - 1 - self.bit, self.count))

    def advance(self, token):
        count, *rest = self.array.shape
        (self.array,) = call(
            join_kernel,
            [shape_bf16(2 * count, *rest)],
            [self.array, self.got],
            name="join",
            wait_for=jax.tree.leaves(token),
        )
        self.bit += 1
        if 1 << self.bit < self.count:
            self.send()
        return self.array


def on_device(
    inputs,
    conditioning,
    grid_sizes,
    ada_weight,
    ada_bias,
    qkv_weight,
    qv_bias,
    proj_weight,
    proj_bias,
    fc1_weight,
    fc1_bias,
    fc2_weight,
    fc2_bias,
    cotangent,
):
    images, strip, width = inputs.shape
    data_count = lax.axis_size("dp")
    core = lax.axis_index("blk")
    other = 1 - core
    place = lax.axis_index("dp")
    part = ada_weight.shape[0]
    hidden = fc1_weight.shape[1]
    half_hidden = hidden // 2
    rows = images * strip
    split = data_count == 16
    sems = lambda count: pltpu.SemaphoreType.DMA((count,))
    buffers = lambda *shapes: [pltpu.VMEM(shape.shape, shape.dtype) for shape in shapes]
    own, own_f32, strip_low = shape_bf16(rows, width), shape_f32(rows, width), shape_bf16(strip, width)
    wide, pair_f32 = shape_bf16(2 * rows, half_hidden), shape_f32(2, rows, width)
    sizes = (grid_sizes, "smem")

    qkv_theirs = swap(qkv_weight)
    proj_theirs = swap(proj_weight)
    qv_bias, proj_bias, fc1_bias, fc2_bias, ada_bias = [
        bias[None, :] for bias in (qv_bias, proj_bias, fc1_bias, fc2_bias, ada_bias)
    ]
    pair, fc1_send, mod_part, silu_low = call(
        prelude_kernel,
        [
            shape_bf16(3, strip, width),
            shape_bf16(part, half_hidden),
            shape_f32(images, 6 * width),
            shape_bf16(images, width),
        ],
        [conditioning] + hbm(inputs, cotangent, ada_weight, fc1_weight),
        [pltpu.VMEM(ada_weight.shape, BF16), sems(6), sems(3)],
        name="prelude",
    )
    mod_got = swap(mod_part)
    pair = swap(pair)
    fc1_theirs = swap(after(fc1_send, (mod_got, pair, proj_theirs)))

    logs_shape = shape_f32(rows, 128)
    outs = (shape_bf16(2, rows, width), own, own, own, logs_shape, own_f32)
    both, query, key, value, logs, attn, h_mlp, modulation = call(
        front_kernel,
        hbm(*outs) + [own, shape_f32(2, 6 * width)],
        [sizes, mod_part, mod_got, ada_bias, qv_bias, proj_bias]
        + hbm(inputs, pair, qkv_weight, qkv_theirs, proj_weight, proj_theirs),
        buffers(own, shape_bf16(width, 3 * width), shape_bf16(width, width), *outs) + [sems(10), sems(7)],
        name="front",
    )
    h_mlp_other = swap(h_mlp)
    both_got = swap(both)

    length = half_hidden // 3
    block = width // 16
    if split:
        extra = hbm(*[shape_bf16(8, block, half_hidden)] * 2)
        staged = buffers(*[shape_bf16(3, 8, block, length)] * 2)
    else:
        extra, staged = hbm(wide), []
    gm_shape = shape_bf16(2 * rows, width)
    results = call(
        hidden_kernel,
        hbm(wide, gm_shape, pair_f32, pair_f32) + [shape_f32(1, half_hidden), shape_f32(1, width)] + extra,
        [sizes, h_mlp, h_mlp_other, modulation, fc1_bias]
        + hbm(cotangent, pair, fc1_weight, fc1_theirs, fc2_weight),
        staged
        + buffers(
            shape_bf16(4, strip, width),
            gm_shape,
            wide,
            wide,
            shape_bf16(width, half_hidden),
            shape_bf16(half_hidden, width),
            shape_f32(2, 2 * rows, width),
            shape_f32(width, length),
        )
        + [sems(13), sems(14)],
        name="hidden",
        wait_for=[both_got],
    )
    act, grad_mlp, own_part, their_part, fc1_bias_part, fc2_bias_part = results[:6]
    act_got = swap(act)
    got_part = swap(after(their_part, act_got))
    token = fc1_bias_part
    if split:
        fc1_flow = Flow(NEAR, *results[6:], shape_f32(block, half_hidden))
        paired = hidden // 32
        flowing = shape_bf16(4, 2, paired, width)
        results = call(
            fc2_grad_kernel,
            hbm(flowing, flowing),
            hbm(act, act_got, grad_mlp),
            buffers(
                shape_bf16(2, 2 * rows, half_hidden),
                gm_shape,
                shape_bf16(2, 2 * rows, part),
                shape_f32(half_hidden, part),
                *[shape_bf16(2, 4, paired, width)] * 2,
            )
            + [sems(7), sems(4)],
            name="fc2_grad",
        )
        fc2_flow = Flow(FAR, *[array.reshape(8, paired, width) for array in results], shape_f32(2 * paired, part))
        token = results[1]

    g_shape = shape_bf16(rows, 4 * part)
    outs = (own_f32, own, own, own, g_shape, g_shape)
    grad_middle, grad_query, grad_key, grad_value, g_mine, g_send, sums = call(
        middle_back_kernel,
        hbm(*outs) + [shape_f32(8, width)],
        [sizes, modulation]
        + hbm(
            inputs,
            cotangent,
            pair,
            attn,
            own_part,
            got_part,
            proj_weight,
            proj_theirs,
            query,
            key,
            value,
            logs,
        ),
        buffers(
            shape_bf16(4, strip, width),
            own_f32,
            pair_f32,
            shape_bf16(width, width),
            own,
            own,
            own,
            logs_shape,
            own,
            *outs,
        )
        + [sems(13), sems(6)],
        name="middle_back",
        wait_for=[token],
    )
    g_got = swap(g_send)
    token = sums
    if split:
        token = fc1_flow.advance(token)
        flowing = shape_bf16(8, block, 4 * part)
        results = call(
            qkv_grad_kernel,
            hbm(flowing, flowing),
            hbm(g_mine, g_got, both, both_got),
            buffers(
                shape_bf16(2 * rows, 4 * part),
                shape_bf16(2, 2 * rows, width),
                shape_f32(width, length),
                *[shape_bf16(3, 8, block, length)] * 2,
            )
            + [sems(6), sems(6)],
            name="qkv_grad",
            wait_for=[token],
        )
        qkv_flow = Flow(NEAR, *results, shape_f32(block, 3 * part), shape_f32(block, part))
        token = fc1_flow.advance(results[1])

    result, result_send, input_grad, input_send, mod_sums = call(
        last_kernel,
        hbm(strip_low, strip_low, shape_f32(strip, width), shape_f32(strip, width)) + [shape_f32(1, 6 * width)],
        [sizes, modulation, fc2_bias, sums]
        + hbm(
            inputs,
            cotangent,
            pair,
            attn,
            own_part,
            got_part,
            qkv_weight,
            qkv_theirs,
            grad_query,
            grad_key,
            grad_value,
            grad_middle,
        ),
        buffers(
            shape_bf16(4, strip, width),
            own_f32,
            pair_f32,
            shape_bf16(width, 3 * width),
            own,
            own,
            own,
            own_f32,
            own,
            own_f32,
        )
        + [sems(13), sems(4)],
        name="last",
        wait_for=[token],
    )

    def advance(token, *flows):
        for flow in flows:
            token = flow.advance(token)
        return token

    token = mod_sums

    together = lambda array, axis: lax.all_gather(array, "blk", axis=axis, tiled=True)
    modulation_low = together(after(mod_sums, token).astype(BF16), 0)
    by_device = lambda array: array.reshape(data_count, -1)
    sums, fc1_bias_part, fc2_bias_part = after((sums, fc1_bias_part, fc2_bias_part), token)
    image_bias = jnp.concatenate([by_device(sums[4:6]), by_device(sums[3]), by_device(fc2_bias_part)], 1)
    small = jnp.concatenate(
        [
            silu_low,
            columns_of(modulation_low, core, 3 * width),
            image_bias.astype(BF16).reshape(images, -1),
            fc1_bias_part.astype(BF16).reshape(images, -1),
        ],
        1,
    )
    gather = Gather(small.astype(BF16).reshape(images, -1, 128))
    back = lambda mine, theirs: in_order(core, mine[None], swap(theirs)[None])
    token = small
    if split:
        token = advance(small, fc2_flow, qkv_flow, gather)
        output, input_grad = back(result, after(result_send, token)), back(input_grad, after(input_send, token))
        token = advance(token, fc1_flow, fc2_flow, qkv_flow, gather, fc2_flow, fc1_flow, gather)
    else:
        output, input_grad = back(result, result_send), back(input_grad, input_send)
    (silu_part,) = call(
        silu_kernel,
        [shape_f32(images, part)],
        [modulation_low] + hbm(ada_weight),
        [pltpu.VMEM(ada_weight.shape, BF16), sems(6)],
        name="silu_grad",
        wait_for=jax.tree.leaves(token),
    )
    silu_grad = together(silu_part, 1)
    cond_grad = jax.vjp(jax.nn.silu, conditioning.astype(F32))[1](silu_grad)[0]
    token = silu_part
    if split:
        token = advance(token, qkv_flow, gather)
    else:
        while 1 << gather.bit < data_count:
            token = gather.advance(token)
    gathered = gather.array.reshape(images * data_count, -1)
    if (width // data_count) % 8 == 0:
        ada_grad, gathered_sums = call(
            ada_kernel,
            [shape_f32(width // data_count, 3 * width), shape_f32(2, gathered.shape[1] - width)],
            [gathered],
            [pltpu.VMEM((width, images * data_count), F32)],
            name="ada_grad",
            wait_for=jax.tree.leaves(token),
        )
    else:
        silu_rows = columns_of(gathered[:, :width], place, width // data_count)
        ada_grad = transpose_product(silu_rows.astype(BF16), gathered[:, width : 4 * width].astype(BF16))
        gathered_sums = jnp.sum(gathered[:, width:].astype(F32).reshape(data_count, images, -1), 0)
    token = gathered_sums
    image_count = image_bias.size // images
    bias_all = gathered_sums[:, 3 * width :]
    image_sums = bias_all[:, :image_count].reshape(data_count, -1)
    hidden_count = half_hidden // images
    hidden_sums = bias_all[:, image_count : image_count + hidden_count].reshape(data_count // 2, -1)
    ada_sums = jnp.sum(gathered_sums[:, : 3 * width], 0).reshape(data_count // 2, -1)
    near_half = jnp.where(place // (data_count // 2) == core, 1.0, 0.0)
    in_half = place % (data_count // 2)
    bias_sums = lax.psum(
        jnp.concatenate(
            [pick(ada_sums, in_half) * near_half, pick(image_sums, place), pick(hidden_sums, in_half) * near_half]
        ),
        "blk",
    )
    ends, at = [], 0
    for count in [6 * width, 2 * width, width, width]:
        at += count // data_count
        ends.append(at)
    ada_bias_grad, qv_bias_grad, proj_bias_grad, fc2_bias_grad, fc1_bias_grad = jnp.split(bias_sums, ends)

    if split:
        token = advance(token, fc2_flow, qkv_flow)
        (fc1_grad,), (fc2_grad,), (qkv_grad, proj_grad) = fc1_flow.totals, fc2_flow.totals, qkv_flow.totals
    else:
        h_mlp_all = jnp.concatenate([h_mlp, h_mlp_other], 0)
        fc1_grad = reduce_scatter(transpose_product(h_mlp_all, results[6]))
        grad_mlp_all = columns_of(grad_mlp, core, part)
        turned = jnp.concatenate([grad_mlp_all[rows:], grad_mlp_all[:rows]], 0)
        fc2_term = in_order(
            core,
            transpose_product(act, grad_mlp_all).astype(BF16),
            transpose_product(act_got, turned).astype(BF16),
        )
        fc2_grad = reduce_scatter(fc2_term)
        g_all = jnp.concatenate([g_mine, g_got], 0)
        h_attn_all = jnp.concatenate([both[0], both_got[0]], 0)
        attended_all = jnp.concatenate([both[1], both_got[1]], 0)
        qkv_grad = reduce_scatter(transpose_product(h_attn_all, g_all[:, : 3 * part]))
        proj_grad = reduce_scatter(transpose_product(attended_all, g_all[:, 3 * part :]))
    return (
        output,
        input_grad,
        cond_grad,
        ada_grad,
        ada_bias_grad,
        qkv_grad,
        qv_bias_grad,
        proj_grad,
        proj_bias_grad,
        fc1_grad,
        fc1_bias_grad,
        fc2_grad,
        fc2_bias_grad,
    )


def solution(mesh):
    rows = P("dp", "blk", None)
    weight = P("blk", None)
    grads = (P("dp", "blk"), P("dp"))
    placed = (rows, P("dp", None), P("dp", None)) + (weight, P()) * 5 + (rows,)
    return jax.shard_map(
        on_device,
        mesh=mesh,
        in_specs=placed,
        out_specs=(rows, rows, P("dp", None)) + grads * 5,
        check_vma=False,
    )
```

```python
import functools
import math

import jax
import jax.numpy as jnp
from jax import lax
from jax.experimental import pallas as pl
from jax.experimental.pallas import tpu as pltpu
from jax.sharding import PartitionSpec as P

HEADS = 16
EPS = 1e-06
MASKED = -1e30
F32 = jnp.float32
BF16 = jnp.bfloat16
GELU_A = math.sqrt(2.0 / math.pi)
GELU_B = 0.044715
NEAR, FAR = 0, 1
COSTS = {}
PLACES = {"hbm": pltpu.HBM, "smem": pltpu.SMEM}


def product(left, right):
    return jnp.dot(left, right, preferred_element_type=F32)


def transpose_product(left, right):
    return lax.dot_general(left, right, (((0,), (0,)), ((), ())), preferred_element_type=F32)


def product_back(left, right):
    return lax.dot_general(left, right, (((1,), (1,)), ((), ())), preferred_element_type=F32)


def swap(values_in):
    return lax.ppermute(values_in, "blk", [(0, 1), (1, 0)])


def pick(values_in, index, axis=0):
    return lax.dynamic_index_in_dim(values_in, index, axis, keepdims=False)


def columns_of(values_in, index, length):
    return lax.dynamic_slice_in_dim(values_in, index * length, length, 1)


def in_order(core, mine, theirs, axis=0):
    first = jnp.where(core == 0, mine, theirs)
    second = jnp.where(core == 0, theirs, mine)
    return jnp.concatenate([first, second], axis)


def after(values_in, token):
    return lax.optimization_barrier((values_in, token))[0]


def call(kernel, outs, ins, scratch=(), name=None, wait_for=()):
    count, waits = len(ins), len(wait_for)
    ins = [*ins, *hbm(*wait_for)]
    body = lambda *refs: kernel(*refs[:count], *refs[count + waits :])
    place = lambda item: pl.BlockSpec(memory_space=PLACES[item[1]] if isinstance(item, tuple) else pltpu.VMEM)
    plain = lambda item: item[0] if isinstance(item, tuple) else item
    return pl.pallas_call(
        body,
        out_shape=tuple(plain(out) for out in outs),
        in_specs=[place(item) for item in ins],
        out_specs=tuple(place(out) for out in outs),
        scratch_shapes=list(scratch),
        compiler_params=pltpu.CompilerParams(vmem_limit_bytes=58 * 1024 * 1024),
        cost_estimate=pl.CostEstimate(flops=COSTS.get(name, 10**11), bytes_accessed=10**6, transcendentals=0),
        name=name,
    )(*[plain(item) for item in ins])


def hbm(*items):
    return [(item, "hbm") for item in items]


class Copies:
    def __init__(self, sems):
        self.sems, self.copies = sems, []

    def start(self, source, target):
        copy = pltpu.make_async_copy(source, target, self.sems.at[len(self.copies)])
        copy.start()
        self.copies.append(copy)
        return copy

    def wait(self):
        for copy in self.copies:
            copy.wait()


def shape_f32(*dims):
    return jax.ShapeDtypeStruct(dims, F32)


def shape_bf16(*dims):
    return jax.ShapeDtypeStruct(dims, BF16)


def row_mean(values_in):
    return jnp.mean(values_in, -1, keepdims=True)


def normalize(values_in):
    centred = values_in - row_mean(values_in)
    inverse = lax.rsqrt(row_mean(centred * centred) + EPS)
    return centred * inverse, inverse


def normalize_back(normed, inverse, grad):
    return inverse * (grad - row_mean(grad) - normed * row_mean(grad * normed))


def head_window(head, size):
    low, high = head * size, (head + 1) * size
    start, stop = low // 128 * 128, -(-high // 128) * 128
    lane = lax.broadcasted_iota(jnp.int32, (1, stop - start), 1) + start
    return slice(start, stop), (lane >= low) & (lane < high)


def device_bits():
    place = lax.axis_index("dp")
    return lax.axis_index("blk"), lambda bit: (place >> bit) & 1


def valid_slots(core, sizes_ref, rows, dimension):
    strip = rows // 2
    shape = (1, rows) if dimension == 1 else (rows, 1)
    near = lax.broadcasted_iota(jnp.int32, shape, dimension)
    position = jnp.where(near < strip, core * strip + near, (1 - core) * strip + near - strip)
    return position < sizes_ref[core, 0] * sizes_ref[core, 1]


def start_rows(core, mine, theirs, target, copies):
    rows = mine.shape[0]
    at = lambda which: target.at[pl.ds(pl.multiple_of(which * rows, 64), rows)]
    return copies.start(mine, at(core)), copies.start(theirs, at(1 - core))


def wait_all(*copies):
    for copy in copies:
        copy.wait()


def pieces_of(mod_ref, width):
    return [mod_ref[0:1, index * width : (index + 1) * width] for index in range(6)]


def column_sum(array):
    return jnp.sum(array, 0, keepdims=True)


def prelude_kernel(
    cond_ref, inputs, cot, ada, w1, pair_ref, w1_ref, part_ref, silu_ref, ada_ref, ada_sems, sems
):
    core, _ = device_bits()
    other = 1 - core
    width, part = inputs.shape[2], ada.shape[0]
    half = w1_ref.shape[1]
    arriving, leaving = Copies(ada_sems), Copies(sems)
    leaving.start(inputs.at[other], pair_ref.at[0])
    leaving.start(cot, pair_ref.at[pl.ds(1, 2)])
    for piece in range(6):
        here = slice(piece * width, (piece + 1) * width)
        arriving.start(ada.at[:, here], ada_ref.at[:, here])
    leaving.start(w1.at[:, pl.ds(pl.multiple_of(other * half, 128), half)], w1_ref)
    cond = cond_ref[...].astype(F32)
    silu = (cond / (1.0 + jnp.exp(-cond))).astype(BF16)
    silu_ref[...] = silu
    low = silu.astype(F32)
    own = jnp.where(core == 0, low[:, :part], low[:, part:]).astype(BF16)
    for piece in range(6):
        here = slice(piece * width, (piece + 1) * width)
        arriving.copies[piece].wait()
        part_ref[:, here] = product(own, ada_ref[:, here])
    leaving.wait()


def front_kernel(
    sizes_ref,
    part_ref,
    got_ref,
    ada_bias_ref,
    qv_bias_ref,
    proj_bias_ref,
    inputs,
    pair,
    wq_mine,
    wq_theirs,
    wp_mine,
    wp_theirs,
    both_out,
    q_out,
    k_out,
    v_out,
    log_out,
    attn_out,
    h_mlp_ref,
    mod_ref,
    tokens_ref,
    wq_ref,
    wp_ref,
    both_ref,
    q_ref,
    k_ref,
    v_ref,
    log_ref,
    attn_ref,
    sems,
    out_sems,
):
    core, _ = device_bits()
    rows, width = q_ref.shape
    size, strip = width // HEADS, rows // 2
    arriving, out = Copies(sems), Copies(out_sems)
    token_copies = (
        arriving.start(inputs.at[core], tokens_ref.at[pl.ds(0, strip)]),
        arriving.start(pair.at[0], tokens_ref.at[pl.ds(strip, strip)]),
    )
    thirds = [pl.ds(index * width, width) for index in range(3)]
    q_copies = [
        start_rows(core, wq_mine.at[:, here], wq_theirs.at[:, here], wq_ref.at[:, here], arriving) for here in thirds
    ]
    p_copies = start_rows(core, wp_mine, wp_theirs, wp_ref, arriving)
    ada_bias = ada_bias_ref[...].astype(F32)
    for row, which in enumerate((core, 1 - core)):
        mod_ref[row : row + 1] = part_ref[pl.ds(which, 1), :] + got_ref[pl.ds(which, 1), :] + ada_bias
    shift_attn, scale_attn, gate_attn, shift_mlp, scale_mlp, _ = pieces_of(mod_ref, width)
    wait_all(*token_copies)
    tokens = tokens_ref[...].astype(F32)
    normed, _ = normalize(tokens)
    h_attn = (normed * (1.0 + scale_attn) + shift_attn).astype(BF16)
    both_ref[0] = h_attn
    out.start(both_ref.at[0], both_out.at[0])
    q_bias = qv_bias_ref[:, :width].astype(F32)
    v_bias = qv_bias_ref[:, width:].astype(F32)
    wait_all(*q_copies[0])
    q_ref[...] = (product(h_attn, wq_ref[:, :width]) + q_bias).astype(BF16)
    wait_all(*q_copies[1])
    k_ref[...] = product(h_attn, wq_ref[:, width : 2 * width]).astype(BF16)
    wait_all(*q_copies[2])
    v_ref[...] = (product(h_attn, wq_ref[:, 2 * width :]) + v_bias).astype(BF16)
    for source, target in ((q_ref, q_out), (k_ref, k_out), (v_ref, v_out)):
        out.start(source, target)

    valid = valid_slots(core, sizes_ref, rows, 1)
    lane = lax.broadcasted_iota(jnp.int32, (1, 128), 1)
    logs = jnp.zeros((rows, 128), F32)
    for head in range(HEADS):
        columns, own = head_window(head, size)
        query = jnp.where(own, q_ref[:, columns].astype(F32), 0.0).astype(BF16)
        scores = jnp.where(valid, product_back(query, k_ref[:, columns]) * size ** (-0.5), MASKED)
        largest = jnp.max(scores, -1, keepdims=True)
        exponent = jnp.exp(scores - largest)
        totals = jnp.sum(exponent, -1, keepdims=True)
        probs = (exponent / totals).astype(BF16)
        attended = product(probs, v_ref[:, columns])
        before = both_ref[1, :, columns].astype(F32)
        both_ref[1, :, columns] = jnp.where(own, attended, before).astype(BF16)
        logs = jnp.where(lane == head, largest + jnp.log(totals), logs)
    log_ref[...] = logs
    out.start(log_ref, log_out)
    out.start(both_ref.at[1], both_out.at[1])

    wait_all(*p_copies)
    proj_bias = proj_bias_ref[...].astype(F32)
    attn = product(both_ref[1], wp_ref[...]) + proj_bias
    attn_ref[...] = attn
    out.start(attn_ref, attn_out)
    normed_mlp, _ = normalize(tokens + gate_attn * attn)
    h_mlp_ref[...] = (normed_mlp * (1.0 + scale_mlp) + shift_mlp).astype(BF16)
    out.wait()


def bits_in_order(kind, core):
    return (core, 1 - core, 2, 3) if kind == NEAR else (2, core, 1 - core, 3)


def store_halves(read, kind, keep_ref, send_ref, columns=slice(None), high=None):
    core, bit_of = device_bits()
    order = bits_in_order(kind, core)
    mine = bit_of(order[0])
    for index in range(8 if high is None else 4):
        if high is None:
            base = ((index >> 2) << order[1]) + (((index >> 1) & 1) << order[2]) + ((index & 1) << order[3])
        else:
            base = ((index >> 1) << order[1]) + ((index & 1) << order[2])
        for target, value in ((keep_ref, mine), (send_ref, 1 - mine)):
            block = base + (value << order[0])
            target[index, :, columns] = read(block).astype(BF16)


def rows_of(total_ref, stride, first, count):
    return lambda block: total_ref[pl.ds(pl.multiple_of(block * stride + first, 8), count), :]


def hidden_kernel(
    sizes_ref,
    h_own_ref,
    h_other_ref,
    mod_ref,
    bias_ref,
    cot,
    pair,
    w1_mine,
    w1_theirs,
    w2,
    act_out,
    gm_out,
    own_out,
    their_out,
    hidden_bias_ref,
    out_bias_ref,
    *rest,
):
    core, _ = device_bits()
    other = 1 - core
    cot_ref, gm_ref, act_ref, gp_ref, w1_ref, w2_ref, part_ref, total_ref, sems, out_sems = rest[-10:]
    flowing = len(rest) > 11
    if flowing:
        keep_out, send_out, keep_ref, send_ref = rest[:4]
    else:
        gp_out = rest[0]
    length, half = total_ref.shape[1], act_ref.shape[1]
    rows, width = h_own_ref.shape
    arriving, out = Copies(sems), Copies(out_sems)
    cots = [
        arriving.start(source, cot_ref.at[at])
        for at, source in enumerate((cot.at[core], pair.at[1 + core], pair.at[1 + other], cot.at[other]))
    ]
    copies = []
    for start in range(0, half, length):
        here = pl.ds(start, length)
        mine = w1_mine.at[:, pl.ds(pl.multiple_of(core * half + start, 128), length)]
        second = arriving.start(w2.at[here], w2_ref.at[here])
        first = start_rows(core, mine, w1_theirs.at[:, here], w1_ref.at[:, here], arriving)
        copies.append((second, *first))
    wait_all(*cots)
    for row, which in enumerate((core, other)):
        array = jnp.concatenate([cot_ref[2 * row], cot_ref[2 * row + 1]], 0).astype(F32)
        valid = valid_slots(which, sizes_ref, rows, 0)
        gate = mod_ref[row : row + 1, 5 * width :]
        grad = (gate * jnp.where(valid, array, 0.0)).astype(BF16)
        gm_ref[row * rows : (row + 1) * rows] = grad
        if row == 0:
            out_bias_ref[...] = column_sum(grad.astype(F32))
    out.start(gm_ref, gm_out)
    h_all = jnp.concatenate([h_own_ref[...], h_other_ref[...]], 0)
    for chunk, start in enumerate(range(0, half, length)):
        wait_all(*copies[chunk])
        here = slice(start, start + length)
        at = pl.multiple_of(core * half + start, 128)
        bias = bias_ref[:, pl.ds(at, length)].astype(F32)
        grad_act = product_back(gm_ref[...], w2_ref[here, :])
        value = product(h_all, w1_ref[:, here]) + bias
        square = value * value
        tanh = jnp.tanh(GELU_A * value * (1.0 + GELU_B * square))
        half_up = 0.5 * (1.0 + tanh)
        act_ref[:, here] = (value * half_up).astype(BF16)
        out.start(act_ref.at[:, here], act_out.at[:, here])
        slope = half_up + 0.5 * value * (1.0 - tanh * tanh) * (GELU_A * (1.0 + 3.0 * GELU_B * square))
        grad_pre = (grad_act * slope).astype(BF16)
        gp_ref[:, here] = grad_pre
        hidden_bias_ref[:, here] = column_sum(grad_pre.astype(F32))
        if flowing:
            total_ref[...] = transpose_product(h_all, grad_pre)
            count = keep_ref.shape[2]
            store_halves(rows_of(total_ref, count, 0, count), NEAR, keep_ref.at[chunk], send_ref.at[chunk])
            out.start(send_ref.at[chunk], send_out.at[:, :, here])
            out.start(keep_ref.at[chunk], keep_out.at[:, :, here])
        else:
            out.start(gp_ref.at[:, here], gp_out.at[:, here])
    step = width // 3
    for index in range(2):
        for start in range(0, width, step):
            here = slice(start, start + step)
            if index == 0:
                part_ref[index, :, here] = product(act_ref[...], w2_ref[:, here])
            else:
                part_ref[index, :, here] = product_back(gp_ref[...], w1_ref[here, :])
        out.start(part_ref.at[index, pl.ds(rows, rows)], their_out.at[index])
        out.start(part_ref.at[index, pl.ds(0, rows)], own_out.at[index])
    out.wait()


def fc2_grad_kernel(
    act, act_got, gm, keep_out, send_out, act_ref, gm_ref, columns_ref, total_ref, keep_ref, send_ref, sems, out_sems
):
    core, _ = device_bits()
    arriving, out = Copies(sems), Copies(out_sems)
    rows, part = gm_ref.shape[0] // 2, columns_ref.shape[2]
    gm_copy = arriving.start(gm, gm_ref)
    length = act_ref.shape[2] // 3
    for side, source in enumerate((act, act_got)):
        for start in range(0, 3 * length, length):
            here = pl.ds(start, length)
            arriving.start(source.at[:, here], act_ref.at[side, :, here])
    gm_copy.wait()
    for index in range(2):

        @pl.when(core == index)
        def _():
            own = gm_ref[:rows, index * part : (index + 1) * part]
            other = gm_ref[rows:, index * part : (index + 1) * part]
            columns_ref[0, :rows] = own
            columns_ref[0, rows:] = other
            columns_ref[1, :rows] = other
            columns_ref[1, rows:] = own

    count = keep_ref.shape[2]
    for side in range(2):
        for index in range(3):
            arriving.copies[1 + 3 * side + index].wait()
            here = slice(index * length, (index + 1) * length)
            total_ref[here, :] = transpose_product(act_ref[side, :, here], columns_ref[side])
        for place in range(2):
            store_halves(
                rows_of(total_ref, 2 * count, place * count, count),
                FAR,
                keep_ref.at[side],
                send_ref.at[side],
                slice(place * part, (place + 1) * part),
                True,
            )
        high = core if side == 0 else 1 - core
        out.start(send_ref.at[side], send_out.at[:, high])
        out.start(keep_ref.at[side], keep_out.at[:, high])
    out.wait()


def advance_kernel(kind, step, keep, got, send_out, next_out, keep_ref, got_ref, sum_ref, sems, out_sems):
    core, bit_of = device_bits()
    mine = bit_of(bits_in_order(kind, core)[step])
    count = send_out.shape[0]
    arriving, out = Copies(sems), Copies(out_sems)
    halves = (1 - mine, mine)
    for index in range(2 * count):
        block = halves[index // count] * count + index % count
        arriving.start(keep.at[block], keep_ref.at[index])
        arriving.start(got.at[block], got_ref.at[index])
    for index in range(2 * count):
        wait_all(*arriving.copies[2 * index : 2 * index + 2])
        sum_ref[index] = (keep_ref[index].astype(F32) + got_ref[index].astype(F32)).astype(BF16)
        out.start(sum_ref.at[index], (send_out if index < count else next_out).at[index % count])
    out.wait()


def advance_call(keep, got, kind, step, token):
    count = keep.shape[0] // 2
    half = shape_bf16(count, *keep.shape[1:])
    buffer = pltpu.VMEM(keep.shape, BF16)
    return call(
        functools.partial(advance_kernel, kind, step),
        hbm(half, half),
        hbm(keep, got),
        (buffer, buffer, buffer, pltpu.SemaphoreType.DMA((4 * count,)), pltpu.SemaphoreType.DMA((2 * count,))),
        name="advance",
        wait_for=jax.tree.leaves(token),
    )


def join_kernel(first_ref, second_ref, out_ref):
    count = first_ref.shape[0]
    out_ref[:count] = first_ref[...]
    out_ref[count:] = second_ref[...]


def finish_kernel(keep_ref, got_ref, *outs):
    total = keep_ref[0].astype(F32) + got_ref[0].astype(F32)
    rows = total.shape[0]
    start = 0
    for out in outs:
        length = out.shape[1]
        for at in range(out.shape[0] // rows):
            out[at * rows : (at + 1) * rows] = total[:, start : start + length]
            start += length


def finish_pair_kernel(keep_ref, got_ref, next_keep_ref, next_got_ref, qkv_ref, proj_ref):
    first = keep_ref[0].astype(F32) + got_ref[0].astype(F32)
    second = next_keep_ref[0].astype(F32) + next_got_ref[0].astype(F32)
    width, rest = first.shape[1], qkv_ref.shape[1] - first.shape[1]
    qkv_ref[:, :width] = first
    qkv_ref[:, width:] = second[:, :rest]
    proj_ref[...] = second[:, rest:]


def ada_kernel(gathered_ref, ada_ref, sums_ref, silu_ref):
    rows, width = gathered_ref.shape[0], silu_ref.shape[0]
    mine = ada_ref.shape[0]
    place = lax.axis_index("dp")
    silu_ref[...] = gathered_ref[:, :width].astype(F32).T
    own = silu_ref[pl.ds(pl.multiple_of(place * mine, 8), mine), :].astype(BF16)
    ada_ref[...] = product(own, gathered_ref[:, width : 4 * width])
    odd = lax.broadcasted_iota(jnp.int32, (2, rows), 1) % 2
    row = lax.broadcasted_iota(jnp.int32, (2, rows), 0)
    sums_ref[...] = product(jnp.where(odd == row, 1.0, 0.0).astype(BF16), gathered_ref[:, width:])


def silu_kernel(grad_ref, ada, out_ref, ada_ref, sems):
    arriving = Copies(sems)
    rows = ada.shape[0] // sems.shape[0]
    for start in range(0, ada.shape[0], rows):
        arriving.start(ada.at[pl.ds(start, rows)], ada_ref.at[pl.ds(start, rows)])
    arriving.wait()
    out_ref[...] = product_back(grad_ref[...], ada_ref[...])


def middle_back_kernel(
    sizes_ref,
    mod_ref,
    inputs,
    cot,
    pair,
    attn,
    own_part,
    got_part,
    wp_mine,
    wp_theirs,
    query_in,
    key_in,
    value_in,
    log_in,
    grad_middle_out,
    gq_out,
    gk_out,
    gv_out,
    g_mine_out,
    g_send_out,
    sums_ref,
    strips_ref,
    attn_ref,
    parts_ref,
    wp_ref,
    q_ref,
    k_ref,
    v_ref,
    log_ref,
    ga_ref,
    grad_middle_ref,
    gq_ref,
    gk_ref,
    gv_ref,
    g_mine_ref,
    g_send_ref,
    sems,
    out_sems,
):
    core, _ = device_bits()
    arriving, out = Copies(sems), Copies(out_sems)
    for at, source in enumerate((inputs.at[core], pair.at[0], cot.at[core], pair.at[1 + core])):
        arriving.start(source, strips_ref.at[at])
    for source, target in ((attn, attn_ref), (own_part.at[1], parts_ref.at[0]), (got_part.at[1], parts_ref.at[1])):
        arriving.start(source, target)
    first = list(arriving.copies)
    p_copies = start_rows(core, wp_mine, wp_theirs, wp_ref, arriving)
    later = [
        arriving.start(source, target)
        for source, target in ((query_in, q_ref), (key_in, k_ref), (value_in, v_ref), (log_in, log_ref))
    ]
    rows, width = q_ref.shape
    size, part = width // HEADS, width // 2
    _, _, gate_attn, _, scale_mlp, _ = pieces_of(mod_ref, width)
    wait_all(*first)
    tokens = jnp.concatenate([strips_ref[0], strips_ref[1]], 0).astype(F32)
    cotangent = jnp.concatenate([strips_ref[2], strips_ref[3]], 0).astype(F32)
    grad_out = jnp.where(valid_slots(core, sizes_ref, rows, 0), cotangent, 0.0)
    grad_h = parts_ref[0] + parts_ref[1]
    normed, inverse = normalize(tokens + gate_attn * attn_ref[...])
    grad_middle = grad_out + normalize_back(normed, inverse, grad_h * (1.0 + scale_mlp))
    grad_middle_ref[...] = grad_middle
    out.start(grad_middle_ref, grad_middle_out)
    grad_attn = (gate_attn * grad_middle).astype(BF16)
    sums_ref[0:1] = column_sum(grad_middle * attn_ref[...])
    sums_ref[1:2] = column_sum(grad_h)
    sums_ref[2:3] = column_sum(grad_h * normed)
    sums_ref[3:4] = column_sum(grad_attn.astype(F32))
    wait_all(*p_copies)
    ga_ref[...] = product_back(grad_attn, wp_ref[...]).astype(BF16)

    valid = valid_slots(core, sizes_ref, rows, 1)
    scale = size ** (-0.5)
    wait_all(*later)
    for head in range(HEADS):
        columns, own = head_window(head, size)
        query = q_ref[:, columns]
        key = k_ref[:, columns]
        grad = ga_ref[:, columns]
        own_query = jnp.where(own, query.astype(F32), 0.0).astype(BF16)
        own_grad = jnp.where(own, grad.astype(F32), 0.0).astype(BF16)
        scores = jnp.where(valid, product_back(own_query, key) * scale, MASKED)
        probs = jnp.exp(scores - log_ref[:, head : head + 1])
        grad_probs = product_back(own_grad, v_ref[:, columns])
        inner = jnp.sum(probs * grad_probs, -1, keepdims=True)
        grad_scores = (probs * (grad_probs - inner)).astype(BF16)
        grad_query = product(grad_scores, key) * scale
        grad_key = transpose_product(grad_scores, query) * scale
        grad_value = transpose_product(probs.astype(BF16), grad)
        gq_ref[:, columns] = jnp.where(own, grad_query, gq_ref[:, columns].astype(F32)).astype(BF16)
        gk_ref[:, columns] = jnp.where(own, grad_key, gk_ref[:, columns].astype(F32)).astype(BF16)
        gv_ref[:, columns] = jnp.where(own, grad_value, gv_ref[:, columns].astype(F32)).astype(BF16)
    for source, target in ((gq_ref, gq_out), (gk_ref, gk_out), (gv_ref, gv_out)):
        out.start(source, target)

    for which, refs in ((0, (g_mine_ref, g_send_ref)), (1, (g_send_ref, g_mine_ref))):

        @pl.when(core == which)
        def _():
            for index, fill in enumerate(refs):
                fill_half(index, fill, grad_attn, gq_ref, gk_ref, gv_ref, width, part)

    out.start(g_send_ref, g_send_out)
    out.start(g_mine_ref, g_mine_out)
    sums_ref[4:5] = column_sum(gq_ref[...].astype(F32))
    sums_ref[5:6] = column_sum(gv_ref[...].astype(F32))
    out.wait()


def fill_half(index, fill, grad_attn, gq_ref, gk_ref, gv_ref, width, part):
    if index == 0:
        fill[:, :width] = gq_ref[...]
        fill[:, width : width + part] = gk_ref[:, :part]
    else:
        fill[:, :part] = gk_ref[:, part:]
        fill[:, part : part + width] = gv_ref[...]
    fill[:, width + part :] = grad_attn[:, index * part : (index + 1) * part]


def qkv_grad_kernel(
    g_mine, g_got, both, both_got, *rest
):
    outs = rest[:4]
    g_ref, x_ref, total_ref, keep_ref, send_ref, sems, out_sems = rest[4:]
    arriving, out = Copies(sems), Copies(out_sems)
    rows, width = both.shape[1:]
    upper, lower = pl.ds(0, rows), pl.ds(rows, rows)
    arriving.start(both.at[0], x_ref.at[0, upper])
    arriving.start(both_got.at[0], x_ref.at[0, lower])
    arriving.start(g_mine, g_ref.at[upper])
    arriving.start(g_got, g_ref.at[lower])
    arriving.start(both.at[1], x_ref.at[1, upper])
    arriving.start(both_got.at[1], x_ref.at[1, lower])
    wide = 3 * width // 2
    count, length = keep_ref.shape[2], total_ref.shape[1]
    wait_all(*arriving.copies[:4])
    for chunk in range(2):
        start = chunk * length
        if start + length <= wide:
            total_ref[...] = transpose_product(x_ref[0], g_ref[:, start : start + length])
        else:
            wait_all(*arriving.copies[4:])
            cut_at = wide - start
            total_ref[:, :cut_at] = transpose_product(x_ref[0], g_ref[:, start:wide])
            total_ref[:, cut_at:] = transpose_product(x_ref[1], g_ref[:, wide:])
        store_halves(rows_of(total_ref, count, 0, count), NEAR, keep_ref.at[chunk], send_ref.at[chunk])
        out.start(send_ref.at[chunk], outs[2 * chunk + 1])
        out.start(keep_ref.at[chunk], outs[2 * chunk])
    out.wait()


def last_kernel(
    sizes_ref,
    mod_ref,
    bias_ref,
    sums_ref,
    inputs,
    cot,
    pair,
    attn,
    own_part,
    got_part,
    wq_mine,
    wq_theirs,
    gq_in,
    gk_in,
    gv_in,
    grad_middle_in,
    result_out,
    result_send_out,
    input_out,
    input_send_out,
    mod_grad_ref,
    strips_ref,
    attn_ref,
    parts_ref,
    wq_ref,
    gq_ref,
    gk_ref,
    gv_ref,
    grad_middle_ref,
    result_ref,
    input_ref,
    sems,
    out_sems,
):
    core, _ = device_bits()
    arriving, out = Copies(sems), Copies(out_sems)
    for at, source in enumerate((inputs.at[core], pair.at[0], cot.at[core], pair.at[1 + core])):
        arriving.start(source, strips_ref.at[at])
    for source, target in ((attn, attn_ref), (own_part.at[0], parts_ref.at[0]), (got_part.at[0], parts_ref.at[1])):
        arriving.start(source, target)
    first = list(arriving.copies)
    grads = [arriving.start(source, target) for source, target in ((gq_in, gq_ref), (gk_in, gk_ref), (gv_in, gv_ref))]
    q_copies = start_rows(core, wq_mine, wq_theirs, wq_ref, arriving)
    middle_copy = arriving.start(grad_middle_in, grad_middle_ref)
    rows, width = gq_ref.shape
    strip = rows // 2
    _, scale_attn, gate_attn, _, _, gate_mlp = pieces_of(mod_ref, width)
    wait_all(*first)
    tokens = jnp.concatenate([strips_ref[0], strips_ref[1]], 0).astype(F32)
    cotangent = jnp.concatenate([strips_ref[2], strips_ref[3]], 0).astype(F32)
    valid = valid_slots(core, sizes_ref, rows, 0)
    mlp = parts_ref[0] + parts_ref[1] + bias_ref[...].astype(F32)
    middle = tokens + gate_attn * attn_ref[...]
    result_ref[...] = jnp.where(valid, middle + gate_mlp * mlp, 0.0).astype(BF16)
    out.start(result_ref.at[pl.ds(strip, strip)], result_send_out)
    out.start(result_ref.at[pl.ds(0, strip)], result_out)
    gate_mlp_sum = column_sum(jnp.where(valid, cotangent, 0.0) * mlp)
    normed, inverse = normalize(tokens)
    wait_all(*grads, *q_copies)
    grad_h = product_back(gq_ref[...], wq_ref[:, :width])
    grad_h += product_back(gk_ref[...], wq_ref[:, width : 2 * width])
    grad_h += product_back(gv_ref[...], wq_ref[:, 2 * width :])
    middle_copy.wait()
    input_ref[...] = grad_middle_ref[...] + normalize_back(normed, inverse, grad_h * (1.0 + scale_attn))
    out.start(input_ref.at[pl.ds(strip, strip)], input_send_out)
    out.start(input_ref.at[pl.ds(0, strip)], input_out)
    parts = (
        column_sum(grad_h),
        column_sum(grad_h * normed),
        sums_ref[0:1],
        sums_ref[1:2],
        sums_ref[2:3],
        gate_mlp_sum,
    )
    for index, value in enumerate(parts):
        mod_grad_ref[:, index * width : (index + 1) * width] = value
    out.wait()


def partners(bit, count):
    return [(index, index ^ (1 << bit)) for index in range(count)]


def reduce_chunk(values_in, order, count):
    bits = count.bit_length() - 1
    place = lax.axis_index("dp")
    left = list(range(bits - 1, -1, -1))
    current = values_in.reshape((2,) * bits + values_in.shape[1:])
    for step, bit in enumerate(order):
        mine = (place >> bit) & 1
        axis = left.index(bit)
        send = pick(current, 1 - mine, axis).astype(BF16)
        keep = pick(current, mine, axis)
        left.pop(axis)
        got = lax.ppermute(send, "dp", partners(bit, count))
        current = keep.astype(F32) + got.astype(F32)
        if step < bits - 1:
            current = current.astype(BF16)
    return current


def reduce_scatter(values_in):
    count = lax.axis_size("dp")
    rows = values_in.shape[0] // count
    blocks = values_in.reshape(count, rows, values_in.shape[1])
    return reduce_chunk(blocks, range(count.bit_length() - 1), count)


class Flow:
    def __init__(self, kind, keep, send, *shapes):
        self.kind, self.step, self.shapes = kind, 0, shapes
        self.keep = keep
        self.send(send)

    def send(self, array):
        pairs = []
        for core in range(2):
            bit = bits_in_order(self.kind, core)[self.step]
            pairs += [(2 * place + core, 2 * (place ^ (1 << bit)) + core) for place in range(16)]
        self.got = lax.ppermute(array, ("dp", "blk"), pairs)

    def advance(self, token):
        got = self.got
        self.step += 1
        if self.step == 4:
            self.totals = call(
                finish_kernel, self.shapes, [self.keep, got], name="finish", wait_for=jax.tree.leaves(token)
            )
            return self.totals[0]
        send, self.keep = advance_call(self.keep, got, self.kind, self.step, token)
        self.send(send)
        return send


class Gather:
    def __init__(self, array):
        self.array, self.bit, self.got = array, 0, None
        self.count = lax.axis_size("dp")
        self.send()

    def send(self):
        bits = self.count.bit_length() - 1
        self.got = lax.ppermute(self.array, "dp", partners(bits - 1 - self.bit, self.count))

    def advance(self, token):
        count, *rest = self.array.shape
        (self.array,) = call(
            join_kernel,
            [shape_bf16(2 * count, *rest)],
            [self.array, self.got],
            name="join",
            wait_for=jax.tree.leaves(token),
        )
        self.bit += 1
        if 1 << self.bit < self.count:
            self.send()
        return self.array


def on_device(
    inputs,
    conditioning,
    grid_sizes,
    ada_weight,
    ada_bias,
    qkv_weight,
    qv_bias,
    proj_weight,
    proj_bias,
    fc1_weight,
    fc1_bias,
    fc2_weight,
    fc2_bias,
    cotangent,
):
    images, strip, width = inputs.shape
    data_count = lax.axis_size("dp")
    core = lax.axis_index("blk")
    other = 1 - core
    place = lax.axis_index("dp")
    part = ada_weight.shape[0]
    hidden = fc1_weight.shape[1]
    half_hidden = hidden // 2
    rows = images * strip
    split = data_count == 16
    sems = lambda count: pltpu.SemaphoreType.DMA((count,))
    buffers = lambda *shapes: [pltpu.VMEM(shape.shape, shape.dtype) for shape in shapes]
    own, own_f32, strip_low = shape_bf16(rows, width), shape_f32(rows, width), shape_bf16(strip, width)
    wide, pair_f32 = shape_bf16(2 * rows, half_hidden), shape_f32(2, rows, width)
    sizes = (grid_sizes, "smem")

    qkv_theirs = swap(qkv_weight)
    proj_theirs = swap(proj_weight)
    qv_bias, proj_bias, fc1_bias, fc2_bias, ada_bias = [
        bias[None, :] for bias in (qv_bias, proj_bias, fc1_bias, fc2_bias, ada_bias)
    ]
    pair, fc1_send, mod_part, silu_low = call(
        prelude_kernel,
        [
            shape_bf16(3, strip, width),
            shape_bf16(part, half_hidden),
            shape_f32(images, 6 * width),
            shape_bf16(images, width),
        ],
        [conditioning] + hbm(inputs, cotangent, ada_weight, fc1_weight),
        [pltpu.VMEM(ada_weight.shape, BF16), sems(6), sems(3)],
        name="prelude",
    )
    mod_got = swap(mod_part)
    pair = swap(pair)
    fc1_theirs = swap(after(fc1_send, (mod_got, pair, proj_theirs)))

    logs_shape = shape_f32(rows, 128)
    outs = (shape_bf16(2, rows, width), own, own, own, logs_shape, own_f32)
    both, query, key, value, logs, attn, h_mlp, modulation = call(
        front_kernel,
        hbm(*outs) + [own, shape_f32(2, 6 * width)],
        [sizes, mod_part, mod_got, ada_bias, qv_bias, proj_bias]
        + hbm(inputs, pair, qkv_weight, qkv_theirs, proj_weight, proj_theirs),
        buffers(own, shape_bf16(width, 3 * width), shape_bf16(width, width), *outs) + [sems(10), sems(7)],
        name="front",
    )
    h_mlp_other = swap(h_mlp)
    both_got = swap(both)

    length = half_hidden // 3
    block = width // 16
    if split:
        extra = hbm(*[shape_bf16(8, block, half_hidden)] * 2)
        staged = buffers(*[shape_bf16(3, 8, block, length)] * 2)
    else:
        extra, staged = hbm(wide), []
    gm_shape = shape_bf16(2 * rows, width)
    results = call(
        hidden_kernel,
        hbm(wide, gm_shape, pair_f32, pair_f32) + [shape_f32(1, half_hidden), shape_f32(1, width)] + extra,
        [sizes, h_mlp, h_mlp_other, modulation, fc1_bias]
        + hbm(cotangent, pair, fc1_weight, fc1_theirs, fc2_weight),
        staged
        + buffers(
            shape_bf16(4, strip, width),
            gm_shape,
            wide,
            wide,
            shape_bf16(width, half_hidden),
            shape_bf16(half_hidden, width),
            shape_f32(2, 2 * rows, width),
            shape_f32(width, length),
        )
        + [sems(13), sems(14)],
        name="hidden",
        wait_for=[both_got],
    )
    act, grad_mlp, own_part, their_part, fc1_bias_part, fc2_bias_part = results[:6]
    act_got = swap(act)
    got_part = swap(after(their_part, act_got))
    token = fc1_bias_part
    if split:
        fc1_flow = Flow(NEAR, *results[6:], shape_f32(block, half_hidden))
        paired = hidden // 32
        flowing = shape_bf16(4, 2, paired, width)
        results = call(
            fc2_grad_kernel,
            hbm(flowing, flowing),
            hbm(act, act_got, grad_mlp),
            buffers(
                shape_bf16(2, 2 * rows, half_hidden),
                gm_shape,
                shape_bf16(2, 2 * rows, part),
                shape_f32(half_hidden, part),
                *[shape_bf16(2, 4, paired, width)] * 2,
            )
            + [sems(7), sems(4)],
            name="fc2_grad",
        )
        fc2_flow = Flow(FAR, *[array.reshape(8, paired, width) for array in results], shape_f32(2 * paired, part))
        token = results[1]

    g_shape = shape_bf16(rows, 4 * part)
    outs = (own_f32, own, own, own, g_shape, g_shape)
    grad_middle, grad_query, grad_key, grad_value, g_mine, g_send, sums = call(
        middle_back_kernel,
        hbm(*outs) + [shape_f32(8, width)],
        [sizes, modulation]
        + hbm(
            inputs,
            cotangent,
            pair,
            attn,
            own_part,
            got_part,
            proj_weight,
            proj_theirs,
            query,
            key,
            value,
            logs,
        ),
        buffers(
            shape_bf16(4, strip, width),
            own_f32,
            pair_f32,
            shape_bf16(width, width),
            own,
            own,
            own,
            logs_shape,
            own,
            *outs,
        )
        + [sems(13), sems(6)],
        name="middle_back",
        wait_for=[token],
    )
    g_got = swap(g_send)
    token = sums
    if split:
        token = fc1_flow.advance(token)
        flowing = shape_bf16(8, block, width)
        results = call(
            qkv_grad_kernel,
            hbm(*[flowing] * 4),
            hbm(g_mine, g_got, both, both_got),
            buffers(
                shape_bf16(2 * rows, 4 * part),
                shape_bf16(2, 2 * rows, width),
                shape_f32(width, width),
                *[shape_bf16(2, 8, block, width)] * 2,
            )
            + [sems(6), sems(4)],
            name="qkv_grad",
            wait_for=[token],
        )
        first_flow = Flow(NEAR, *results[:2])
        second_flow = Flow(NEAR, *results[2:])
        token = fc1_flow.advance(results[1])

    result, result_send, input_grad, input_send, mod_sums = call(
        last_kernel,
        hbm(strip_low, strip_low, shape_f32(strip, width), shape_f32(strip, width)) + [shape_f32(1, 6 * width)],
        [sizes, modulation, fc2_bias, sums]
        + hbm(
            inputs,
            cotangent,
            pair,
            attn,
            own_part,
            got_part,
            qkv_weight,
            qkv_theirs,
            grad_query,
            grad_key,
            grad_value,
            grad_middle,
        ),
        buffers(
            shape_bf16(4, strip, width),
            own_f32,
            pair_f32,
            shape_bf16(width, 3 * width),
            own,
            own,
            own,
            own_f32,
            own,
            own_f32,
        )
        + [sems(13), sems(4)],
        name="last",
        wait_for=[token],
    )

    def advance(token, *flows):
        for flow in flows:
            token = flow.advance(token)
        return token

    token = mod_sums

    together = lambda array, axis: lax.all_gather(array, "blk", axis=axis, tiled=True)
    modulation_low = together(after(mod_sums, token).astype(BF16), 0)
    by_device = lambda array: array.reshape(data_count, -1)
    sums, fc1_bias_part, fc2_bias_part = after((sums, fc1_bias_part, fc2_bias_part), token)
    image_bias = jnp.concatenate([by_device(sums[4:6]), by_device(sums[3]), by_device(fc2_bias_part)], 1)
    small = jnp.concatenate(
        [
            silu_low,
            columns_of(modulation_low, core, 3 * width),
            image_bias.astype(BF16).reshape(images, -1),
            fc1_bias_part.astype(BF16).reshape(images, -1),
        ],
        1,
    )
    gather = Gather(small.astype(BF16).reshape(images, -1, 128))
    back = lambda mine, theirs: in_order(core, mine[None], swap(theirs)[None])
    token = small
    if split:
        token = advance(small, first_flow, fc2_flow, second_flow, gather)
        output, input_grad = back(result, after(result_send, token)), back(input_grad, after(input_send, token))
        token = advance(token, fc1_flow, first_flow)
    else:
        output, input_grad = back(result, result_send), back(input_grad, input_send)
    (silu_part,) = call(
        silu_kernel,
        [shape_f32(images, part)],
        [modulation_low] + hbm(ada_weight),
        [pltpu.VMEM(ada_weight.shape, BF16), sems(6)],
        name="silu_grad",
        wait_for=jax.tree.leaves(token),
    )
    silu_grad = together(silu_part, 1)
    cond_grad = jax.vjp(jax.nn.silu, conditioning.astype(F32))[1](silu_grad)[0]
    token = silu_part
    if split:
        token = advance(token, gather, fc2_flow, second_flow, first_flow, gather, fc2_flow, fc1_flow, second_flow, gather)
    else:
        while 1 << gather.bit < data_count:
            token = gather.advance(token)
    gathered = gather.array.reshape(images * data_count, -1)
    if (width // data_count) % 8 == 0:
        ada_grad, gathered_sums = call(
            ada_kernel,
            [shape_f32(width // data_count, 3 * width), shape_f32(2, gathered.shape[1] - width)],
            [gathered],
            [pltpu.VMEM((width, images * data_count), F32)],
            name="ada_grad",
            wait_for=jax.tree.leaves(token),
        )
    else:
        silu_rows = columns_of(gathered[:, :width], place, width // data_count)
        ada_grad = transpose_product(silu_rows.astype(BF16), gathered[:, width : 4 * width].astype(BF16))
        gathered_sums = jnp.sum(gathered[:, width:].astype(F32).reshape(data_count, images, -1), 0)
    token = gathered_sums
    image_count = image_bias.size // images
    bias_all = gathered_sums[:, 3 * width :]
    image_sums = bias_all[:, :image_count].reshape(data_count, -1)
    hidden_count = half_hidden // images
    hidden_sums = bias_all[:, image_count : image_count + hidden_count].reshape(data_count // 2, -1)
    ada_sums = jnp.sum(gathered_sums[:, : 3 * width], 0).reshape(data_count // 2, -1)
    near_half = jnp.where(place // (data_count // 2) == core, 1.0, 0.0)
    in_half = place % (data_count // 2)
    bias_sums = lax.psum(
        jnp.concatenate(
            [pick(ada_sums, in_half) * near_half, pick(image_sums, place), pick(hidden_sums, in_half) * near_half]
        ),
        "blk",
    )
    ends, at = [], 0
    for count in [6 * width, 2 * width, width, width]:
        at += count // data_count
        ends.append(at)
    ada_bias_grad, qv_bias_grad, proj_bias_grad, fc2_bias_grad, fc1_bias_grad = jnp.split(bias_sums, ends)

    if split:
        token = advance(token, fc2_flow)
        qkv_grad, proj_grad = call(
            finish_pair_kernel,
            [shape_f32(block, 3 * part), shape_f32(block, part)],
            [first_flow.keep, first_flow.got, second_flow.keep, second_flow.got],
            name="finish",
            wait_for=[token],
        )
        (fc1_grad,), (fc2_grad,) = fc1_flow.totals, fc2_flow.totals
    else:
        h_mlp_all = jnp.concatenate([h_mlp, h_mlp_other], 0)
        fc1_grad = reduce_scatter(transpose_product(h_mlp_all, results[6]))
        grad_mlp_all = columns_of(grad_mlp, core, part)
        turned = jnp.concatenate([grad_mlp_all[rows:], grad_mlp_all[:rows]], 0)
        fc2_term = in_order(
            core,
            transpose_product(act, grad_mlp_all).astype(BF16),
            transpose_product(act_got, turned).astype(BF16),
        )
        fc2_grad = reduce_scatter(fc2_term)
        g_all = jnp.concatenate([g_mine, g_got], 0)
        h_attn_all = jnp.concatenate([both[0], both_got[0]], 0)
        attended_all = jnp.concatenate([both[1], both_got[1]], 0)
        qkv_grad = reduce_scatter(transpose_product(h_attn_all, g_all[:, : 3 * part]))
        proj_grad = reduce_scatter(transpose_product(attended_all, g_all[:, 3 * part :]))
    return (
        output,
        input_grad,
        cond_grad,
        ada_grad,
        ada_bias_grad,
        qkv_grad,
        qv_bias_grad,
        proj_grad,
        proj_bias_grad,
        fc1_grad,
        fc1_bias_grad,
        fc2_grad,
        fc2_bias_grad,
    )


def solution(mesh):
    rows = P("dp", "blk", None)
    weight = P("blk", None)
    grads = (P("dp", "blk"), P("dp"))
    placed = (rows, P("dp", None), P("dp", None)) + (weight, P()) * 5 + (rows,)
    return jax.shard_map(
        on_device,
        mesh=mesh,
        in_specs=placed,
        out_specs=(rows, rows, P("dp", None)) + grads * 5,
        check_vma=False,
    )
```

```python
import functools
import math

import jax
import jax.numpy as jnp
from jax import lax
from jax.experimental import pallas as pl
from jax.experimental.pallas import tpu as pltpu
from jax.sharding import PartitionSpec as P

HEADS = 16
EPS = 1e-06
MASKED = -1e30
F32 = jnp.float32
BF16 = jnp.bfloat16
GELU_A = math.sqrt(2.0 / math.pi)
GELU_B = 0.044715
NEAR, FAR = 0, 1
COSTS = {}
PLACES = {"hbm": pltpu.HBM, "smem": pltpu.SMEM}


def product(left, right):
    return jnp.dot(left, right, preferred_element_type=F32)


def transpose_product(left, right):
    return lax.dot_general(left, right, (((0,), (0,)), ((), ())), preferred_element_type=F32)


def product_back(left, right):
    return lax.dot_general(left, right, (((1,), (1,)), ((), ())), preferred_element_type=F32)


def swap(values_in):
    return lax.ppermute(values_in, "blk", [(0, 1), (1, 0)])


def pick(values_in, index, axis=0):
    return lax.dynamic_index_in_dim(values_in, index, axis, keepdims=False)


def columns_of(values_in, index, length):
    return lax.dynamic_slice_in_dim(values_in, index * length, length, 1)


def in_order(core, mine, theirs, axis=0):
    first = jnp.where(core == 0, mine, theirs)
    second = jnp.where(core == 0, theirs, mine)
    return jnp.concatenate([first, second], axis)


def after(values_in, token):
    return lax.optimization_barrier((values_in, token))[0]


def call(kernel, outs, ins, scratch=(), name=None, wait_for=()):
    count, waits = len(ins), len(wait_for)
    ins = [*ins, *hbm(*wait_for)]
    body = lambda *refs: kernel(*refs[:count], *refs[count + waits :])
    place = lambda item: pl.BlockSpec(memory_space=PLACES[item[1]] if isinstance(item, tuple) else pltpu.VMEM)
    plain = lambda item: item[0] if isinstance(item, tuple) else item
    return pl.pallas_call(
        body,
        out_shape=tuple(plain(out) for out in outs),
        in_specs=[place(item) for item in ins],
        out_specs=tuple(place(out) for out in outs),
        scratch_shapes=list(scratch),
        compiler_params=pltpu.CompilerParams(vmem_limit_bytes=58 * 1024 * 1024),
        cost_estimate=pl.CostEstimate(flops=COSTS.get(name, 10**11), bytes_accessed=10**6, transcendentals=0),
        name=name,
    )(*[plain(item) for item in ins])


def hbm(*items):
    return [(item, "hbm") for item in items]


class Copies:
    def __init__(self, sems):
        self.sems, self.copies = sems, []

    def start(self, source, target):
        copy = pltpu.make_async_copy(source, target, self.sems.at[len(self.copies)])
        copy.start()
        self.copies.append(copy)
        return copy

    def wait(self):
        for copy in self.copies:
            copy.wait()


def shape_f32(*dims):
    return jax.ShapeDtypeStruct(dims, F32)


def shape_bf16(*dims):
    return jax.ShapeDtypeStruct(dims, BF16)


def row_mean(values_in):
    return jnp.mean(values_in, -1, keepdims=True)


def normalize(values_in):
    centred = values_in - row_mean(values_in)
    inverse = lax.rsqrt(row_mean(centred * centred) + EPS)
    return centred * inverse, inverse


def normalize_back(normed, inverse, grad):
    return inverse * (grad - row_mean(grad) - normed * row_mean(grad * normed))


def head_window(head, size):
    low, high = head * size, (head + 1) * size
    start, stop = low // 128 * 128, -(-high // 128) * 128
    lane = lax.broadcasted_iota(jnp.int32, (1, stop - start), 1) + start
    return slice(start, stop), (lane >= low) & (lane < high)


def device_bits():
    place = lax.axis_index("dp")
    return lax.axis_index("blk"), lambda bit: (place >> bit) & 1


def valid_slots(core, sizes_ref, rows, dimension):
    strip = rows // 2
    shape = (1, rows) if dimension == 1 else (rows, 1)
    near = lax.broadcasted_iota(jnp.int32, shape, dimension)
    position = jnp.where(near < strip, core * strip + near, (1 - core) * strip + near - strip)
    return position < sizes_ref[core, 0] * sizes_ref[core, 1]


def start_rows(core, mine, theirs, target, copies):
    rows = mine.shape[0]
    at = lambda which: target.at[pl.ds(pl.multiple_of(which * rows, 64), rows)]
    return copies.start(mine, at(core)), copies.start(theirs, at(1 - core))


def wait_all(*copies):
    for copy in copies:
        copy.wait()


def pieces_of(mod_ref, width):
    return [mod_ref[0:1, index * width : (index + 1) * width] for index in range(6)]


def column_sum(array):
    return jnp.sum(array, 0, keepdims=True)


def prelude_kernel(
    cond_ref, inputs, cot, ada, w1, pair_ref, w1_ref, part_ref, silu_ref, ada_ref, ada_sems, sems
):
    core, _ = device_bits()
    other = 1 - core
    width, part = inputs.shape[2], ada.shape[0]
    half = w1_ref.shape[1]
    arriving, leaving = Copies(ada_sems), Copies(sems)
    leaving.start(inputs.at[other], pair_ref.at[0])
    leaving.start(cot, pair_ref.at[pl.ds(1, 2)])
    for piece in range(6):
        here = slice(piece * width, (piece + 1) * width)
        arriving.start(ada.at[:, here], ada_ref.at[:, here])
    leaving.start(w1.at[:, pl.ds(pl.multiple_of(other * half, 128), half)], w1_ref)
    cond = cond_ref[...].astype(F32)
    silu = (cond / (1.0 + jnp.exp(-cond))).astype(BF16)
    silu_ref[...] = silu
    low = silu.astype(F32)
    own = jnp.where(core == 0, low[:, :part], low[:, part:]).astype(BF16)
    for piece in range(6):
        here = slice(piece * width, (piece + 1) * width)
        arriving.copies[piece].wait()
        part_ref[:, here] = product(own, ada_ref[:, here])
    leaving.wait()


def front_kernel(
    sizes_ref,
    part_ref,
    got_ref,
    ada_bias_ref,
    qv_bias_ref,
    proj_bias_ref,
    inputs,
    pair,
    wq_mine,
    wq_theirs,
    wp_mine,
    wp_theirs,
    both_out,
    q_out,
    k_out,
    v_out,
    log_out,
    attn_out,
    h_mlp_ref,
    mod_ref,
    tokens_ref,
    wq_ref,
    wp_ref,
    both_ref,
    q_ref,
    k_ref,
    v_ref,
    log_ref,
    attn_ref,
    sems,
    out_sems,
):
    core, _ = device_bits()
    rows, width = q_ref.shape
    size, strip = width // HEADS, rows // 2
    arriving, out = Copies(sems), Copies(out_sems)
    token_copies = (
        arriving.start(inputs.at[core], tokens_ref.at[pl.ds(0, strip)]),
        arriving.start(pair.at[0], tokens_ref.at[pl.ds(strip, strip)]),
    )
    thirds = [pl.ds(index * width, width) for index in range(3)]
    q_copies = [
        start_rows(core, wq_mine.at[:, here], wq_theirs.at[:, here], wq_ref.at[:, here], arriving) for here in thirds
    ]
    p_copies = start_rows(core, wp_mine, wp_theirs, wp_ref, arriving)
    ada_bias = ada_bias_ref[...].astype(F32)
    for row, which in enumerate((core, 1 - core)):
        mod_ref[row : row + 1] = part_ref[pl.ds(which, 1), :] + got_ref[pl.ds(which, 1), :] + ada_bias
    shift_attn, scale_attn, gate_attn, shift_mlp, scale_mlp, _ = pieces_of(mod_ref, width)
    wait_all(*token_copies)
    tokens = tokens_ref[...].astype(F32)
    normed, _ = normalize(tokens)
    h_attn = (normed * (1.0 + scale_attn) + shift_attn).astype(BF16)
    both_ref[0] = h_attn
    out.start(both_ref.at[0], both_out.at[0])
    q_bias = qv_bias_ref[:, :width].astype(F32)
    v_bias = qv_bias_ref[:, width:].astype(F32)
    wait_all(*q_copies[0])
    q_ref[...] = (product(h_attn, wq_ref[:, :width]) + q_bias).astype(BF16)
    wait_all(*q_copies[1])
    k_ref[...] = product(h_attn, wq_ref[:, width : 2 * width]).astype(BF16)
    wait_all(*q_copies[2])
    v_ref[...] = (product(h_attn, wq_ref[:, 2 * width :]) + v_bias).astype(BF16)
    for source, target in ((q_ref, q_out), (k_ref, k_out), (v_ref, v_out)):
        out.start(source, target)

    valid = valid_slots(core, sizes_ref, rows, 1)
    lane = lax.broadcasted_iota(jnp.int32, (1, 128), 1)
    logs = jnp.zeros((rows, 128), F32)
    for head in range(HEADS):
        columns, own = head_window(head, size)
        query = jnp.where(own, q_ref[:, columns].astype(F32), 0.0).astype(BF16)
        scores = jnp.where(valid, product_back(query, k_ref[:, columns]) * size ** (-0.5), MASKED)
        largest = jnp.max(scores, -1, keepdims=True)
        exponent = jnp.exp(scores - largest)
        totals = jnp.sum(exponent, -1, keepdims=True)
        probs = (exponent / totals).astype(BF16)
        attended = product(probs, v_ref[:, columns])
        before = both_ref[1, :, columns].astype(F32)
        both_ref[1, :, columns] = jnp.where(own, attended, before).astype(BF16)
        logs = jnp.where(lane == head, largest + jnp.log(totals), logs)
    log_ref[...] = logs
    out.start(log_ref, log_out)
    out.start(both_ref.at[1], both_out.at[1])

    wait_all(*p_copies)
    proj_bias = proj_bias_ref[...].astype(F32)
    attn = product(both_ref[1], wp_ref[...]) + proj_bias
    attn_ref[...] = attn
    out.start(attn_ref, attn_out)
    normed_mlp, _ = normalize(tokens + gate_attn * attn)
    h_mlp_ref[...] = (normed_mlp * (1.0 + scale_mlp) + shift_mlp).astype(BF16)
    out.wait()


def bits_in_order(kind, core):
    return (core, 1 - core, 2, 3) if kind == NEAR else (2, core, 1 - core, 3)


def store_halves(read, kind, keep_ref, send_ref, columns=slice(None), high=None):
    core, bit_of = device_bits()
    order = bits_in_order(kind, core)
    mine = bit_of(order[0])
    for index in range(8 if high is None else 4):
        if high is None:
            base = ((index >> 2) << order[1]) + (((index >> 1) & 1) << order[2]) + ((index & 1) << order[3])
        else:
            base = ((index >> 1) << order[1]) + ((index & 1) << order[2])
        for target, value in ((keep_ref, mine), (send_ref, 1 - mine)):
            block = base + (value << order[0])
            target[index, :, columns] = read(block).astype(BF16)


def rows_of(total_ref, stride, first, count):
    return lambda block: total_ref[pl.ds(pl.multiple_of(block * stride + first, 8), count), :]


def hidden_kernel(
    sizes_ref,
    h_own_ref,
    h_other_ref,
    mod_ref,
    bias_ref,
    cot,
    pair,
    w1_mine,
    w1_theirs,
    w2,
    act_out,
    gm_out,
    own_out,
    their_out,
    hidden_bias_ref,
    out_bias_ref,
    *rest,
):
    core, _ = device_bits()
    other = 1 - core
    cot_ref, gm_ref, act_ref, gp_ref, w1_ref, w2_ref, part_ref, total_ref, sems, out_sems = rest[-10:]
    flowing = len(rest) > 11
    if flowing:
        keep_out, send_out, keep_ref, send_ref = rest[:4]
    else:
        gp_out = rest[0]
    length, half = total_ref.shape[1], act_ref.shape[1]
    rows, width = h_own_ref.shape
    arriving, out = Copies(sems), Copies(out_sems)
    cots = [
        arriving.start(source, cot_ref.at[at])
        for at, source in enumerate((cot.at[core], pair.at[1 + core], pair.at[1 + other], cot.at[other]))
    ]
    copies = []
    for start in range(0, half, length):
        here = pl.ds(start, length)
        mine = w1_mine.at[:, pl.ds(pl.multiple_of(core * half + start, 128), length)]
        second = arriving.start(w2.at[here], w2_ref.at[here])
        first = start_rows(core, mine, w1_theirs.at[:, here], w1_ref.at[:, here], arriving)
        copies.append((second, *first))
    wait_all(*cots)
    for row, which in enumerate((core, other)):
        array = jnp.concatenate([cot_ref[2 * row], cot_ref[2 * row + 1]], 0).astype(F32)
        valid = valid_slots(which, sizes_ref, rows, 0)
        gate = mod_ref[row : row + 1, 5 * width :]
        grad = (gate * jnp.where(valid, array, 0.0)).astype(BF16)
        gm_ref[row * rows : (row + 1) * rows] = grad
        if row == 0:
            out_bias_ref[...] = column_sum(grad.astype(F32))
    out.start(gm_ref, gm_out)
    h_all = jnp.concatenate([h_own_ref[...], h_other_ref[...]], 0)
    for chunk, start in enumerate(range(0, half, length)):
        wait_all(*copies[chunk])
        here = slice(start, start + length)
        at = pl.multiple_of(core * half + start, 128)
        bias = bias_ref[:, pl.ds(at, length)].astype(F32)
        grad_act = product_back(gm_ref[...], w2_ref[here, :])
        value = product(h_all, w1_ref[:, here]) + bias
        square = value * value
        tanh = jnp.tanh(GELU_A * value * (1.0 + GELU_B * square))
        half_up = 0.5 * (1.0 + tanh)
        act_ref[:, here] = (value * half_up).astype(BF16)
        out.start(act_ref.at[:, here], act_out.at[:, here])
        slope = half_up + 0.5 * value * (1.0 - tanh * tanh) * (GELU_A * (1.0 + 3.0 * GELU_B * square))
        grad_pre = (grad_act * slope).astype(BF16)
        gp_ref[:, here] = grad_pre
        hidden_bias_ref[:, here] = column_sum(grad_pre.astype(F32))
        if flowing:
            total_ref[...] = transpose_product(h_all, grad_pre)
            count = keep_ref.shape[2]
            store_halves(rows_of(total_ref, count, 0, count), NEAR, keep_ref.at[chunk], send_ref.at[chunk])
            out.start(send_ref.at[chunk], send_out.at[:, :, here])
            out.start(keep_ref.at[chunk], keep_out.at[:, :, here])
        else:
            out.start(gp_ref.at[:, here], gp_out.at[:, here])
    step = width // 3
    for index in range(2):
        for start in range(0, width, step):
            here = slice(start, start + step)
            if index == 0:
                part_ref[index, :, here] = product(act_ref[...], w2_ref[:, here])
            else:
                part_ref[index, :, here] = product_back(gp_ref[...], w1_ref[here, :])
        out.start(part_ref.at[index, pl.ds(rows, rows)], their_out.at[index])
        out.start(part_ref.at[index, pl.ds(0, rows)], own_out.at[index])
    out.wait()


def fc2_grad_kernel(
    act, act_got, gm, keep_out, send_out, act_ref, gm_ref, columns_ref, total_ref, keep_ref, send_ref, sems, out_sems
):
    core, _ = device_bits()
    arriving, out = Copies(sems), Copies(out_sems)
    rows, part = gm_ref.shape[0] // 2, columns_ref.shape[2]
    gm_copy = arriving.start(gm, gm_ref)
    length = act_ref.shape[2] // 3
    for side, source in enumerate((act, act_got)):
        for start in range(0, 3 * length, length):
            here = pl.ds(start, length)
            arriving.start(source.at[:, here], act_ref.at[side, :, here])
    gm_copy.wait()
    for index in range(2):

        @pl.when(core == index)
        def _():
            own = gm_ref[:rows, index * part : (index + 1) * part]
            other = gm_ref[rows:, index * part : (index + 1) * part]
            columns_ref[0, :rows] = own
            columns_ref[0, rows:] = other
            columns_ref[1, :rows] = other
            columns_ref[1, rows:] = own

    count = keep_ref.shape[2]
    for side in range(2):
        for index in range(3):
            arriving.copies[1 + 3 * side + index].wait()
            here = slice(index * length, (index + 1) * length)
            total_ref[here, :] = transpose_product(act_ref[side, :, here], columns_ref[side])
        for place in range(2):
            store_halves(
                rows_of(total_ref, 2 * count, place * count, count),
                FAR,
                keep_ref.at[side],
                send_ref.at[side],
                slice(place * part, (place + 1) * part),
                True,
            )
        high = core if side == 0 else 1 - core
        out.start(send_ref.at[side], send_out.at[:, high])
        out.start(keep_ref.at[side], keep_out.at[:, high])
    out.wait()


def advance_kernel(kind, step, keep, got, send_out, next_out, keep_ref, got_ref, sum_ref, sems, out_sems):
    core, bit_of = device_bits()
    mine = bit_of(bits_in_order(kind, core)[step])
    count = send_out.shape[0]
    arriving, out = Copies(sems), Copies(out_sems)
    halves = (1 - mine, mine)
    for index in range(2 * count):
        block = halves[index // count] * count + index % count
        arriving.start(keep.at[block], keep_ref.at[index])
        arriving.start(got.at[block], got_ref.at[index])
    for index in range(2 * count):
        wait_all(*arriving.copies[2 * index : 2 * index + 2])
        sum_ref[index] = (keep_ref[index].astype(F32) + got_ref[index].astype(F32)).astype(BF16)
        out.start(sum_ref.at[index], (send_out if index < count else next_out).at[index % count])
    out.wait()


def advance_call(keep, got, kind, step, token):
    count = keep.shape[0] // 2
    half = shape_bf16(count, *keep.shape[1:])
    buffer = pltpu.VMEM(keep.shape, BF16)
    return call(
        functools.partial(advance_kernel, kind, step),
        hbm(half, half),
        hbm(keep, got),
        (buffer, buffer, buffer, pltpu.SemaphoreType.DMA((4 * count,)), pltpu.SemaphoreType.DMA((2 * count,))),
        name="advance",
        wait_for=jax.tree.leaves(token),
    )


def join_kernel(first_ref, second_ref, out_ref):
    count = first_ref.shape[0]
    out_ref[:count] = first_ref[...]
    out_ref[count:] = second_ref[...]


def finish_kernel(keep_ref, got_ref, *outs):
    total = keep_ref[0].astype(F32) + got_ref[0].astype(F32)
    rows = total.shape[0]
    start = 0
    for out in outs:
        length = out.shape[1]
        for at in range(out.shape[0] // rows):
            out[at * rows : (at + 1) * rows] = total[:, start : start + length]
            start += length


def finish_pair_kernel(keep_ref, got_ref, next_keep_ref, next_got_ref, qkv_ref, proj_ref):
    first = keep_ref[0].astype(F32) + got_ref[0].astype(F32)
    second = next_keep_ref[0].astype(F32) + next_got_ref[0].astype(F32)
    width, rest = first.shape[1], qkv_ref.shape[1] - first.shape[1]
    qkv_ref[:, :width] = first
    qkv_ref[:, width:] = second[:, :rest]
    proj_ref[...] = second[:, rest:]


def ada_kernel(gathered_ref, ada_ref, sums_ref, silu_ref):
    rows, width = gathered_ref.shape[0], silu_ref.shape[0]
    mine = ada_ref.shape[0]
    place = lax.axis_index("dp")
    silu_ref[...] = gathered_ref[:, :width].astype(F32).T
    own = silu_ref[pl.ds(pl.multiple_of(place * mine, 8), mine), :].astype(BF16)
    ada_ref[...] = product(own, gathered_ref[:, width : 4 * width])
    odd = lax.broadcasted_iota(jnp.int32, (2, rows), 1) % 2
    row = lax.broadcasted_iota(jnp.int32, (2, rows), 0)
    sums_ref[...] = product(jnp.where(odd == row, 1.0, 0.0).astype(BF16), gathered_ref[:, width:])


def silu_kernel(grad_ref, ada, out_ref, ada_ref, sems):
    arriving = Copies(sems)
    rows = ada.shape[0] // sems.shape[0]
    for start in range(0, ada.shape[0], rows):
        arriving.start(ada.at[pl.ds(start, rows)], ada_ref.at[pl.ds(start, rows)])
    arriving.wait()
    out_ref[...] = product_back(grad_ref[...], ada_ref[...])


def middle_back_kernel(
    sizes_ref,
    mod_ref,
    inputs,
    cot,
    pair,
    attn,
    own_part,
    got_part,
    wp_mine,
    wp_theirs,
    query_in,
    key_in,
    value_in,
    log_in,
    grad_middle_out,
    gq_out,
    gk_out,
    gv_out,
    g_mine_out,
    g_send_out,
    sums_ref,
    strips_ref,
    attn_ref,
    parts_ref,
    wp_ref,
    q_ref,
    k_ref,
    v_ref,
    log_ref,
    ga_ref,
    grad_middle_ref,
    gq_ref,
    gk_ref,
    gv_ref,
    g_mine_ref,
    g_send_ref,
    sems,
    out_sems,
):
    core, _ = device_bits()
    arriving, out = Copies(sems), Copies(out_sems)
    for at, source in enumerate((inputs.at[core], pair.at[0], cot.at[core], pair.at[1 + core])):
        arriving.start(source, strips_ref.at[at])
    for source, target in ((attn, attn_ref), (own_part.at[1], parts_ref.at[0]), (got_part.at[1], parts_ref.at[1])):
        arriving.start(source, target)
    first = list(arriving.copies)
    p_copies = start_rows(core, wp_mine, wp_theirs, wp_ref, arriving)
    later = [
        arriving.start(source, target)
        for source, target in ((query_in, q_ref), (key_in, k_ref), (value_in, v_ref), (log_in, log_ref))
    ]
    rows, width = q_ref.shape
    size, part = width // HEADS, width // 2
    _, _, gate_attn, _, scale_mlp, _ = pieces_of(mod_ref, width)
    wait_all(*first)
    tokens = jnp.concatenate([strips_ref[0], strips_ref[1]], 0).astype(F32)
    cotangent = jnp.concatenate([strips_ref[2], strips_ref[3]], 0).astype(F32)
    grad_out = jnp.where(valid_slots(core, sizes_ref, rows, 0), cotangent, 0.0)
    grad_h = parts_ref[0] + parts_ref[1]
    normed, inverse = normalize(tokens + gate_attn * attn_ref[...])
    grad_middle = grad_out + normalize_back(normed, inverse, grad_h * (1.0 + scale_mlp))
    grad_middle_ref[...] = grad_middle
    out.start(grad_middle_ref, grad_middle_out)
    grad_attn = (gate_attn * grad_middle).astype(BF16)
    sums_ref[0:1] = column_sum(grad_middle * attn_ref[...])
    sums_ref[1:2] = column_sum(grad_h)
    sums_ref[2:3] = column_sum(grad_h * normed)
    sums_ref[3:4] = column_sum(grad_attn.astype(F32))
    wait_all(*p_copies)
    ga_ref[...] = product_back(grad_attn, wp_ref[...]).astype(BF16)

    valid = valid_slots(core, sizes_ref, rows, 1)
    scale = size ** (-0.5)
    wait_all(*later)
    for head in range(HEADS):
        columns, own = head_window(head, size)
        query = q_ref[:, columns]
        key = k_ref[:, columns]
        grad = ga_ref[:, columns]
        own_query = jnp.where(own, query.astype(F32), 0.0).astype(BF16)
        own_grad = jnp.where(own, grad.astype(F32), 0.0).astype(BF16)
        scores = jnp.where(valid, product_back(own_query, key) * scale, MASKED)
        probs = jnp.exp(scores - log_ref[:, head : head + 1])
        grad_probs = product_back(own_grad, v_ref[:, columns])
        inner = jnp.sum(probs * grad_probs, -1, keepdims=True)
        grad_scores = (probs * (grad_probs - inner)).astype(BF16)
        grad_query = product(grad_scores, key) * scale
        grad_key = transpose_product(grad_scores, query) * scale
        grad_value = transpose_product(probs.astype(BF16), grad)
        gq_ref[:, columns] = jnp.where(own, grad_query, gq_ref[:, columns].astype(F32)).astype(BF16)
        gk_ref[:, columns] = jnp.where(own, grad_key, gk_ref[:, columns].astype(F32)).astype(BF16)
        gv_ref[:, columns] = jnp.where(own, grad_value, gv_ref[:, columns].astype(F32)).astype(BF16)
    for source, target in ((gq_ref, gq_out), (gk_ref, gk_out), (gv_ref, gv_out)):
        out.start(source, target)

    for which, refs in ((0, (g_mine_ref, g_send_ref)), (1, (g_send_ref, g_mine_ref))):

        @pl.when(core == which)
        def _():
            for index, fill in enumerate(refs):
                fill_half(index, fill, grad_attn, gq_ref, gk_ref, gv_ref, width, part)

    out.start(g_send_ref, g_send_out)
    out.start(g_mine_ref, g_mine_out)
    sums_ref[4:5] = column_sum(gq_ref[...].astype(F32))
    sums_ref[5:6] = column_sum(gv_ref[...].astype(F32))
    out.wait()


def fill_half(index, fill, grad_attn, gq_ref, gk_ref, gv_ref, width, part):
    if index == 0:
        fill[:, :width] = gq_ref[...]
        fill[:, width : width + part] = gk_ref[:, :part]
    else:
        fill[:, :part] = gk_ref[:, part:]
        fill[:, part : part + width] = gv_ref[...]
    fill[:, width + part :] = grad_attn[:, index * part : (index + 1) * part]


def qkv_grad_kernel(
    g_mine, g_got, both, both_got, *rest
):
    outs = rest[:4]
    g_ref, x_ref, total_ref, keep_ref, send_ref, sems, out_sems = rest[4:]
    arriving, out = Copies(sems), Copies(out_sems)
    rows, width = both.shape[1:]
    upper, lower = pl.ds(0, rows), pl.ds(rows, rows)
    arriving.start(both.at[0], x_ref.at[0, upper])
    arriving.start(both_got.at[0], x_ref.at[0, lower])
    arriving.start(g_mine, g_ref.at[upper])
    arriving.start(g_got, g_ref.at[lower])
    arriving.start(both.at[1], x_ref.at[1, upper])
    arriving.start(both_got.at[1], x_ref.at[1, lower])
    wide = 3 * width // 2
    count, length = keep_ref.shape[2], total_ref.shape[1]
    wait_all(*arriving.copies[:4])
    for chunk in range(2):
        start = chunk * length
        if start + length <= wide:
            total_ref[...] = transpose_product(x_ref[0], g_ref[:, start : start + length])
        else:
            wait_all(*arriving.copies[4:])
            cut_at = wide - start
            total_ref[:, :cut_at] = transpose_product(x_ref[0], g_ref[:, start:wide])
            total_ref[:, cut_at:] = transpose_product(x_ref[1], g_ref[:, wide:])
        store_halves(rows_of(total_ref, count, 0, count), NEAR, keep_ref.at[chunk], send_ref.at[chunk])
        out.start(send_ref.at[chunk], outs[2 * chunk + 1])
        out.start(keep_ref.at[chunk], outs[2 * chunk])
    out.wait()


def last_kernel(
    sizes_ref,
    mod_ref,
    bias_ref,
    sums_ref,
    inputs,
    cot,
    pair,
    attn,
    own_part,
    got_part,
    wq_mine,
    wq_theirs,
    gq_in,
    gk_in,
    gv_in,
    grad_middle_in,
    result_out,
    result_send_out,
    input_out,
    input_send_out,
    mod_grad_ref,
    strips_ref,
    attn_ref,
    parts_ref,
    wq_ref,
    gq_ref,
    gk_ref,
    gv_ref,
    grad_middle_ref,
    result_ref,
    input_ref,
    sems,
    out_sems,
):
    core, _ = device_bits()
    arriving, out = Copies(sems), Copies(out_sems)
    for at, source in enumerate((inputs.at[core], pair.at[0], cot.at[core], pair.at[1 + core])):
        arriving.start(source, strips_ref.at[at])
    for source, target in ((attn, attn_ref), (own_part.at[0], parts_ref.at[0]), (got_part.at[0], parts_ref.at[1])):
        arriving.start(source, target)
    first = list(arriving.copies)
    grads = [arriving.start(source, target) for source, target in ((gq_in, gq_ref), (gk_in, gk_ref), (gv_in, gv_ref))]
    q_copies = start_rows(core, wq_mine, wq_theirs, wq_ref, arriving)
    middle_copy = arriving.start(grad_middle_in, grad_middle_ref)
    rows, width = gq_ref.shape
    strip = rows // 2
    _, scale_attn, gate_attn, _, _, gate_mlp = pieces_of(mod_ref, width)
    wait_all(*first)
    tokens = jnp.concatenate([strips_ref[0], strips_ref[1]], 0).astype(F32)
    cotangent = jnp.concatenate([strips_ref[2], strips_ref[3]], 0).astype(F32)
    valid = valid_slots(core, sizes_ref, rows, 0)
    mlp = parts_ref[0] + parts_ref[1] + bias_ref[...].astype(F32)
    middle = tokens + gate_attn * attn_ref[...]
    result_ref[...] = jnp.where(valid, middle + gate_mlp * mlp, 0.0).astype(BF16)
    out.start(result_ref.at[pl.ds(strip, strip)], result_send_out)
    out.start(result_ref.at[pl.ds(0, strip)], result_out)
    gate_mlp_sum = column_sum(jnp.where(valid, cotangent, 0.0) * mlp)
    normed, inverse = normalize(tokens)
    wait_all(*grads, *q_copies)
    grad_h = product_back(gq_ref[...], wq_ref[:, :width])
    grad_h += product_back(gk_ref[...], wq_ref[:, width : 2 * width])
    grad_h += product_back(gv_ref[...], wq_ref[:, 2 * width :])
    middle_copy.wait()
    input_ref[...] = grad_middle_ref[...] + normalize_back(normed, inverse, grad_h * (1.0 + scale_attn))
    out.start(input_ref.at[pl.ds(strip, strip)], input_send_out)
    out.start(input_ref.at[pl.ds(0, strip)], input_out)
    parts = (
        column_sum(grad_h),
        column_sum(grad_h * normed),
        sums_ref[0:1],
        sums_ref[1:2],
        sums_ref[2:3],
        gate_mlp_sum,
    )
    for index, value in enumerate(parts):
        mod_grad_ref[:, index * width : (index + 1) * width] = value
    out.wait()


def partners(bit, count):
    return [(index, index ^ (1 << bit)) for index in range(count)]


def reduce_chunk(values_in, order, count):
    bits = count.bit_length() - 1
    place = lax.axis_index("dp")
    left = list(range(bits - 1, -1, -1))
    current = values_in.reshape((2,) * bits + values_in.shape[1:])
    for step, bit in enumerate(order):
        mine = (place >> bit) & 1
        axis = left.index(bit)
        send = pick(current, 1 - mine, axis).astype(BF16)
        keep = pick(current, mine, axis)
        left.pop(axis)
        got = lax.ppermute(send, "dp", partners(bit, count))
        current = keep.astype(F32) + got.astype(F32)
        if step < bits - 1:
            current = current.astype(BF16)
    return current


def reduce_scatter(values_in):
    count = lax.axis_size("dp")
    rows = values_in.shape[0] // count
    blocks = values_in.reshape(count, rows, values_in.shape[1])
    return reduce_chunk(blocks, range(count.bit_length() - 1), count)


class Flow:
    def __init__(self, kind, keep, send, *shapes):
        self.kind, self.step, self.shapes = kind, 0, shapes
        self.keep = keep
        self.send(send)

    def send(self, array):
        pairs = []
        for core in range(2):
            bit = bits_in_order(self.kind, core)[self.step]
            pairs += [(2 * place + core, 2 * (place ^ (1 << bit)) + core) for place in range(16)]
        self.got = lax.ppermute(array, ("dp", "blk"), pairs)

    def advance(self, token):
        got = self.got
        self.step += 1
        if self.step == 4:
            self.totals = call(
                finish_kernel, self.shapes, [self.keep, got], name="finish", wait_for=jax.tree.leaves(token)
            )
            return self.totals[0]
        send, self.keep = advance_call(self.keep, got, self.kind, self.step, token)
        self.send(send)
        return send


class Gather:
    def __init__(self, array):
        self.array, self.bit, self.got = array, 0, None
        self.count = lax.axis_size("dp")
        self.send()

    def send(self):
        bits = self.count.bit_length() - 1
        self.got = lax.ppermute(self.array, "dp", partners(bits - 1 - self.bit, self.count))

    def advance(self, token):
        count, *rest = self.array.shape
        (self.array,) = call(
            join_kernel,
            [shape_bf16(2 * count, *rest)],
            [self.array, self.got],
            name="join",
            wait_for=jax.tree.leaves(token),
        )
        self.bit += 1
        if 1 << self.bit < self.count:
            self.send()
        return self.array


def on_device(
    inputs,
    conditioning,
    grid_sizes,
    ada_weight,
    ada_bias,
    qkv_weight,
    qv_bias,
    proj_weight,
    proj_bias,
    fc1_weight,
    fc1_bias,
    fc2_weight,
    fc2_bias,
    cotangent,
):
    images, strip, width = inputs.shape
    data_count = lax.axis_size("dp")
    core = lax.axis_index("blk")
    other = 1 - core
    place = lax.axis_index("dp")
    part = ada_weight.shape[0]
    hidden = fc1_weight.shape[1]
    half_hidden = hidden // 2
    rows = images * strip
    split = data_count == 16
    sems = lambda count: pltpu.SemaphoreType.DMA((count,))
    buffers = lambda *shapes: [pltpu.VMEM(shape.shape, shape.dtype) for shape in shapes]
    own, own_f32, strip_low = shape_bf16(rows, width), shape_f32(rows, width), shape_bf16(strip, width)
    wide, pair_f32 = shape_bf16(2 * rows, half_hidden), shape_f32(2, rows, width)
    sizes = (grid_sizes, "smem")

    qkv_theirs = swap(qkv_weight)
    proj_theirs = swap(proj_weight)
    qv_bias, proj_bias, fc1_bias, fc2_bias, ada_bias = [
        bias[None, :] for bias in (qv_bias, proj_bias, fc1_bias, fc2_bias, ada_bias)
    ]
    pair, fc1_send, mod_part, silu_low = call(
        prelude_kernel,
        [
            shape_bf16(3, strip, width),
            shape_bf16(part, half_hidden),
            shape_f32(images, 6 * width),
            shape_bf16(images, width),
        ],
        [conditioning] + hbm(inputs, cotangent, ada_weight, fc1_weight),
        [pltpu.VMEM(ada_weight.shape, BF16), sems(6), sems(3)],
        name="prelude",
    )
    mod_got = swap(mod_part)
    pair = swap(pair)
    fc1_theirs = swap(after(fc1_send, (mod_got, pair, proj_theirs)))

    logs_shape = shape_f32(rows, 128)
    outs = (shape_bf16(2, rows, width), own, own, own, logs_shape, own_f32)
    both, query, key, value, logs, attn, h_mlp, modulation = call(
        front_kernel,
        hbm(*outs) + [own, shape_f32(2, 6 * width)],
        [sizes, mod_part, mod_got, ada_bias, qv_bias, proj_bias]
        + hbm(inputs, pair, qkv_weight, qkv_theirs, proj_weight, proj_theirs),
        buffers(own, shape_bf16(width, 3 * width), shape_bf16(width, width), *outs) + [sems(10), sems(7)],
        name="front",
    )
    h_mlp_other = swap(h_mlp)
    both_got = swap(both)

    length = half_hidden // 3
    block = width // 16
    if split:
        extra = hbm(*[shape_bf16(8, block, half_hidden)] * 2)
        staged = buffers(*[shape_bf16(3, 8, block, length)] * 2)
    else:
        extra, staged = hbm(wide), []
    gm_shape = shape_bf16(2 * rows, width)
    results = call(
        hidden_kernel,
        hbm(wide, gm_shape, pair_f32, pair_f32) + [shape_f32(1, half_hidden), shape_f32(1, width)] + extra,
        [sizes, h_mlp, h_mlp_other, modulation, fc1_bias]
        + hbm(cotangent, pair, fc1_weight, fc1_theirs, fc2_weight),
        staged
        + buffers(
            shape_bf16(4, strip, width),
            gm_shape,
            wide,
            wide,
            shape_bf16(width, half_hidden),
            shape_bf16(half_hidden, width),
            shape_f32(2, 2 * rows, width),
            shape_f32(width, length),
        )
        + [sems(13), sems(14)],
        name="hidden",
    )
    act, grad_mlp, own_part, their_part, fc1_bias_part, fc2_bias_part = results[:6]
    act_got = swap(act)
    got_part = swap(after(their_part, act_got))
    token = fc1_bias_part
    if split:
        fc1_flow = Flow(NEAR, *results[6:], shape_f32(block, half_hidden))
        paired = hidden // 32
        flowing = shape_bf16(4, 2, paired, width)
        results = call(
            fc2_grad_kernel,
            hbm(flowing, flowing),
            hbm(act, act_got, grad_mlp),
            buffers(
                shape_bf16(2, 2 * rows, half_hidden),
                gm_shape,
                shape_bf16(2, 2 * rows, part),
                shape_f32(half_hidden, part),
                *[shape_bf16(2, 4, paired, width)] * 2,
            )
            + [sems(7), sems(4)],
            name="fc2_grad",
        )
        fc2_flow = Flow(FAR, *[array.reshape(8, paired, width) for array in results], shape_f32(2 * paired, part))
        token = results[1]

    g_shape = shape_bf16(rows, 4 * part)
    outs = (own_f32, own, own, own, g_shape, g_shape)
    grad_middle, grad_query, grad_key, grad_value, g_mine, g_send, sums = call(
        middle_back_kernel,
        hbm(*outs) + [shape_f32(8, width)],
        [sizes, modulation]
        + hbm(
            inputs,
            cotangent,
            pair,
            attn,
            own_part,
            got_part,
            proj_weight,
            proj_theirs,
            query,
            key,
            value,
            logs,
        ),
        buffers(
            shape_bf16(4, strip, width),
            own_f32,
            pair_f32,
            shape_bf16(width, width),
            own,
            own,
            own,
            logs_shape,
            own,
            *outs,
        )
        + [sems(13), sems(6)],
        name="middle_back",
        wait_for=[token],
    )
    g_got = swap(g_send)
    token = sums
    if split:
        token = fc1_flow.advance(token)
        flowing = shape_bf16(8, block, width)
        results = call(
            qkv_grad_kernel,
            hbm(*[flowing] * 4),
            hbm(g_mine, g_got, both, both_got),
            buffers(
                shape_bf16(2 * rows, 4 * part),
                shape_bf16(2, 2 * rows, width),
                shape_f32(width, width),
                *[shape_bf16(2, 8, block, width)] * 2,
            )
            + [sems(6), sems(4)],
            name="qkv_grad",
            wait_for=[token],
        )
        first_flow = Flow(NEAR, *results[:2])
        second_flow = Flow(NEAR, *results[2:])
        token = fc1_flow.advance(results[1])

    result, result_send, input_grad, input_send, mod_sums = call(
        last_kernel,
        hbm(strip_low, strip_low, shape_f32(strip, width), shape_f32(strip, width)) + [shape_f32(1, 6 * width)],
        [sizes, modulation, fc2_bias, sums]
        + hbm(
            inputs,
            cotangent,
            pair,
            attn,
            own_part,
            got_part,
            qkv_weight,
            qkv_theirs,
            grad_query,
            grad_key,
            grad_value,
            grad_middle,
        ),
        buffers(
            shape_bf16(4, strip, width),
            own_f32,
            pair_f32,
            shape_bf16(width, 3 * width),
            own,
            own,
            own,
            own_f32,
            own,
            own_f32,
        )
        + [sems(13), sems(4)],
        name="last",
        wait_for=[token],
    )

    def advance(token, *flows):
        for flow in flows:
            token = flow.advance(token)
        return token

    token = mod_sums

    together = lambda array, axis: lax.all_gather(array, "blk", axis=axis, tiled=True)
    modulation_low = together(after(mod_sums, token).astype(BF16), 0)
    by_device = lambda array: array.reshape(data_count, -1)
    sums, fc1_bias_part, fc2_bias_part = after((sums, fc1_bias_part, fc2_bias_part), token)
    image_bias = jnp.concatenate([by_device(sums[4:6]), by_device(sums[3]), by_device(fc2_bias_part)], 1)
    small = jnp.concatenate(
        [
            silu_low,
            columns_of(modulation_low, core, 3 * width),
            image_bias.astype(BF16).reshape(images, -1),
            fc1_bias_part.astype(BF16).reshape(images, -1),
        ],
        1,
    )
    gather = Gather(small.astype(BF16).reshape(images, -1, 128))
    back = lambda mine, theirs: in_order(core, mine[None], swap(theirs)[None])
    token = small
    if split:
        token = advance(small, first_flow, fc2_flow, second_flow, gather)
        output, input_grad = back(result, after(result_send, token)), back(input_grad, after(input_send, token))
        token = advance(token, fc1_flow, first_flow)
    else:
        output, input_grad = back(result, result_send), back(input_grad, input_send)
    (silu_part,) = call(
        silu_kernel,
        [shape_f32(images, part)],
        [modulation_low] + hbm(ada_weight),
        [pltpu.VMEM(ada_weight.shape, BF16), sems(6)],
        name="silu_grad",
        wait_for=jax.tree.leaves(token),
    )
    silu_grad = together(silu_part, 1)
    cond_grad = jax.vjp(jax.nn.silu, conditioning.astype(F32))[1](silu_grad)[0]
    token = silu_part
    if split:
        token = advance(token, gather, fc2_flow, second_flow, first_flow, gather, fc2_flow, second_flow, fc1_flow, gather)
    else:
        while 1 << gather.bit < data_count:
            token = gather.advance(token)
    gathered = gather.array.reshape(images * data_count, -1)
    if (width // data_count) % 8 == 0:
        ada_grad, gathered_sums = call(
            ada_kernel,
            [shape_f32(width // data_count, 3 * width), shape_f32(2, gathered.shape[1] - width)],
            [gathered],
            [pltpu.VMEM((width, images * data_count), F32)],
            name="ada_grad",
            wait_for=jax.tree.leaves(token),
        )
    else:
        silu_rows = columns_of(gathered[:, :width], place, width // data_count)
        ada_grad = transpose_product(silu_rows.astype(BF16), gathered[:, width : 4 * width].astype(BF16))
        gathered_sums = jnp.sum(gathered[:, width:].astype(F32).reshape(data_count, images, -1), 0)
    token = gathered_sums
    image_count = image_bias.size // images
    bias_all = gathered_sums[:, 3 * width :]
    image_sums = bias_all[:, :image_count].reshape(data_count, -1)
    hidden_count = half_hidden // images
    hidden_sums = bias_all[:, image_count : image_count + hidden_count].reshape(data_count // 2, -1)
    ada_sums = jnp.sum(gathered_sums[:, : 3 * width], 0).reshape(data_count // 2, -1)
    near_half = jnp.where(place // (data_count // 2) == core, 1.0, 0.0)
    in_half = place % (data_count // 2)
    bias_sums = lax.psum(
        jnp.concatenate(
            [pick(ada_sums, in_half) * near_half, pick(image_sums, place), pick(hidden_sums, in_half) * near_half]
        ),
        "blk",
    )
    ends, at = [], 0
    for count in [6 * width, 2 * width, width, width]:
        at += count // data_count
        ends.append(at)
    ada_bias_grad, qv_bias_grad, proj_bias_grad, fc2_bias_grad, fc1_bias_grad = jnp.split(bias_sums, ends)

    if split:
        token = advance(token, fc2_flow)
        qkv_grad, proj_grad = call(
            finish_pair_kernel,
            [shape_f32(block, 3 * part), shape_f32(block, part)],
            [first_flow.keep, first_flow.got, second_flow.keep, second_flow.got],
            name="finish",
            wait_for=[token],
        )
        (fc1_grad,), (fc2_grad,) = fc1_flow.totals, fc2_flow.totals
    else:
        h_mlp_all = jnp.concatenate([h_mlp, h_mlp_other], 0)
        fc1_grad = reduce_scatter(transpose_product(h_mlp_all, results[6]))
        grad_mlp_all = columns_of(grad_mlp, core, part)
        turned = jnp.concatenate([grad_mlp_all[rows:], grad_mlp_all[:rows]], 0)
        fc2_term = in_order(
            core,
            transpose_product(act, grad_mlp_all).astype(BF16),
            transpose_product(act_got, turned).astype(BF16),
        )
        fc2_grad = reduce_scatter(fc2_term)
        g_all = jnp.concatenate([g_mine, g_got], 0)
        h_attn_all = jnp.concatenate([both[0], both_got[0]], 0)
        attended_all = jnp.concatenate([both[1], both_got[1]], 0)
        qkv_grad = reduce_scatter(transpose_product(h_attn_all, g_all[:, : 3 * part]))
        proj_grad = reduce_scatter(transpose_product(attended_all, g_all[:, 3 * part :]))
    return (
        output,
        input_grad,
        cond_grad,
        ada_grad,
        ada_bias_grad,
        qkv_grad,
        qv_bias_grad,
        proj_grad,
        proj_bias_grad,
        fc1_grad,
        fc1_bias_grad,
        fc2_grad,
        fc2_bias_grad,
    )


def solution(mesh):
    rows = P("dp", "blk", None)
    weight = P("blk", None)
    grads = (P("dp", "blk"), P("dp"))
    placed = (rows, P("dp", None), P("dp", None)) + (weight, P()) * 5 + (rows,)
    return jax.shard_map(
        on_device,
        mesh=mesh,
        in_specs=placed,
        out_specs=(rows, rows, P("dp", None)) + grads * 5,
        check_vma=False,
    )
```
